32 devices in a mesh: seq: 4 (over z), tp: 4 (over y, x), fsdp: 2 (over core).
Axes of the slice: x: 2, y: 2, z: 4, core: 2. Of those that a mesh axis runs over, the one named last changes fastest.
Arguments:
- decoder_in: bfloat16 [32, 128, 1024], P(('seq', 'fsdp')), may hold values from -6 to 6
- memory: bfloat16 [32, 2048, 1024], P(('seq', 'fsdp')), may hold values from -6 to 6
- buckets: int32 [128, 128], replicated, may hold values from 0 to 31
- norm_gains: bfloat16 [3, 1024], P(None, ('seq', 'fsdp')), may hold values from 0.5 to 1.5
- rel_bias: bfloat16 [32, 16], P(('seq', 'fsdp'), 'tp'), may hold values from -4 to 4
- self_q: bfloat16 [1024, 1024], P(('seq', 'fsdp'), 'tp'), may hold values from -0.1875 to 0.1875
- self_kv: bfloat16 [1024, 2, 512], P(('seq', 'fsdp'), None, 'tp'), may hold values from -0.1875 to 0.1875
- self_out: bfloat16 [1024, 1024], P('tp', ('seq', 'fsdp')), may hold values from -0.75 to 0.75
- cross_q: bfloat16 [1024, 1024], P(('seq', 'fsdp'), 'tp'), may hold values from -0.1875 to 0.1875
- cross_kv: bfloat16 [1024, 2, 512], P(('seq', 'fsdp'), None, 'tp'), may hold values from -0.1875 to 0.1875
- cross_out: bfloat16 [1024, 1024], P('tp', ('seq', 'fsdp')), may hold values from -3 to 3
- gate_up: bfloat16 [1024, 2, 2816], P(('seq', 'fsdp'), None, 'tp'), may hold values from -0.1875 to 0.1875
- down: bfloat16 [2816, 1024], P('tp', ('seq', 'fsdp')), may hold values from -0.109375 to 0.109375
- cotangent: bfloat16 [32, 128, 1024], P(('seq', 'fsdp')), may hold values from -6 to 6
Outputs:
- decoder_out: bfloat16 [32, 128, 1024], P(('seq', 'fsdp'))
- decoder_grad: float32 [32, 128, 1024], P(('seq', 'fsdp'))
- memory_grad: bfloat16 [32, 2048, 1024], P(('seq', 'fsdp'), None, 'tp')
- gains_grad: float32 [3, 1024], P(None, ('seq', 'fsdp'))
- bias_grad: float32 [32, 16], P(('seq', 'fsdp'), 'tp')
- self_q_grad: float32 [1024, 1024], P(('seq', 'fsdp'), 'tp')
- self_kv_grad: float32 [1024, 2, 512], P(('seq', 'fsdp'), None, 'tp')
- self_out_grad: float32 [1024, 1024], P('tp', ('seq', 'fsdp'))
- cross_q_grad: float32 [1024, 1024], P(('seq', 'fsdp'), 'tp')
- cross_kv_grad: float32 [1024, 2, 512], P(('seq', 'fsdp'), None, 'tp')
- cross_out_grad: float32 [1024, 1024], P('tp', ('seq', 'fsdp'))
- gate_up_grad: float32 [1024, 2, 2816], P(('seq', 'fsdp'), None, 'tp')
- down_grad: float32 [2816, 1024], P('tp', ('seq', 'fsdp'))
The draws below stay inside these ranges and needn't reach their ends.
Inputs may be any that keep to these rules, and one draw needn't show every extreme that they name: `buckets`: the bucket of query position i and key position j, the same for every sequence and head.
All inputs are finite; a program needn't handle non-finite values.
Results may differ from the reference program's by a relative error of at most 0.04.
Values may be sent and summed in bfloat16 or wider, within the bound.
No kernel may reach another device: no remote copies, remote signals or barrier semaphores. Data moves between devices by JAX's collectives and lax.ppermute only.
A program may use at most 192 MiB of HBM per device.

```python
import jax
import jax.numpy as jnp
from jax import lax

D = 1024
H = 16
DH = 64
G = 8
FF = 2816
NB = 32
LEN = 128
MEM = 2048
SEQS = 32


def set_ends(array, own_key, least, top_value):
    dims = array.shape
    index_at = [jax.random.randint(jax.random.fold_in(own_key, axis), (), 0, dims[axis]) for axis in range(len(dims))]
    array = array.at[tuple(index_at)].set(least)
    longest = dims.index(max(dims))
    index_at[longest] = (index_at[longest] + 1) % dims[longest]
    return array.at[tuple(index_at)].set(top_value)


def spiked(result, rng, source, target, parts, factor):
    owner, partner = [(jnp.arange(result.shape[dim]) // (result.shape[dim] // parts)).reshape([-1 if axis == dim else 1 for axis in range(result.ndim)]) for dim in (source, target)]
    chosen = jax.random.permutation(rng, parts)[partner]
    strong = (owner == chosen) | (owner == (partner + parts // 2) % parts)
    return jnp.where(strong, factor * result, result)


def level_of(key, dims, cuts, smallest, high):
    level = 1.0
    for axis_at, blocks in cuts:
        draws = jax.random.uniform(jax.random.fold_in(jax.random.fold_in(key, 6), axis_at), (blocks,), jnp.float32, smallest / len(cuts), high / len(cuts))
        level = level * jnp.repeat(jnp.exp(draws), dims[axis_at] // blocks).reshape((-1,) + (1,) * (len(dims) - 1 - axis_at))
    return level


def normal_values(stream_key, shape, width, bound, pieces=(), kind=jnp.bfloat16):
    values = width * jax.random.normal(stream_key, shape, jnp.float32)
    if pieces:
        values = values * level_of(stream_key, shape, pieces, -0.22, 0.18)
    return jnp.clip(values, -bound, bound).astype(kind)


def noise_with(stream_key, extent, deviation, bound, shards, heavy, kind=jnp.bfloat16):
    result = deviation * jax.random.normal(stream_key, extent, jnp.float32)
    if shards:
        result = result * level_of(stream_key, extent, shards, -0.22, 0.18)
    return jnp.clip(spiked(result, jax.random.fold_in(stream_key, 3), *heavy), -bound, bound).astype(kind)


def setup_inputs(seed: int = 0) -> dict:
    seeds = jax.random.split(jax.random.key(seed), 15)
    return {
        "decoder_in": normal_values(seeds[0], (SEQS, LEN, D), 1.0, 6.0, ((0, 8),)),
        "memory": normal_values(seeds[1], (SEQS, MEM, D), 1.0, 6.0, ((0, 8),)),
        "buckets": set_ends(jax.random.randint(seeds[2], (LEN, LEN), 0, NB), jax.random.fold_in(seeds[2], 1), 0, NB - 1).astype(jnp.int32),
        "norm_gains": jnp.clip(1.0 + 0.1 * jax.random.normal(seeds[3], (3, D), jnp.float32), 0.5, 1.5).astype(jnp.bfloat16),
        "rel_bias": normal_values(seeds[4], (NB, H), 1.0, 4.0, ((0, 8), (1, 4))),
        "self_q": normal_values(seeds[5], (D, H * DH), D ** -0.5, 0.1875, ((0, 8), (1, 4))),
        "self_kv": normal_values(seeds[6], (D, 2, G * DH), D ** -0.5, 0.1875, ((0, 8), (2, 4))),
        "self_out": normal_values(seeds[7], (H * DH, D), (H * DH * 8 // LEN) ** -0.5, 0.75, ((0, 4), (1, 8))),
        "cross_q": normal_values(seeds[8], (D, H * DH), D ** -0.5, 0.1875, ((0, 8), (1, 4))),
        "cross_kv": normal_values(seeds[9], (D, 2, G * DH), D ** -0.5, 0.1875, ((0, 8), (2, 4))),
        "cross_out": normal_values(seeds[10], (H * DH, D), (H * DH * 8 // MEM) ** -0.5, 3.0, ((0, 4), (1, 8))),
        "gate_up": normal_values(seeds[11], (D, 2, FF), D ** -0.5, 0.1875, ((0, 8), (2, 4))),
        "down": normal_values(seeds[12], (FF, D), FF ** -0.5, 0.109375, ((0, 4), (1, 8))),
        "cotangent": noise_with(seeds[13], (SEQS, LEN, D), 1.0, 6.0, ((0, 8),), (0, 2, 8, 2.0)),
    }


@jax.custom_vjp
def low(v):
    return lax.optimization_barrier(v.astype(jnp.bfloat16)).astype(jnp.float32)

@jax.custom_vjp
def low_back(v):
    return v

def low_keep(v):
    return (low(v), None)

def low_pass(kept, grad):
    return (grad,)

def back_keep(v):
    return (v, None)

def back_low(kept, grad):
    return (low(grad),)
low.defvjp(low_keep, low_pass)
low_back.defvjp(back_keep, back_low)
HIGHEST = lax.Precision.HIGHEST
EPSILON = 1e-06
MASKED = -1e+30

def both_ways(values):
    return low_back(low(values))

def rms_norm(values, gain):
    return values * lax.rsqrt(lax.optimization_barrier(jnp.mean(values * values, axis=-1, keepdims=True)) + EPSILON) * gain

def attend(query, keys, values, bias, causal):
    rows = query.shape[0]
    span = keys.shape[0]
    query_heads = query.reshape(rows, H, DH)
    key_heads = jnp.repeat(keys.reshape(span, G, DH), H // G, axis=1)
    value_heads = jnp.repeat(values.reshape(span, G, DH), H // G, axis=1)
    scores = jnp.einsum('ihd,jhd->hij', query_heads, key_heads, precision=HIGHEST) * DH ** (-0.5)
    if bias is not None:
        scores = scores + bias
    scores = low_back(scores)
    if causal is not None:
        scores = jnp.where(causal, scores, MASKED)
    row_max = lax.optimization_barrier(jnp.max(scores, axis=-1, keepdims=True))
    exponent = jnp.exp(scores - row_max)
    probs = exponent / lax.optimization_barrier(jnp.sum(exponent, axis=-1, keepdims=True))
    mixed = jnp.einsum('hij,jhd->ihd', low(probs), value_heads, precision=HIGHEST)
    return mixed.reshape(rows, H * DH)

def layer(tokens, memory, weights, onehot, causal):
    gains, table, self_q, self_kv, self_out, cross_q, cross_kv, cross_out, gate_up, down = weights
    normed = low(rms_norm(tokens, gains[0]))
    query = both_ways(jnp.dot(normed, self_q, precision=HIGHEST))
    keys = both_ways(jnp.dot(normed, self_kv[:, 0], precision=HIGHEST))
    values = both_ways(jnp.dot(normed, self_kv[:, 1], precision=HIGHEST))
    bias = jnp.einsum('ijn,nh->hij', onehot, table, precision=HIGHEST)
    mixed = both_ways(attend(query, keys, values, bias, causal))
    after_self = tokens + low_back(jnp.dot(mixed, self_out, precision=HIGHEST))
    normed = low(rms_norm(after_self, gains[1]))
    query = both_ways(jnp.dot(normed, cross_q, precision=HIGHEST))
    keys = both_ways(jnp.dot(memory, cross_kv[:, 0], precision=HIGHEST))
    values = both_ways(jnp.dot(memory, cross_kv[:, 1], precision=HIGHEST))
    mixed = both_ways(attend(query, keys, values, None, None))
    after_cross = after_self + low_back(jnp.dot(mixed, cross_out, precision=HIGHEST))
    normed = low(rms_norm(after_cross, gains[2]))
    gate = low_back(jnp.dot(normed, gate_up[:, 0], precision=HIGHEST))
    up = low_back(jnp.dot(normed, gate_up[:, 1], precision=HIGHEST))
    hidden = low(jax.nn.gelu(gate, approximate=True) * up)
    return after_cross + low_back(jnp.dot(hidden, down, precision=HIGHEST))

def reference(decoder_in, memory, buckets, norm_gains, rel_bias, self_q, self_kv, self_out, cross_q, cross_kv, cross_out, gate_up, down, cotangent):
    weights = tuple((weight.astype(jnp.float32) for weight in (norm_gains, rel_bias, self_q, self_kv, self_out, cross_q, cross_kv, cross_out, gate_up, down)))
    positions = jnp.arange(LEN, dtype=jnp.int32)
    causal = positions[:, None] >= positions[None, :]
    onehot = (buckets[:, :, None] == jnp.arange(NB, dtype=jnp.int32)[None, None, :]).astype(jnp.float32)

    def one_sequence(totals, inputs):
        sequence_tokens, sequence_memory, sequence_grad = inputs

        def forward(tokens, memory_rows, weight_set):
            return layer(tokens, memory_rows, weight_set, onehot, causal)
        output, pull = jax.vjp(forward, sequence_tokens.astype(jnp.float32), sequence_memory.astype(jnp.float32), weights)
        grad_tokens, grad_memory, grad_weights = pull(sequence_grad.astype(jnp.float32))
        totals = jax.tree.map(jnp.add, totals, grad_weights)
        return (totals, (output.astype(jnp.bfloat16), grad_tokens, grad_memory.astype(jnp.bfloat16)))
    start = jax.tree.map(jnp.zeros_like, weights)
    totals, (outputs, token_grads, memory_grads) = lax.scan(one_sequence, start, (decoder_in, memory, cotangent))
    return (outputs, token_grads, memory_grads, totals[0], totals[1], totals[2], totals[3], totals[4], totals[5], totals[6], totals[7], totals[8], totals[9])
```

```python
import jax
import jax.numpy as jnp
from jax import lax
from jax.experimental import pallas as pl
from jax.experimental.pallas import tpu as pltpu
from jax.sharding import PartitionSpec as P

DH = 64
NB = 32
MICRO = 2


EPSILON = 1e-06
MASKED = -1e30


def rms_norm(values, gain):
    return values * lax.rsqrt(jnp.mean(values * values, axis=-1, keepdims=True) + EPSILON) * gain


def gelu_product(gate, up):
    return jax.nn.gelu(gate, approximate=True) * up


def flatten(weight):
    return weight.reshape(weight.shape[0], -1)


def gather_weights(
    gains, table, self_q, self_kv, self_out, cross_q, cross_kv, cross_out, gate_up, down
):
    return (
        lax.all_gather(gains, ("seq", "fsdp"), axis=1, tiled=True),
        lax.all_gather(table, ("seq", "fsdp"), axis=0, tiled=True),
        lax.all_gather(self_q, ("seq", "fsdp"), axis=0, tiled=True),
        lax.all_gather(self_kv, ("seq", "fsdp"), axis=0, tiled=True),
        lax.all_gather(self_out, ("seq", "fsdp"), axis=1, tiled=True),
        lax.all_gather(cross_q, ("seq", "fsdp"), axis=0, tiled=True),
        lax.all_gather(cross_kv, ("seq", "fsdp"), axis=0, tiled=True),
        lax.all_gather(cross_out, ("seq", "fsdp"), axis=1, tiled=True),
        lax.all_gather(gate_up, ("seq", "fsdp"), axis=0, tiled=True),
        lax.all_gather(down, ("seq", "fsdp"), axis=1, tiled=True),
    )


def branch_total(partial_value):
    return lax.psum(partial_value.astype(jnp.bfloat16), "tp").astype(jnp.float32)


def input_total(partial_value):
    return lax.psum(partial_value.astype(jnp.bfloat16), "tp").astype(jnp.float32)


def split_heads(query, keys, values):
    batch, rows, width = query.shape
    span = keys.shape[1]
    groups = keys.shape[2] // DH
    ratio = width // DH // groups
    return (
        query.reshape(batch, rows, groups, ratio, DH),
        keys.reshape(batch, span, groups, DH),
        values.reshape(batch, span, groups, DH),
    )


def scores_of(query_heads, key_heads, bias, causal):
    scores = jnp.einsum(
        "bigrd,bjgd->bgrij", query_heads, key_heads, preferred_element_type=jnp.float32
    ) * DH ** (-0.5)
    if bias is not None:
        scores = scores + bias
    if causal is not None:
        scores = jnp.where(causal, scores, MASKED)
    return scores


def attend_forward(query, keys, values, bias, causal):
    query_heads, key_heads, value_heads = split_heads(query, keys, values)
    scores = scores_of(query_heads, key_heads, bias, causal)
    row_max = jnp.max(scores, axis=-1, keepdims=True)
    exponent = jnp.exp(scores - row_max)
    total = jnp.sum(exponent, axis=-1, keepdims=True)
    probs = (exponent / total).astype(jnp.bfloat16)
    mixed = jnp.einsum("bgrij,bjgd->bigrd", probs, value_heads, preferred_element_type=jnp.float32)
    return (mixed.reshape(query.shape).astype(jnp.bfloat16), row_max + jnp.log(total))


def attend_backward(query, keys, values, bias, causal, log_total, grad_mixed):
    query_heads, key_heads, value_heads = split_heads(query, keys, values)
    probs = jnp.exp(scores_of(query_heads, key_heads, bias, causal) - log_total)
    grad_heads = grad_mixed.reshape(query_heads.shape)
    grad_probs = jnp.einsum(
        "bigrd,bjgd->bgrij", grad_heads, value_heads, preferred_element_type=jnp.float32
    )
    inner = jnp.sum(probs * grad_probs, axis=-1, keepdims=True)
    grad_scores = (probs * (grad_probs - inner)).astype(jnp.bfloat16)
    scale = DH ** (-0.5)
    grad_query = (
        jnp.einsum("bgrij,bjgd->bigrd", grad_scores, key_heads, preferred_element_type=jnp.float32)
        * scale
    ).astype(jnp.bfloat16)
    grad_keys = (
        jnp.einsum(
            "bgrij,bigrd->bjgd", grad_scores, query_heads, preferred_element_type=jnp.float32
        )
        * scale
    ).astype(jnp.bfloat16)
    grad_values = jnp.einsum(
        "bgrij,bigrd->bjgd",
        probs.astype(jnp.bfloat16),
        grad_heads,
        preferred_element_type=jnp.float32,
    ).astype(jnp.bfloat16)
    return (
        grad_query.reshape(query.shape),
        grad_keys.reshape(keys.shape),
        grad_values.reshape(values.shape),
        grad_scores,
    )


def forward(tokens, memory, weights, onehot, causal):
    gains, table, self_q, self_kv, self_out, cross_q, cross_kv, cross_out, gate_up, down = weights
    gain_rows = gains.astype(jnp.float32)
    start = tokens.astype(jnp.float32)
    normed_self = rms_norm(start, gain_rows[0]).astype(jnp.bfloat16)
    query_self = jnp.dot(normed_self, self_q, preferred_element_type=jnp.float32).astype(
        jnp.bfloat16
    )
    pair_self = jnp.dot(normed_self, flatten(self_kv), preferred_element_type=jnp.float32).astype(
        jnp.bfloat16
    )
    half = pair_self.shape[-1] // 2
    keys_self = pair_self[..., :half]
    values_self = pair_self[..., half:]
    groups = half // DH
    heads = table.shape[1]
    rows = tokens.shape[1]
    bias = jnp.einsum("ijn,nh->hij", onehot, table, preferred_element_type=jnp.float32).reshape(
        groups, heads // groups, rows, rows
    )
    mixed_self, log_self = attend_forward(query_self, keys_self, values_self, bias, causal)
    after_self = start + branch_total(
        jnp.dot(mixed_self, self_out, preferred_element_type=jnp.float32)
    )
    normed_cross = rms_norm(after_self, gain_rows[1]).astype(jnp.bfloat16)
    query_cross = jnp.dot(normed_cross, cross_q, preferred_element_type=jnp.float32).astype(
        jnp.bfloat16
    )
    pair_cross = jnp.dot(memory, flatten(cross_kv), preferred_element_type=jnp.float32).astype(
        jnp.bfloat16
    )
    keys_cross = pair_cross[..., :half]
    values_cross = pair_cross[..., half:]
    mixed_cross, log_cross = attend_forward(query_cross, keys_cross, values_cross, None, None)
    after_cross = after_self + branch_total(
        jnp.dot(mixed_cross, cross_out, preferred_element_type=jnp.float32)
    )
    normed_ffn = rms_norm(after_cross, gain_rows[2]).astype(jnp.bfloat16)
    joined = jnp.dot(normed_ffn, flatten(gate_up), preferred_element_type=jnp.float32)
    hidden_width = joined.shape[-1] // 2
    gate = joined[..., :hidden_width]
    up = joined[..., hidden_width:]
    hidden = gelu_product(gate, up).astype(jnp.bfloat16)
    output = after_cross + branch_total(jnp.dot(hidden, down, preferred_element_type=jnp.float32))
    saved = (
        start,
        after_self,
        after_cross,
        normed_self,
        query_self,
        keys_self,
        values_self,
        bias,
        mixed_self,
        log_self,
        normed_cross,
        query_cross,
        keys_cross,
        values_cross,
        mixed_cross,
        log_cross,
        normed_ffn,
        gate,
        up,
        hidden,
    )
    return (output, saved)


def backward(saved, grad_out, memory, weights, onehot, causal):
    (
        start,
        after_self,
        after_cross,
        normed_self,
        query_self,
        keys_self,
        values_self,
        bias,
        mixed_self,
        log_self,
        normed_cross,
        query_cross,
        keys_cross,
        values_cross,
        mixed_cross,
        log_cross,
        normed_ffn,
        gate,
        up,
        hidden,
    ) = saved
    gains, table, self_q, self_kv, self_out, cross_q, cross_kv, cross_out, gate_up, down = weights
    gain_rows = gains.astype(jnp.float32)
    grad_ffn = grad_out.astype(jnp.float32)
    rounded = grad_ffn.astype(jnp.bfloat16)
    down_grad = jnp.einsum("blf,bld->fd", hidden, rounded, preferred_element_type=jnp.float32)
    grad_hidden = jnp.einsum("bld,fd->blf", rounded, down, preferred_element_type=jnp.float32)
    _, pull = jax.vjp(gelu_product, gate, up)
    grad_gate, grad_up = pull(grad_hidden)
    grad_joined = jnp.concatenate([grad_gate, grad_up], axis=-1).astype(jnp.bfloat16)
    gate_up_grad = jnp.einsum(
        "bld,blf->df", normed_ffn, grad_joined, preferred_element_type=jnp.float32
    ).reshape(gate_up.shape)
    grad_normed = input_total(
        jnp.einsum("blf,df->bld", grad_joined, flatten(gate_up), preferred_element_type=jnp.float32)
    )
    _, pull = jax.vjp(rms_norm, after_cross, gain_rows[2])
    grad_residual, gain_ffn = pull(grad_normed)
    grad_cross = grad_ffn + grad_residual
    rounded = grad_cross.astype(jnp.bfloat16)
    cross_out_grad = jnp.einsum(
        "blh,bld->hd", mixed_cross, rounded, preferred_element_type=jnp.float32
    )
    grad_mixed = jnp.einsum(
        "bld,hd->blh", rounded, cross_out, preferred_element_type=jnp.float32
    ).astype(jnp.bfloat16)
    grad_query, grad_keys, grad_values, _ = attend_backward(
        query_cross, keys_cross, values_cross, None, None, log_cross, grad_mixed
    )
    grad_pair_cross = jnp.concatenate([grad_keys, grad_values], axis=-1)
    cross_q_grad = jnp.einsum(
        "bld,blh->dh", normed_cross, grad_query, preferred_element_type=jnp.float32
    )
    cross_kv_grad = jnp.einsum(
        "bsd,bsw->dw", memory, grad_pair_cross, preferred_element_type=jnp.float32
    ).reshape(cross_kv.shape)
    grad_normed = input_total(
        jnp.einsum("blh,dh->bld", grad_query, cross_q, preferred_element_type=jnp.float32)
    )
    _, pull = jax.vjp(rms_norm, after_self, gain_rows[1])
    grad_residual, gain_cross = pull(grad_normed)
    grad_self = grad_cross + grad_residual
    rounded = grad_self.astype(jnp.bfloat16)
    self_out_grad = jnp.einsum(
        "blh,bld->hd", mixed_self, rounded, preferred_element_type=jnp.float32
    )
    grad_mixed = jnp.einsum(
        "bld,hd->blh", rounded, self_out, preferred_element_type=jnp.float32
    ).astype(jnp.bfloat16)
    grad_query, grad_keys, grad_values, grad_scores = attend_backward(
        query_self, keys_self, values_self, bias, causal, log_self, grad_mixed
    )
    batch = grad_scores.shape[0]
    rows = grad_scores.shape[-1]
    table_grad = jnp.einsum(
        "ijn,bhij->nh",
        onehot,
        grad_scores.reshape(batch, -1, rows, rows),
        preferred_element_type=jnp.float32,
    )
    grad_pair = jnp.concatenate([grad_keys, grad_values], axis=-1)
    self_q_grad = jnp.einsum(
        "bld,blh->dh", normed_self, grad_query, preferred_element_type=jnp.float32
    )
    self_kv_grad = jnp.einsum(
        "bld,blw->dw", normed_self, grad_pair, preferred_element_type=jnp.float32
    ).reshape(self_kv.shape)
    grad_normed = input_total(
        jnp.einsum("blh,dh->bld", grad_query, self_q, preferred_element_type=jnp.float32)
        + jnp.einsum("blw,dw->bld", grad_pair, flatten(self_kv), preferred_element_type=jnp.float32)
    )
    _, pull = jax.vjp(rms_norm, start, gain_rows[0])
    grad_residual, gain_self = pull(grad_normed)
    grad_tokens = grad_self + grad_residual
    gains_grad = jnp.stack([gain_self, gain_cross, gain_ffn])
    grads = (
        gains_grad,
        table_grad,
        self_q_grad,
        self_kv_grad,
        self_out_grad,
        cross_q_grad,
        cross_kv_grad,
        cross_out_grad,
        gate_up_grad,
        down_grad,
    )
    return (grad_tokens, grad_pair_cross, grads)


def per_device(
    decoder_in,
    memory,
    buckets,
    norm_gains,
    rel_bias,
    self_q,
    self_kv,
    self_out,
    cross_q,
    cross_kv,
    cross_out,
    gate_up,
    down,
    cotangent,
):
    local = decoder_in.shape[0]
    rows = decoder_in.shape[1]
    per_batch = local // MICRO
    positions = jnp.arange(rows, dtype=jnp.int32)
    causal = positions[:, None] >= positions[None, :]
    onehot = (buckets[:, :, None] == jnp.arange(NB, dtype=jnp.int32)[None, None, :]).astype(
        jnp.bfloat16
    )
    weights = gather_weights(
        norm_gains, rel_bias, self_q, self_kv, self_out, cross_q, cross_kv, cross_out, gate_up, down
    )
    outputs = []
    token_grads = []
    memory_grads = []
    totals = None
    for index in range(MICRO):
        lower = index * per_batch
        upper = lower + per_batch
        memory_part = memory[lower:upper]
        output, saved = forward(decoder_in[lower:upper], memory_part, weights, onehot, causal)
        grad_tokens, grad_pair_cross, grads = backward(
            saved, cotangent[lower:upper], memory_part, weights, onehot, causal
        )
        memory_term = jnp.einsum(
            "bsw,dw->bsd", grad_pair_cross, flatten(weights[6]), preferred_element_type=jnp.float32
        )
        memory_part_grad = lax.psum_scatter(
            memory_term.astype(jnp.bfloat16), "tp", scatter_dimension=2, tiled=True
        )
        memory_grads.append(memory_part_grad)
        outputs.append(output.astype(jnp.bfloat16))
        token_grads.append(grad_tokens)
        grads = (
            lax.psum_scatter(
                grads[0].astype(jnp.bfloat16), ("seq", "fsdp"), scatter_dimension=1, tiled=True
            ).astype(jnp.float32),
            lax.psum_scatter(
                grads[1].astype(jnp.bfloat16), ("seq", "fsdp"), scatter_dimension=0, tiled=True
            ).astype(jnp.float32),
            lax.psum_scatter(
                grads[2].astype(jnp.bfloat16), ("seq", "fsdp"), scatter_dimension=0, tiled=True
            ).astype(jnp.float32),
            lax.psum_scatter(
                grads[3].astype(jnp.bfloat16), ("seq", "fsdp"), scatter_dimension=0, tiled=True
            ).astype(jnp.float32),
            lax.psum_scatter(
                grads[4].astype(jnp.bfloat16), ("seq", "fsdp"), scatter_dimension=1, tiled=True
            ).astype(jnp.float32),
            lax.psum_scatter(
                grads[5].astype(jnp.bfloat16), ("seq", "fsdp"), scatter_dimension=0, tiled=True
            ).astype(jnp.float32),
            lax.psum_scatter(
                grads[6].astype(jnp.bfloat16), ("seq", "fsdp"), scatter_dimension=0, tiled=True
            ).astype(jnp.float32),
            lax.psum_scatter(
                grads[7].astype(jnp.bfloat16), ("seq", "fsdp"), scatter_dimension=1, tiled=True
            ).astype(jnp.float32),
            lax.psum_scatter(
                grads[8].astype(jnp.bfloat16), ("seq", "fsdp"), scatter_dimension=0, tiled=True
            ).astype(jnp.float32),
            lax.psum_scatter(
                grads[9].astype(jnp.bfloat16), ("seq", "fsdp"), scatter_dimension=1, tiled=True
            ).astype(jnp.float32),
        )
        totals = grads if totals is None else jax.tree.map(jnp.add, totals, grads)
    return (
        jnp.concatenate(outputs, axis=0),
        jnp.concatenate(token_grads, axis=0),
        jnp.concatenate(memory_grads, axis=0),
        totals[0],
        totals[1],
        totals[2],
        totals[3],
        totals[4],
        totals[5],
        totals[6],
        totals[7],
        totals[8],
        totals[9],
    )


GROUP = 128


def lane_blocks(value):
    count = value.shape[1] // GROUP
    return jnp.concatenate(
        [value[:, b * GROUP : (b + 1) * GROUP] for b in range(count)], axis=0
    )


def dot(left, right):
    return jnp.dot(left, right, preferred_element_type=jnp.float32)


def dot_t(left, right):
    return lax.dot_general(left, right, (((1,), (1,)), ((), ())), preferred_element_type=jnp.float32)


def t_dot(left, right):
    return lax.dot_general(left, right, (((0,), (0,)), ((), ())), preferred_element_type=jnp.float32)


def low(value):
    return value.astype(jnp.bfloat16)


def high(value):
    return value.astype(jnp.float32)


def norm_backward(values, gain, cotangent):
    _, pull = jax.vjp(rms_norm, values, gain)
    return pull(cotangent)


def stacked(block, pair, lanes):
    block = high(block[:, pair * GROUP : (pair + 1) * GROUP])
    other = pltpu.roll(block, DH, 1)
    if pair == 0:
        rows = jnp.concatenate([block, other], axis=0)
        keep = lanes < DH
    else:
        rows = jnp.concatenate([other, block], axis=0)
        keep = lanes >= DH
    return low(jnp.where(keep, rows, 0.0))


def unstacked(parts):
    heads = []
    for pair, value in enumerate(parts):
        half = value[:, pair * DH : (pair + 1) * DH]
        heads += [half[0:GROUP], half[GROUP : 2 * GROUP]]
    return jnp.concatenate(heads, axis=1)


def cross_forward_kernel(q_ref, kv_ref, o_ref, lse_ref, scores, probs):
    span = kv_ref.shape[0]
    chunk = 256
    lanes = lax.broadcasted_iota(jnp.int32, (1, GROUP), 1)
    outs = []
    for pair in range(2):
        query = stacked(q_ref[...], pair, lanes)

        def first(index, best):
            rows = pl.ds(index * chunk, chunk)
            part = dot_t(kv_ref[rows, 0:GROUP], query)
            scores[rows, :] = part
            return jnp.maximum(best, jnp.max(part, axis=0, keepdims=True))

        best = lax.fori_loop(
            0, span // chunk, first, jnp.full((1, 2 * GROUP), MASKED, jnp.float32), unroll=2
        )

        def second(index, total):
            rows = pl.ds(index * chunk, chunk)
            part = jnp.exp(scores[rows, :] - best)
            probs[rows, :] = low(part)
            return total + jnp.sum(part, axis=0, keepdims=True)

        total = lax.fori_loop(
            0, span // chunk, second, jnp.zeros((1, 2 * GROUP), jnp.float32), unroll=2
        )
        mixed = t_dot(kv_ref[:, GROUP : 2 * GROUP], probs[...])
        outs.append((mixed / total).T)
        lse_ref[0, pair : pair + 1, :] = best + jnp.log(total)
    o_ref[...] = low(unstacked(outs))


def inner_of(dout, out):
    return jnp.sum((high(dout) * high(out)).T, axis=0, keepdims=True)


def cross_backward_kernel(q_ref, do_ref, o_ref, kv_ref, lse_ref, dq_ref, dkv_ref, probs, grads):
    span = kv_ref.shape[0]
    chunk = 256
    lanes = lax.broadcasted_iota(jnp.int32, (1, GROUP), 1)
    queries = []
    douts = []
    for pair in range(2):
        query = stacked(q_ref[...], pair, lanes)
        dout = stacked(do_ref[...], pair, lanes)
        inner = inner_of(dout, stacked(o_ref[...], pair, lanes))
        lse = lse_ref[0, pair : pair + 1, :]
        columns = slice(pair * 2 * GROUP, (pair + 1) * 2 * GROUP)

        def step(index, carry):
            rows = pl.ds(index * chunk, chunk)
            prob = jnp.exp(dot_t(kv_ref[rows, 0:GROUP], query) - lse)
            grad = prob * (dot_t(kv_ref[rows, GROUP : 2 * GROUP], dout) - inner)
            probs[rows, columns] = low(prob)
            grads[rows, columns] = low(grad)
            return carry

        lax.fori_loop(0, span // chunk, step, 0, unroll=2)
        queries.append(query)
        douts.append(dout)
    query = jnp.concatenate(queries, axis=0)
    dout = jnp.concatenate(douts, axis=0)
    dkv_ref[:, 0:GROUP] = low(dot(grads[...], query))
    dkv_ref[:, GROUP : 2 * GROUP] = low(dot(probs[...], dout))
    dq = (t_dot(kv_ref[:, 0:GROUP], grads[...]) * DH ** (-0.5)).T
    dq_ref[...] = low(unstacked([dq[0 : 2 * GROUP], dq[2 * GROUP :]]))


def self_scores(kv_ref, query, bias_ref, pair):
    rows = kv_ref.shape[0]
    scores = dot_t(kv_ref[:, 0:GROUP], query)
    scores = scores + jnp.concatenate([bias_ref[2 * pair], bias_ref[2 * pair + 1]], axis=1)
    key_at = lax.broadcasted_iota(jnp.int32, scores.shape, 0)
    query_at = lax.broadcasted_iota(jnp.int32, scores.shape, 1) % rows
    return scores, key_at <= query_at


def self_forward_kernel(q_ref, kv_ref, bias_ref, o_ref, lse_ref):
    lanes = lax.broadcasted_iota(jnp.int32, (1, GROUP), 1)
    outs = []
    for pair in range(2):
        query = stacked(q_ref[...], pair, lanes)
        scores, seen = self_scores(kv_ref, query, bias_ref, pair)
        scores = jnp.where(seen, scores, MASKED)
        best = jnp.max(scores, axis=0, keepdims=True)
        part = jnp.exp(scores - best)
        total = jnp.sum(part, axis=0, keepdims=True)
        mixed = t_dot(kv_ref[:, GROUP : 2 * GROUP], low(part / total))
        outs.append(mixed.T)
        lse_ref[0, pair : pair + 1, :] = best + jnp.log(total)
    o_ref[...] = low(unstacked(outs))


def self_backward_kernel(
    q_ref, do_ref, o_ref, kv_ref, lse_ref, bias_ref, dq_ref, dkv_ref, ds_ref
):
    lanes = lax.broadcasted_iota(jnp.int32, (1, GROUP), 1)
    dqs = []
    dk = 0.0
    dv = 0.0
    for pair in range(2):
        query = stacked(q_ref[...], pair, lanes)
        dout = stacked(do_ref[...], pair, lanes)
        inner = inner_of(dout, stacked(o_ref[...], pair, lanes))
        scores, seen = self_scores(kv_ref, query, bias_ref, pair)
        prob = jnp.exp(jnp.where(seen, scores - lse_ref[0, pair : pair + 1, :], MASKED))
        grad = low(prob * (dot_t(kv_ref[:, GROUP : 2 * GROUP], dout) - inner))
        ds_ref[2 * pair] = grad[:, 0:GROUP]
        ds_ref[2 * pair + 1] = grad[:, GROUP : 2 * GROUP]
        dk = dk + dot(grad, query)
        dv = dv + dot(low(prob), dout)
        dqs.append((t_dot(kv_ref[:, 0:GROUP], grad) * DH ** (-0.5)).T)
    dkv_ref[:, 0:GROUP] = low(dk)
    dkv_ref[:, GROUP : 2 * GROUP] = low(dv)
    dq_ref[...] = low(unstacked(dqs))


def attention_specs(rows, span):
    narrow = pl.BlockSpec((rows, 2 * GROUP), lambda k: (0, k))
    tall = pl.BlockSpec((span, 2 * GROUP), lambda k: (0, k))
    lse = pl.BlockSpec((1, 2, 2 * GROUP), lambda k: (k, 0, 0))
    square = pl.BlockSpec((4, rows, rows), lambda k: (k, 0, 0))
    return narrow, tall, lse, square


def kernel_call(kernel, name, blocks, specs, outs, scratch, cost, arguments, limit=32):
    return pl.pallas_call(
        kernel,
        grid=(blocks,),
        in_specs=specs,
        out_specs=[spec for spec, _, _ in outs],
        out_shape=[jax.ShapeDtypeStruct(shape, kind) for _, shape, kind in outs],
        scratch_shapes=scratch,
        compiler_params=pltpu.CompilerParams(vmem_limit_bytes=limit * 2**20),
        cost_estimate=pl.CostEstimate(flops=cost[0], bytes_accessed=cost[1], transcendentals=cost[2]),
        name=name,
    )(*arguments)


def attention_forward(query, pairs, bias):
    rows, span = query.shape[0], pairs.shape[0]
    blocks = query.shape[1] // (2 * GROUP)
    narrow, tall, lse, square = attention_specs(rows, span)
    cost = (
        16 * rows * span * DH * blocks,
        2 * (2 * query.size + pairs.size),
        4 * rows * span * blocks,
    )
    outs = [
        (narrow, query.shape, jnp.bfloat16),
        (lse, (blocks, 2, 2 * GROUP), jnp.float32),
    ]
    if bias is not None:
        return kernel_call(
            self_forward_kernel,
            "self_forward",
            blocks,
            [narrow, tall, square],
            outs,
            [],
            cost,
            (query, pairs, bias),
        )
    return kernel_call(
        cross_forward_kernel,
        "cross_forward",
        blocks,
        [narrow, tall],
        outs,
        [
            pltpu.VMEM((span, 2 * GROUP), jnp.float32),
            pltpu.VMEM((span, 2 * GROUP), jnp.bfloat16),
        ],
        cost,
        (query, pairs),
    )


def attention_backward(query, dout, out, pairs, lse_value, bias):
    rows, span = query.shape[0], pairs.shape[0]
    blocks = query.shape[1] // (2 * GROUP)
    narrow, tall, lse, square = attention_specs(rows, span)
    cost = (
        40 * rows * span * DH * blocks,
        2 * (4 * query.size + 2 * pairs.size),
        4 * rows * span * blocks,
    )
    outs = [(narrow, query.shape, jnp.bfloat16), (tall, pairs.shape, jnp.bfloat16)]
    if bias is not None:
        return kernel_call(
            self_backward_kernel,
            "self_backward",
            blocks,
            [narrow, narrow, narrow, tall, lse, square],
            outs + [(square, (4 * blocks, rows, rows), jnp.bfloat16)],
            [],
            cost,
            (query, dout, out, pairs, lse_value, bias),
        )
    return kernel_call(
        cross_backward_kernel,
        "cross_backward",
        blocks,
        [narrow, narrow, narrow, tall, lse],
        outs,
        [pltpu.VMEM((span, 4 * GROUP), jnp.bfloat16)] * 2,
        cost,
        (query, dout, out, pairs, lse_value),
    )


def with_index(kernel, name, grid, specs, outs, scratch, cost, index, arguments, limit=32):
    return pl.pallas_call(
        kernel,
        grid_spec=pltpu.PrefetchScalarGridSpec(
            num_scalar_prefetch=1,
            grid=grid,
            in_specs=specs,
            out_specs=[spec for spec, _, _ in outs],
            scratch_shapes=scratch,
        ),
        out_shape=[jax.ShapeDtypeStruct(shape, kind) for _, shape, kind in outs],
        compiler_params=pltpu.CompilerParams(vmem_limit_bytes=limit * 2**20),
        cost_estimate=pl.CostEstimate(flops=cost[0], bytes_accessed=cost[1], transcendentals=0),
        name=name,
    )(index, *arguments)


def unpack_heads(index, near, far, depth, top, rows_first, width, extra):
    tp = near[0].shape[0]
    listed = isinstance(far[0], list)
    seq = (far[0][0].shape[0] if listed else far[0].shape[1]) + 1
    shard = width // (2 * seq)
    sides = tuple(far[0]) + tuple(far[1]) if listed else tuple(far)

    def kernel(index_ref, *refs):
        near_refs, far_refs = refs[0:2], refs[2 : 2 + len(sides)]
        outs = refs[2 + len(sides) :]

        def place(q, side, read):
            row = 2 * (index_ref[0] ^ q) + (index_ref[2] ^ side)
            at = pl.ds(pl.multiple_of(row * shard, shard), shard)
            for entry, (out, down) in enumerate(zip(outs, rows_first)):
                start = entry * 2 * shard
                if down:
                    out[:, at] = read(start, 2 * shard)
                else:
                    for b in range(2):
                        out[at, b * GROUP : (b + 1) * GROUP] = read(start + b * shard, shard)
            if extra:
                outs[-1][0, row] = read(depth - extra, extra)

        for side in range(2):
            place(0, side, lambda start, size: near_refs[side][0, top + start : top + start + size, :])
            for q in range(1, seq):
                if listed:
                    for k in range(tp):

                        @pl.when(pl.program_id(0) == k)
                        def _():
                            ref = far_refs[side * tp + k]
                            place(q, side, lambda start, size: ref[q - 1, start : start + size, :])

                else:
                    place(
                        q,
                        side,
                        lambda start, size: far_refs[side][0, q - 1, start : start + size, :],
                    )

    specs = [pl.BlockSpec((1,) + near[0].shape[1:], lambda k, index: (k ^ index[1], 0, 0))] * 2
    for value in sides:
        if listed:
            specs.append(pl.BlockSpec(value.shape, lambda k, index: (0, 0, 0)))
        else:
            specs.append(
                pl.BlockSpec((1,) + value.shape[1:], lambda k, index: (k ^ index[1], 0, 0, 0))
            )
    outs = []
    for down in rows_first:
        if down:
            spec = pl.BlockSpec((2 * GROUP, width), lambda k, index: (k, 0))
            outs.append((spec, (tp * 2 * GROUP, width), jnp.bfloat16))
        else:
            spec = pl.BlockSpec((width, 2 * GROUP), lambda k, index: (0, k))
            outs.append((spec, (width, tp * 2 * GROUP), jnp.bfloat16))
    if extra:
        spec = pl.BlockSpec((1, 2 * seq, extra, GROUP), lambda k, index: (k, 0, 0, 0))
        outs.append((spec, (tp, 2 * seq, extra, GROUP), jnp.bfloat16))
    return with_index(
        kernel,
        "unpack_heads",
        (tp,),
        specs,
        outs,
        [],
        (0, 8 * tp * seq * depth * GROUP),
        index,
        (*near, *sides),
    )


def unpack_hidden(value, width, hidden_width):
    count = value.shape[0]
    shard = width // count
    columns = 2 * hidden_width // GROUP

    def kernel(in_ref, gate_up_ref, down_ref):
        for b in range(columns):
            gate_up_ref[:, b * GROUP : (b + 1) * GROUP] = in_ref[0, b * shard : (b + 1) * shard, :]
        down_ref[...] = in_ref[0, columns * shard :, :]

    return kernel_call(
        kernel,
        "unpack_hidden",
        count,
        [pl.BlockSpec((1, value.shape[1], GROUP), lambda k: (k, 0, 0))],
        [
            (
                pl.BlockSpec((shard, 2 * hidden_width), lambda k: (k, 0)),
                (width, 2 * hidden_width),
                jnp.bfloat16,
            ),
            (
                pl.BlockSpec((hidden_width, shard), lambda k: (0, k)),
                (hidden_width, width),
                jnp.bfloat16,
            ),
        ],
        [],
        (0, 4 * value.size, 0),
        (value,),
    )


def memory_terms(index, pairs, weight, tp):
    rows, width = pairs.shape
    features = weight.shape[0] // tp
    steps = 4
    block = rows // steps

    def kernel(index_ref, pairs_ref, weight_ref, *outs):
        for k, out in enumerate(outs):
            at = pl.multiple_of((index_ref[1] ^ k) * features, features)
            out[...] = low(dot_t(pairs_ref[...], weight_ref[pl.ds(at, features), :]))

    spec = pl.BlockSpec((block, features), lambda k, index: (k, 0))
    return with_index(
        kernel,
        "memory_terms",
        (steps,),
        [
            pl.BlockSpec((block, width), lambda k, index: (k, 0)),
            pl.BlockSpec(weight.shape, lambda k, index: (0, 0)),
        ],
        [(spec, (rows, features), jnp.bfloat16)] * tp,
        [],
        (2 * rows * width * weight.shape[0], 2 * (2 * pairs.size + weight.size)),
        index,
        (pairs, weight),
    )


def hidden_out(index, hidden, weight, values, tp):
    rows = hidden.shape[0] // tp
    width = weight.shape[1]

    def kernel(index_ref, hidden_ref, weight_ref, values_ref, out_ref):
        part = dot(hidden_ref[...], weight_ref[...])

        @pl.when(pl.program_id(0) == 0)
        def _():
            out_ref[0] = low(part + values_ref[...])

        @pl.when(pl.program_id(0) != 0)
        def _():
            out_ref[0] = low(part)

    return with_index(
        kernel,
        "hidden_out",
        (tp,),
        [
            pl.BlockSpec((rows, hidden.shape[1]), lambda k, index: (k, 0)),
            pl.BlockSpec(weight.shape, lambda k, index: (0, 0)),
            pl.BlockSpec(values.shape, lambda k, index: (0, 0)),
        ],
        [
            (
                pl.BlockSpec((1, rows, width), lambda k, index: (k ^ index[1], 0, 0)),
                (tp, rows, width),
                jnp.bfloat16,
            )
        ],
        [],
        (2 * hidden.size * width, 2 * (hidden.size + weight.size + tp * rows * width)),
        index,
        (hidden, weight, values),
    )[0]


def row_terms(index, seq, name, pairs):
    rows = pairs[0][0].shape[-2]
    width = pairs[0][0].shape[-1]
    shard = width // (2 * seq)
    columns = sum(right.shape[1] for _, right in pairs)

    def row_of(step, index):
        return 2 * (index[0] ^ (step % seq)) + (index[2] ^ (1 - step // seq))

    def kernel(index_ref, *refs):
        sent_ref, kept_ref = refs[-2:]
        parts = []
        for entry in range(len(pairs)):
            left, right = refs[2 * entry], refs[2 * entry + 1]
            left = left[0] if len(left.shape) == 3 else left[...]
            parts.append(t_dot(left, right[...]))

        def put(ref, kind):
            at = 0
            for part in parts:
                ref[0, :, at : at + part.shape[1]] = part.astype(kind)
                at += part.shape[1]

        @pl.when(pl.program_id(0) < seq)
        def _():
            put(sent_ref, jnp.bfloat16)

        @pl.when(pl.program_id(0) >= seq)
        def _():
            put(kept_ref, jnp.float32)

    specs = []
    arguments = []
    for left, right in pairs:
        if left.ndim == 3:
            specs.append(
                pl.BlockSpec((1, rows, shard), lambda s, index: (index[1], 0, row_of(s, index)))
            )
        else:
            specs.append(pl.BlockSpec((rows, shard), lambda s, index: (0, row_of(s, index))))
        specs.append(pl.BlockSpec(right.shape, lambda s, index: (0, 0)))
        arguments += [left, right]
    shape = (seq, shard, columns)
    block = (1, shard, columns)
    return with_index(
        kernel,
        name,
        (2 * seq,),
        specs,
        [
            (
                pl.BlockSpec(block, lambda s, index: (jnp.minimum(s, seq - 1), 0, 0)),
                shape,
                jnp.bfloat16,
            ),
            (
                pl.BlockSpec(block, lambda s, index: (jnp.maximum(s - seq, 0), 0, 0)),
                shape,
                jnp.float32,
            ),
        ],
        [],
        (2 * rows * width * columns, 2 * rows * (width + columns) + 3 * width * columns),
        index,
        tuple(arguments),
    )


def hidden_terms(normed, grad_joined, rounded, hidden):
    rows, width = normed.shape
    columns = grad_joined.shape[1] + hidden.shape[1]
    split = grad_joined.shape[1]
    steps = width // GROUP

    def kernel(normed_ref, joined_ref, rounded_ref, hidden_ref, out_ref):
        out_ref[:, :split] = low(t_dot(normed_ref[...], joined_ref[...]))
        out_ref[:, split:] = low(t_dot(rounded_ref[...], hidden_ref[...]))

    left = pl.BlockSpec((rows, GROUP), lambda k: (0, k))
    return kernel_call(
        kernel,
        "hidden_terms",
        steps,
        [
            left,
            pl.BlockSpec(grad_joined.shape, lambda k: (0, 0)),
            left,
            pl.BlockSpec(hidden.shape, lambda k: (0, 0)),
        ],
        [(pl.BlockSpec((GROUP, columns), lambda k: (k, 0)), (width, columns), jnp.bfloat16)],
        [],
        (2 * rows * width * columns, 4 * rows * (width + columns) + 2 * width * columns, 0),
        (normed, grad_joined, rounded, hidden),
    )[0]


def one_each(seq, tp):
    everyone = ("seq", "tp", "fsdp")

    def after(value, *earlier):
        return lax.optimization_barrier((value, earlier))[0]

    def swap(value, axis, flip):
        size = {"seq": seq, "tp": tp, "fsdp": 2}[axis]
        return lax.ppermute(value, axis, [(place, place ^ flip) for place in range(size)])

    def gather(value, axis, size):
        return [value] + [swap(value, axis, flip) for flip in range(1, size)]

    def exchange(parts, axis):
        return [parts[0]] + [swap(parts[k], axis, k) for k in range(1, len(parts))]

    def exchange_all(value):
        return lax.all_to_all(value, "tp", 0, 0, tiled=True)

    def to_everyone(value):
        return exchange_all(jnp.broadcast_to(value[None], (tp,) + value.shape))

    def total(parts):
        result = high(parts[0])
        for part in parts[1:]:
            result = result + high(part)
        return result

    def run(
        decoder_in,
        memory,
        buckets,
        norm_gains,
        rel_bias,
        self_q,
        self_kv,
        self_out,
        cross_q,
        cross_kv,
        cross_out,
        gate_up,
        down,
        cotangent,
    ):
        count, rows, width = decoder_in.shape
        z = lax.axis_index("seq")
        t = lax.axis_index("tp")
        c = lax.axis_index("fsdp")
        index = jnp.stack([z, t, c]).astype(jnp.int32)
        cores = 2
        shard = self_q.shape[0]
        tables = rel_bias.shape[0]
        heads = rel_bias.shape[1]
        hidden_width = down.shape[0]
        extra = 16

        def own(value):
            return lax.dynamic_index_in_dim(value, t, 0, keepdims=False)

        def from_here(value):
            return [
                lax.dynamic_index_in_dim(value, t ^ k, 0, keepdims=False) for k in range(tp)
            ]

        def in_order(parts, kind):
            result = jnp.zeros((count,) + parts[0].shape, kind)
            for k, part in enumerate(parts):
                result = lax.dynamic_update_index_in_dim(result, part.astype(kind), t ^ k, 0)
            return result

        def head_blocks(value):
            size = value.shape[1] // tp
            return [value[:, k * size : (k + 1) * size] for k in range(tp)]

        small = jnp.concatenate(
            [
                norm_gains,
                jnp.pad(rel_bias.reshape(1, -1), ((0, 0), (0, GROUP - rel_bias.size))),
                jnp.zeros((extra - 4, GROUP), jnp.bfloat16),
            ],
            axis=0,
        )
        pack_a = jnp.concatenate(
            [lane_blocks(flatten(cross_kv)), lane_blocks(self_q), lane_blocks(flatten(self_kv)), small],
            axis=0,
        )
        pack_b = jnp.concatenate([self_out, lane_blocks(cross_q), cross_out], axis=0)
        pack_f = jnp.concatenate([lane_blocks(flatten(gate_up)), down], axis=0)

        depth_a, depth_b = pack_a.shape[0], pack_b.shape[0]
        near = to_everyone(jnp.concatenate([pack_a, pack_b], axis=0))
        ring_a = gather(pack_a, "seq", seq)
        ring_b = gather(after(pack_b, *ring_a), "seq", seq)
        far_a = to_everyone(after(jnp.stack(ring_a[1:]), near))
        far_b = gather(after(jnp.stack(ring_b[1:]), far_a), "tp", tp)
        full_f = lax.all_gather(after(pack_f, *ring_b), ("seq", "fsdp"), axis=0, tiled=True)
        near = [near, swap(near, "fsdp", 1)]
        far_a = [far_a, swap(far_a, "fsdp", 1)]

        cross_pairs, weight_self_q, weight_self_kv, smalls = unpack_heads(
            index, near, far_a, depth_a, 0, (False, False, False), width, extra
        )
        weight_gate_up, weight_down = unpack_hidden(
            full_f.reshape(seq * cores, -1, GROUP), width, hidden_width
        )
        gain_rows = high(smalls[0, :, 0:3].transpose(1, 0, 2).reshape(3, width))
        table = smalls[:, :, 3, 0 : tables * heads].reshape(tp, seq * cores, tables, heads)
        table = table.transpose(1, 2, 0, 3).reshape(NB, tp * heads)
        onehot = (
            buckets.T[:, :, None] == jnp.arange(NB, dtype=jnp.int32)[None, None, :]
        ).astype(jnp.bfloat16)
        bias = jnp.einsum("jin,nh->hji", onehot, table, preferred_element_type=jnp.float32)

        pairs = low(dot(own(memory), cross_pairs))
        start = high(own(decoder_in))
        scale = DH ** (-0.5)

        normed_self = low(rms_norm(start, gain_rows[0]))
        query_self = low(dot(normed_self, weight_self_q) * scale)
        pair_self = low(dot(normed_self, weight_self_kv))
        mixed_self, log_self = attention_forward(query_self, pair_self, bias)
        far_b = [after(part, mixed_self, pairs) for part in far_b]
        far_b = [far_b, [swap(part, "fsdp", 1) for part in far_b]]
        weight_self_out, weight_cross_q, weight_cross_out = unpack_heads(
            index, near, far_b, depth_b, depth_a, (True, False, True), width, 0
        )
        after_self = start + dot(mixed_self, weight_self_out)

        normed_cross = low(rms_norm(after_self, gain_rows[1]))
        query_cross = low(dot(normed_cross, weight_cross_q) * scale)
        mixed_cross, log_cross = attention_forward(query_cross, pairs, None)
        after_cross = after_self + dot(mixed_cross, weight_cross_out)
        normed_ffn = low(rms_norm(after_cross, gain_rows[2]))

        all_cross = lax.all_gather(normed_cross, "tp", axis=0, tiled=True)
        all_normed = jnp.concatenate(gather(normed_ffn, "tp", tp), axis=0)
        rounded = jnp.concatenate(from_here(cotangent), axis=0)
        joined = dot(all_normed, weight_gate_up)
        gate = joined[:, :hidden_width]
        up = joined[:, hidden_width:]
        grad_hidden = dot_t(rounded, weight_down)
        hidden = low(gelu_product(gate, up))
        _, pull = jax.vjp(gelu_product, gate, up)
        grad_gate, grad_up = pull(grad_hidden)
        grad_joined = low(jnp.concatenate([grad_gate, grad_up], axis=-1))

        def row_parts(value):
            return [value[k * rows : (k + 1) * rows] for k in range(tp)]

        grad_parts = exchange(row_parts(low(dot_t(grad_joined, weight_gate_up))), "tp")
        hidden_grads = hidden_terms(all_normed, grad_joined, rounded, hidden)
        partial_out = hidden_out(index, hidden, weight_down, after_cross, tp)
        grad_normed = total([after(grad_parts[0], hidden_grads, partial_out)] + grad_parts[1:])
        decoder_out = lax.psum(after(partial_out, *grad_parts), "tp")
        hidden_grads = high(
            lax.psum_scatter(hidden_grads, ("seq", "fsdp"), scatter_dimension=0, tiled=True)
        )

        grad_residual, gain_ffn = norm_backward(after_cross, gain_rows[2], grad_normed)
        grad_cross = high(rounded[:rows]) + grad_residual
        rounded_cross = low(grad_cross)
        grad_mixed = low(dot_t(rounded_cross, weight_cross_out))
        cross_parts = exchange(
            [
                jnp.concatenate([rounded_cross, o_self, o_cross], axis=1)
                for o_self, o_cross in zip(head_blocks(mixed_self), head_blocks(mixed_cross))
            ],
            "tp",
        )
        grad_query, grad_pairs = attention_backward(
            query_cross, grad_mixed, mixed_cross, pairs, log_cross, None
        )
        grad_normed = dot_t(grad_query, weight_cross_q)
        grad_residual, gain_cross = norm_backward(after_self, gain_rows[1], grad_normed)
        grad_self = grad_cross + grad_residual
        rounded_self = low(grad_self)
        self_parts = exchange(
            after(
                [
                    jnp.concatenate([rounded_self, block], axis=1)
                    for block in head_blocks(grad_query)
                ],
                *cross_parts,
            ),
            "tp",
        )

        grad_mixed_self = low(dot_t(rounded_self, weight_self_out))
        grad_query_self, grad_pair_self, grad_scores = attention_backward(
            query_self, after(grad_mixed_self, *cross_parts), mixed_self, pair_self, log_self, bias
        )
        grad_normed = dot_t(grad_query_self, weight_self_q) + dot_t(grad_pair_self, weight_self_kv)
        grad_residual, gain_self = norm_backward(start, gain_rows[0], grad_normed)
        grad_tokens = low(grad_self + grad_residual)
        last_parts = [
            jnp.concatenate([grad_tokens, q_block, kv_block], axis=1)
            for q_block, kv_block in zip(head_blocks(grad_query_self), head_blocks(grad_pair_self))
        ]
        grad_pairs = after(grad_pairs, *last_parts, *self_parts)
        last_parts = exchange(after(last_parts, *self_parts), "tp")
        decoder_grad = in_order([part[:, :width] for part in last_parts], jnp.float32)

        memory_grad = in_order(
            exchange(after(memory_terms(index, grad_pairs, cross_pairs, tp), *last_parts), "tp"),
            jnp.bfloat16,
        )

        def core_sum(name, *terms):
            sent, kept = row_terms(index, seq, name, terms)
            return kept + high(swap(sent, "fsdp", 1))

        kv_rows = core_sum("memory_weights", (memory, grad_pairs))
        step = seq // 2
        while step:
            kv_rows = kv_rows[:step] + high(swap(low(kv_rows[step:]), "seq", step))
            step //= 2
        kv_rows = kv_rows[0]
        cross_kv_grad = total(
            exchange([kv_rows[:, : 2 * GROUP]] + head_blocks(low(kv_rows))[1:], "tp")
        )
        all_back = jnp.concatenate(cross_parts, axis=0)
        all_self = jnp.concatenate(self_parts, axis=0)
        all_last = jnp.concatenate([part[:, width:] for part in last_parts], axis=0)
        cross_grads = core_sum(
            "cross_weights",
            (jnp.concatenate(from_here(all_cross.reshape(tp, rows, width)), axis=0), all_self[:, width:]),
            (all_back[:, :width], all_back[:, width + 2 * GROUP :]),
        )
        all_start = low(
            rms_norm(high(jnp.concatenate(from_here(decoder_in), axis=0)), gain_rows[0])
        )
        self_grads = core_sum(
            "self_weights",
            (all_start, all_last),
            (all_self[:, :width], all_back[:, width : width + 2 * GROUP]),
        )

        both_grads = low(jnp.concatenate([cross_grads, self_grads], axis=2))
        both_grads = jnp.concatenate(
            [
                lax.dynamic_index_in_dim(both_grads, z ^ k, 0, keepdims=True) for k in range(seq)
            ],
            axis=0,
        )
        both_grads = jnp.sum(
            high(lax.all_to_all(both_grads, "seq", 0, 0, tiled=True)), axis=0
        )
        cross_grads = both_grads[:, : 4 * GROUP]
        self_grads = both_grads[:, 4 * GROUP :]

        table_grad = jnp.einsum(
            "jin,hji->nh", onehot, grad_scores, preferred_element_type=jnp.float32
        )
        gains = jnp.stack([gain_self, gain_cross, gain_ffn])
        gain_parts = gains.reshape(3, seq, 1, cores, GROUP).transpose(1, 2, 3, 0, 4)
        gain_parts = jnp.broadcast_to(gain_parts, (seq, tp, cores, 3, GROUP))
        table_parts = table_grad.reshape(seq, cores, tables, tp, heads)
        table_parts = jnp.stack(
            [
                lax.dynamic_index_in_dim(table_parts, t ^ k, 3, keepdims=False)
                for k in range(tp)
            ],
            axis=1,
        )
        table_parts = jnp.pad(
            table_parts.reshape(seq, tp, cores, 1, -1),
            ((0, 0),) * 4 + ((0, GROUP - tables * heads),),
        )
        little = jnp.concatenate([gain_parts, table_parts], axis=3)
        little = jnp.pad(low(little), ((0, 0),) * 3 + ((0, 4), (0, 0)))
        little = lax.all_to_all(
            after(little.reshape(-1, 8, GROUP), both_grads), everyone, 0, 0, tiled=True
        )
        little = jnp.sum(high(little), axis=0)

        return (
            decoder_out,
            decoder_grad,
            memory_grad,
            little[0:3],
            little[3, 0 : tables * heads].reshape(tables, heads),
            self_grads[:, 0 : 2 * GROUP],
            self_grads[:, 2 * GROUP : 4 * GROUP].reshape(self_kv.shape),
            self_grads[:, 4 * GROUP :].T,
            cross_grads[:, 0 : 2 * GROUP],
            cross_kv_grad.reshape(cross_kv.shape),
            cross_grads[:, 2 * GROUP :].T,
            hidden_grads[:, : 2 * hidden_width].reshape(gate_up.shape),
            hidden_grads[:, 2 * hidden_width :].T,
        )

    return run


def plan_of(mesh):
    seq, tp, cores = (mesh.shape[axis] for axis in ("seq", "tp", "fsdp"))

    def chosen(*arrays):
        count, rows, width = arrays[0].shape
        fits = (
            cores == 2
            and seq & (seq - 1) == 0
            and tp & (tp - 1) == 0
            and count == tp
            and rows == GROUP
            and width == 2 * seq * GROUP
            and arrays[5].shape[1] == 4 * DH
            and arrays[6].shape[2] == 2 * DH
            and arrays[4].size <= GROUP
            and 2 * arrays[12].shape[0] % GROUP == 0
        )
        return (one_each(seq, tp) if fits else per_device)(*arrays)

    return chosen


def solution(mesh):
    return jax.shard_map(
        plan_of(mesh),
        mesh=mesh,
        in_specs=(
            P(("seq", "fsdp"), None, None),
            P(("seq", "fsdp"), None, None),
            P(),
            P(None, ("seq", "fsdp")),
            P(("seq", "fsdp"), "tp"),
            P(("seq", "fsdp"), "tp"),
            P(("seq", "fsdp"), None, "tp"),
            P("tp", ("seq", "fsdp")),
            P(("seq", "fsdp"), "tp"),
            P(("seq", "fsdp"), None, "tp"),
            P("tp", ("seq", "fsdp")),
            P(("seq", "fsdp"), None, "tp"),
            P("tp", ("seq", "fsdp")),
            P(("seq", "fsdp"), None, None),
        ),
        out_specs=(
            P(("seq", "fsdp"), None, None),
            P(("seq", "fsdp"), None, None),
            P(("seq", "fsdp"), None, "tp"),
            P(None, ("seq", "fsdp")),
            P(("seq", "fsdp"), "tp"),
            P(("seq", "fsdp"), "tp"),
            P(("seq", "fsdp"), None, "tp"),
            P("tp", ("seq", "fsdp")),
            P(("seq", "fsdp"), "tp"),
            P(("seq", "fsdp"), None, "tp"),
            P("tp", ("seq", "fsdp")),
            P(("seq", "fsdp"), None, "tp"),
            P("tp", ("seq", "fsdp")),
        ),
        check_vma=False,
    )
```

```python
import jax
import jax.numpy as jnp
from jax import lax
from jax.experimental import pallas as pl
from jax.experimental.pallas import tpu as pltpu
from jax.sharding import PartitionSpec as P

DH = 64
NB = 32
MICRO = 2


EPSILON = 1e-06
MASKED = -1e30


def rms_norm(values, gain):
    return values * lax.rsqrt(jnp.mean(values * values, axis=-1, keepdims=True) + EPSILON) * gain


def gelu_product(gate, up):
    return jax.nn.gelu(gate, approximate=True) * up


def flatten(weight):
    return weight.reshape(weight.shape[0], -1)


def gather_weights(
    gains, table, self_q, self_kv, self_out, cross_q, cross_kv, cross_out, gate_up, down
):
    return (
        lax.all_gather(gains, ("seq", "fsdp"), axis=1, tiled=True),
        lax.all_gather(table, ("seq", "fsdp"), axis=0, tiled=True),
        lax.all_gather(self_q, ("seq", "fsdp"), axis=0, tiled=True),
        lax.all_gather(self_kv, ("seq", "fsdp"), axis=0, tiled=True),
        lax.all_gather(self_out, ("seq", "fsdp"), axis=1, tiled=True),
        lax.all_gather(cross_q, ("seq", "fsdp"), axis=0, tiled=True),
        lax.all_gather(cross_kv, ("seq", "fsdp"), axis=0, tiled=True),
        lax.all_gather(cross_out, ("seq", "fsdp"), axis=1, tiled=True),
        lax.all_gather(gate_up, ("seq", "fsdp"), axis=0, tiled=True),
        lax.all_gather(down, ("seq", "fsdp"), axis=1, tiled=True),
    )


def branch_total(partial_value):
    return lax.psum(partial_value.astype(jnp.bfloat16), "tp").astype(jnp.float32)


def input_total(partial_value):
    return lax.psum(partial_value.astype(jnp.bfloat16), "tp").astype(jnp.float32)


def split_heads(query, keys, values):
    batch, rows, width = query.shape
    span = keys.shape[1]
    groups = keys.shape[2] // DH
    ratio = width // DH // groups
    return (
        query.reshape(batch, rows, groups, ratio, DH),
        keys.reshape(batch, span, groups, DH),
        values.reshape(batch, span, groups, DH),
    )


def scores_of(query_heads, key_heads, bias, causal):
    scores = jnp.einsum(
        "bigrd,bjgd->bgrij", query_heads, key_heads, preferred_element_type=jnp.float32
    ) * DH ** (-0.5)
    if bias is not None:
        scores = scores + bias
    if causal is not None:
        scores = jnp.where(causal, scores, MASKED)
    return scores


def attend_forward(query, keys, values, bias, causal):
    query_heads, key_heads, value_heads = split_heads(query, keys, values)
    scores = scores_of(query_heads, key_heads, bias, causal)
    row_max = jnp.max(scores, axis=-1, keepdims=True)
    exponent = jnp.exp(scores - row_max)
    total = jnp.sum(exponent, axis=-1, keepdims=True)
    probs = (exponent / total).astype(jnp.bfloat16)
    mixed = jnp.einsum("bgrij,bjgd->bigrd", probs, value_heads, preferred_element_type=jnp.float32)
    return (mixed.reshape(query.shape).astype(jnp.bfloat16), row_max + jnp.log(total))


def attend_backward(query, keys, values, bias, causal, log_total, grad_mixed):
    query_heads, key_heads, value_heads = split_heads(query, keys, values)
    probs = jnp.exp(scores_of(query_heads, key_heads, bias, causal) - log_total)
    grad_heads = grad_mixed.reshape(query_heads.shape)
    grad_probs = jnp.einsum(
        "bigrd,bjgd->bgrij", grad_heads, value_heads, preferred_element_type=jnp.float32
    )
    inner = jnp.sum(probs * grad_probs, axis=-1, keepdims=True)
    grad_scores = (probs * (grad_probs - inner)).astype(jnp.bfloat16)
    scale = DH ** (-0.5)
    grad_query = (
        jnp.einsum("bgrij,bjgd->bigrd", grad_scores, key_heads, preferred_element_type=jnp.float32)
        * scale
    ).astype(jnp.bfloat16)
    grad_keys = (
        jnp.einsum(
            "bgrij,bigrd->bjgd", grad_scores, query_heads, preferred_element_type=jnp.float32
        )
        * scale
    ).astype(jnp.bfloat16)
    grad_values = jnp.einsum(
        "bgrij,bigrd->bjgd",
        probs.astype(jnp.bfloat16),
        grad_heads,
        preferred_element_type=jnp.float32,
    ).astype(jnp.bfloat16)
    return (
        grad_query.reshape(query.shape),
        grad_keys.reshape(keys.shape),
        grad_values.reshape(values.shape),
        grad_scores,
    )


def forward(tokens, memory, weights, onehot, causal):
    gains, table, self_q, self_kv, self_out, cross_q, cross_kv, cross_out, gate_up, down = weights
    gain_rows = gains.astype(jnp.float32)
    start = tokens.astype(jnp.float32)
    normed_self = rms_norm(start, gain_rows[0]).astype(jnp.bfloat16)
    query_self = jnp.dot(normed_self, self_q, preferred_element_type=jnp.float32).astype(
        jnp.bfloat16
    )
    pair_self = jnp.dot(normed_self, flatten(self_kv), preferred_element_type=jnp.float32).astype(
        jnp.bfloat16
    )
    half = pair_self.shape[-1] // 2
    keys_self = pair_self[..., :half]
    values_self = pair_self[..., half:]
    groups = half // DH
    heads = table.shape[1]
    rows = tokens.shape[1]
    bias = jnp.einsum("ijn,nh->hij", onehot, table, preferred_element_type=jnp.float32).reshape(
        groups, heads // groups, rows, rows
    )
    mixed_self, log_self = attend_forward(query_self, keys_self, values_self, bias, causal)
    after_self = start + branch_total(
        jnp.dot(mixed_self, self_out, preferred_element_type=jnp.float32)
    )
    normed_cross = rms_norm(after_self, gain_rows[1]).astype(jnp.bfloat16)
    query_cross = jnp.dot(normed_cross, cross_q, preferred_element_type=jnp.float32).astype(
        jnp.bfloat16
    )
    pair_cross = jnp.dot(memory, flatten(cross_kv), preferred_element_type=jnp.float32).astype(
        jnp.bfloat16
    )
    keys_cross = pair_cross[..., :half]
    values_cross = pair_cross[..., half:]
    mixed_cross, log_cross = attend_forward(query_cross, keys_cross, values_cross, None, None)
    after_cross = after_self + branch_total(
        jnp.dot(mixed_cross, cross_out, preferred_element_type=jnp.float32)
    )
    normed_ffn = rms_norm(after_cross, gain_rows[2]).astype(jnp.bfloat16)
    joined = jnp.dot(normed_ffn, flatten(gate_up), preferred_element_type=jnp.float32)
    hidden_width = joined.shape[-1] // 2
    gate = joined[..., :hidden_width]
    up = joined[..., hidden_width:]
    hidden = gelu_product(gate, up).astype(jnp.bfloat16)
    output = after_cross + branch_total(jnp.dot(hidden, down, preferred_element_type=jnp.float32))
    saved = (
        start,
        after_self,
        after_cross,
        normed_self,
        query_self,
        keys_self,
        values_self,
        bias,
        mixed_self,
        log_self,
        normed_cross,
        query_cross,
        keys_cross,
        values_cross,
        mixed_cross,
        log_cross,
        normed_ffn,
        gate,
        up,
        hidden,
    )
    return (output, saved)


def backward(saved, grad_out, memory, weights, onehot, causal):
    (
        start,
        after_self,
        after_cross,
        normed_self,
        query_self,
        keys_self,
        values_self,
        bias,
        mixed_self,
        log_self,
        normed_cross,
        query_cross,
        keys_cross,
        values_cross,
        mixed_cross,
        log_cross,
        normed_ffn,
        gate,
        up,
        hidden,
    ) = saved
    gains, table, self_q, self_kv, self_out, cross_q, cross_kv, cross_out, gate_up, down = weights
    gain_rows = gains.astype(jnp.float32)
    grad_ffn = grad_out.astype(jnp.float32)
    rounded = grad_ffn.astype(jnp.bfloat16)
    down_grad = jnp.einsum("blf,bld->fd", hidden, rounded, preferred_element_type=jnp.float32)
    grad_hidden = jnp.einsum("bld,fd->blf", rounded, down, preferred_element_type=jnp.float32)
    _, pull = jax.vjp(gelu_product, gate, up)
    grad_gate, grad_up = pull(grad_hidden)
    grad_joined = jnp.concatenate([grad_gate, grad_up], axis=-1).astype(jnp.bfloat16)
    gate_up_grad = jnp.einsum(
        "bld,blf->df", normed_ffn, grad_joined, preferred_element_type=jnp.float32
    ).reshape(gate_up.shape)
    grad_normed = input_total(
        jnp.einsum("blf,df->bld", grad_joined, flatten(gate_up), preferred_element_type=jnp.float32)
    )
    _, pull = jax.vjp(rms_norm, after_cross, gain_rows[2])
    grad_residual, gain_ffn = pull(grad_normed)
    grad_cross = grad_ffn + grad_residual
    rounded = grad_cross.astype(jnp.bfloat16)
    cross_out_grad = jnp.einsum(
        "blh,bld->hd", mixed_cross, rounded, preferred_element_type=jnp.float32
    )
    grad_mixed = jnp.einsum(
        "bld,hd->blh", rounded, cross_out, preferred_element_type=jnp.float32
    ).astype(jnp.bfloat16)
    grad_query, grad_keys, grad_values, _ = attend_backward(
        query_cross, keys_cross, values_cross, None, None, log_cross, grad_mixed
    )
    grad_pair_cross = jnp.concatenate([grad_keys, grad_values], axis=-1)
    cross_q_grad = jnp.einsum(
        "bld,blh->dh", normed_cross, grad_query, preferred_element_type=jnp.float32
    )
    cross_kv_grad = jnp.einsum(
        "bsd,bsw->dw", memory, grad_pair_cross, preferred_element_type=jnp.float32
    ).reshape(cross_kv.shape)
    grad_normed = input_total(
        jnp.einsum("blh,dh->bld", grad_query, cross_q, preferred_element_type=jnp.float32)
    )
    _, pull = jax.vjp(rms_norm, after_self, gain_rows[1])
    grad_residual, gain_cross = pull(grad_normed)
    grad_self = grad_cross + grad_residual
    rounded = grad_self.astype(jnp.bfloat16)
    self_out_grad = jnp.einsum(
        "blh,bld->hd", mixed_self, rounded, preferred_element_type=jnp.float32
    )
    grad_mixed = jnp.einsum(
        "bld,hd->blh", rounded, self_out, preferred_element_type=jnp.float32
    ).astype(jnp.bfloat16)
    grad_query, grad_keys, grad_values, grad_scores = attend_backward(
        query_self, keys_self, values_self, bias, causal, log_self, grad_mixed
    )
    batch = grad_scores.shape[0]
    rows = grad_scores.shape[-1]
    table_grad = jnp.einsum(
        "ijn,bhij->nh",
        onehot,
        grad_scores.reshape(batch, -1, rows, rows),
        preferred_element_type=jnp.float32,
    )
    grad_pair = jnp.concatenate([grad_keys, grad_values], axis=-1)
    self_q_grad = jnp.einsum(
        "bld,blh->dh", normed_self, grad_query, preferred_element_type=jnp.float32
    )
    self_kv_grad = jnp.einsum(
        "bld,blw->dw", normed_self, grad_pair, preferred_element_type=jnp.float32
    ).reshape(self_kv.shape)
    grad_normed = input_total(
        jnp.einsum("blh,dh->bld", grad_query, self_q, preferred_element_type=jnp.float32)
        + jnp.einsum("blw,dw->bld", grad_pair, flatten(self_kv), preferred_element_type=jnp.float32)
    )
    _, pull = jax.vjp(rms_norm, start, gain_rows[0])
    grad_residual, gain_self = pull(grad_normed)
    grad_tokens = grad_self + grad_residual
    gains_grad = jnp.stack([gain_self, gain_cross, gain_ffn])
    grads = (
        gains_grad,
        table_grad,
        self_q_grad,
        self_kv_grad,
        self_out_grad,
        cross_q_grad,
        cross_kv_grad,
        cross_out_grad,
        gate_up_grad,
        down_grad,
    )
    return (grad_tokens, grad_pair_cross, grads)


def per_device(
    decoder_in,
    memory,
    buckets,
    norm_gains,
    rel_bias,
    self_q,
    self_kv,
    self_out,
    cross_q,
    cross_kv,
    cross_out,
    gate_up,
    down,
    cotangent,
):
    local = decoder_in.shape[0]
    rows = decoder_in.shape[1]
    per_batch = local // MICRO
    positions = jnp.arange(rows, dtype=jnp.int32)
    causal = positions[:, None] >= positions[None, :]
    onehot = (buckets[:, :, None] == jnp.arange(NB, dtype=jnp.int32)[None, None, :]).astype(
        jnp.bfloat16
    )
    weights = gather_weights(
        norm_gains, rel_bias, self_q, self_kv, self_out, cross_q, cross_kv, cross_out, gate_up, down
    )
    outputs = []
    token_grads = []
    memory_grads = []
    totals = None
    for index in range(MICRO):
        lower = index * per_batch
        upper = lower + per_batch
        memory_part = memory[lower:upper]
        output, saved = forward(decoder_in[lower:upper], memory_part, weights, onehot, causal)
        grad_tokens, grad_pair_cross, grads = backward(
            saved, cotangent[lower:upper], memory_part, weights, onehot, causal
        )
        memory_term = jnp.einsum(
            "bsw,dw->bsd", grad_pair_cross, flatten(weights[6]), preferred_element_type=jnp.float32
        )
        memory_part_grad = lax.psum_scatter(
            memory_term.astype(jnp.bfloat16), "tp", scatter_dimension=2, tiled=True
        )
        memory_grads.append(memory_part_grad)
        outputs.append(output.astype(jnp.bfloat16))
        token_grads.append(grad_tokens)
        grads = (
            lax.psum_scatter(
                grads[0].astype(jnp.bfloat16), ("seq", "fsdp"), scatter_dimension=1, tiled=True
            ).astype(jnp.float32),
            lax.psum_scatter(
                grads[1].astype(jnp.bfloat16), ("seq", "fsdp"), scatter_dimension=0, tiled=True
            ).astype(jnp.float32),
            lax.psum_scatter(
                grads[2].astype(jnp.bfloat16), ("seq", "fsdp"), scatter_dimension=0, tiled=True
            ).astype(jnp.float32),
            lax.psum_scatter(
                grads[3].astype(jnp.bfloat16), ("seq", "fsdp"), scatter_dimension=0, tiled=True
            ).astype(jnp.float32),
            lax.psum_scatter(
                grads[4].astype(jnp.bfloat16), ("seq", "fsdp"), scatter_dimension=1, tiled=True
            ).astype(jnp.float32),
            lax.psum_scatter(
                grads[5].astype(jnp.bfloat16), ("seq", "fsdp"), scatter_dimension=0, tiled=True
            ).astype(jnp.float32),
            lax.psum_scatter(
                grads[6].astype(jnp.bfloat16), ("seq", "fsdp"), scatter_dimension=0, tiled=True
            ).astype(jnp.float32),
            lax.psum_scatter(
                grads[7].astype(jnp.bfloat16), ("seq", "fsdp"), scatter_dimension=1, tiled=True
            ).astype(jnp.float32),
            lax.psum_scatter(
                grads[8].astype(jnp.bfloat16), ("seq", "fsdp"), scatter_dimension=0, tiled=True
            ).astype(jnp.float32),
            lax.psum_scatter(
                grads[9].astype(jnp.bfloat16), ("seq", "fsdp"), scatter_dimension=1, tiled=True
            ).astype(jnp.float32),
        )
        totals = grads if totals is None else jax.tree.map(jnp.add, totals, grads)
    return (
        jnp.concatenate(outputs, axis=0),
        jnp.concatenate(token_grads, axis=0),
        jnp.concatenate(memory_grads, axis=0),
        totals[0],
        totals[1],
        totals[2],
        totals[3],
        totals[4],
        totals[5],
        totals[6],
        totals[7],
        totals[8],
        totals[9],
    )


GROUP = 128


def lane_blocks(value):
    count = value.shape[1] // GROUP
    return jnp.concatenate(
        [value[:, b * GROUP : (b + 1) * GROUP] for b in range(count)], axis=0
    )


def dot(left, right):
    return jnp.dot(left, right, preferred_element_type=jnp.float32)


def dot_t(left, right):
    return lax.dot_general(left, right, (((1,), (1,)), ((), ())), preferred_element_type=jnp.float32)


def t_dot(left, right):
    return lax.dot_general(left, right, (((0,), (0,)), ((), ())), preferred_element_type=jnp.float32)


def low(value):
    return value.astype(jnp.bfloat16)


def high(value):
    return value.astype(jnp.float32)


def norm_backward(values, gain, cotangent):
    _, pull = jax.vjp(rms_norm, values, gain)
    return pull(cotangent)


def stacked(block, pair, lanes):
    block = high(block[:, pair * GROUP : (pair + 1) * GROUP])
    other = pltpu.roll(block, DH, 1)
    if pair == 0:
        rows = jnp.concatenate([block, other], axis=0)
        keep = lanes < DH
    else:
        rows = jnp.concatenate([other, block], axis=0)
        keep = lanes >= DH
    return low(jnp.where(keep, rows, 0.0))


def unstacked(parts):
    heads = []
    for pair, value in enumerate(parts):
        half = value[:, pair * DH : (pair + 1) * DH]
        heads += [half[0:GROUP], half[GROUP : 2 * GROUP]]
    return jnp.concatenate(heads, axis=1)


def cross_forward_kernel(q_ref, kv_ref, o_ref, lse_ref, scores, probs):
    span = kv_ref.shape[0]
    chunk = 256
    lanes = lax.broadcasted_iota(jnp.int32, (1, GROUP), 1)
    outs = []
    for pair in range(2):
        query = stacked(q_ref[...], pair, lanes)

        def first(index, best):
            rows = pl.ds(index * chunk, chunk)
            part = dot_t(kv_ref[rows, 0:GROUP], query)
            scores[rows, :] = part
            return jnp.maximum(best, jnp.max(part, axis=0, keepdims=True))

        best = lax.fori_loop(
            0, span // chunk, first, jnp.full((1, 2 * GROUP), MASKED, jnp.float32), unroll=2
        )

        def second(index, total):
            rows = pl.ds(index * chunk, chunk)
            part = jnp.exp(scores[rows, :] - best)
            probs[rows, :] = low(part)
            return total + jnp.sum(part, axis=0, keepdims=True)

        total = lax.fori_loop(
            0, span // chunk, second, jnp.zeros((1, 2 * GROUP), jnp.float32), unroll=2
        )
        mixed = t_dot(kv_ref[:, GROUP : 2 * GROUP], probs[...])
        outs.append((mixed / total).T)
        lse_ref[0, pair : pair + 1, :] = best + jnp.log(total)
    o_ref[...] = low(unstacked(outs))


def inner_of(dout, out):
    return jnp.sum((high(dout) * high(out)).T, axis=0, keepdims=True)


def cross_backward_kernel(q_ref, do_ref, o_ref, kv_ref, lse_ref, dq_ref, dkv_ref, probs, grads):
    span = kv_ref.shape[0]
    chunk = 256
    lanes = lax.broadcasted_iota(jnp.int32, (1, GROUP), 1)
    queries = []
    douts = []
    for pair in range(2):
        query = stacked(q_ref[...], pair, lanes)
        dout = stacked(do_ref[...], pair, lanes)
        inner = inner_of(dout, stacked(o_ref[...], pair, lanes))
        lse = lse_ref[0, pair : pair + 1, :]
        columns = slice(pair * 2 * GROUP, (pair + 1) * 2 * GROUP)

        def step(index, carry):
            rows = pl.ds(index * chunk, chunk)
            prob = jnp.exp(dot_t(kv_ref[rows, 0:GROUP], query) - lse)
            grad = prob * (dot_t(kv_ref[rows, GROUP : 2 * GROUP], dout) - inner)
            probs[rows, columns] = low(prob)
            grads[rows, columns] = low(grad)
            return carry

        lax.fori_loop(0, span // chunk, step, 0, unroll=2)
        queries.append(query)
        douts.append(dout)
    query = jnp.concatenate(queries, axis=0)
    dout = jnp.concatenate(douts, axis=0)
    dkv_ref[:, 0:GROUP] = low(dot(grads[...], query))
    dkv_ref[:, GROUP : 2 * GROUP] = low(dot(probs[...], dout))
    dq = (t_dot(kv_ref[:, 0:GROUP], grads[...]) * DH ** (-0.5)).T
    dq_ref[...] = low(unstacked([dq[0 : 2 * GROUP], dq[2 * GROUP :]]))


def self_scores(kv_ref, query, bias_ref, pair):
    rows = kv_ref.shape[0]
    scores = dot_t(kv_ref[:, 0:GROUP], query)
    scores = scores + jnp.concatenate([bias_ref[2 * pair], bias_ref[2 * pair + 1]], axis=1)
    key_at = lax.broadcasted_iota(jnp.int32, scores.shape, 0)
    query_at = lax.broadcasted_iota(jnp.int32, scores.shape, 1) % rows
    return scores, key_at <= query_at


def self_forward_kernel(q_ref, kv_ref, bias_ref, o_ref, lse_ref):
    lanes = lax.broadcasted_iota(jnp.int32, (1, GROUP), 1)
    outs = []
    for pair in range(2):
        query = stacked(q_ref[...], pair, lanes)
        scores, seen = self_scores(kv_ref, query, bias_ref, pair)
        scores = jnp.where(seen, scores, MASKED)
        best = jnp.max(scores, axis=0, keepdims=True)
        part = jnp.exp(scores - best)
        total = jnp.sum(part, axis=0, keepdims=True)
        mixed = t_dot(kv_ref[:, GROUP : 2 * GROUP], low(part / total))
        outs.append(mixed.T)
        lse_ref[0, pair : pair + 1, :] = best + jnp.log(total)
    o_ref[...] = low(unstacked(outs))


def self_backward_kernel(
    q_ref, do_ref, o_ref, kv_ref, lse_ref, bias_ref, dq_ref, dkv_ref, ds_ref
):
    lanes = lax.broadcasted_iota(jnp.int32, (1, GROUP), 1)
    dqs = []
    dk = 0.0
    dv = 0.0
    for pair in range(2):
        query = stacked(q_ref[...], pair, lanes)
        dout = stacked(do_ref[...], pair, lanes)
        inner = inner_of(dout, stacked(o_ref[...], pair, lanes))
        scores, seen = self_scores(kv_ref, query, bias_ref, pair)
        prob = jnp.exp(jnp.where(seen, scores - lse_ref[0, pair : pair + 1, :], MASKED))
        grad = low(prob * (dot_t(kv_ref[:, GROUP : 2 * GROUP], dout) - inner))
        ds_ref[2 * pair] = grad[:, 0:GROUP]
        ds_ref[2 * pair + 1] = grad[:, GROUP : 2 * GROUP]
        dk = dk + dot(grad, query)
        dv = dv + dot(low(prob), dout)
        dqs.append((t_dot(kv_ref[:, 0:GROUP], grad) * DH ** (-0.5)).T)
    dkv_ref[:, 0:GROUP] = low(dk)
    dkv_ref[:, GROUP : 2 * GROUP] = low(dv)
    dq_ref[...] = low(unstacked(dqs))


def attention_specs(rows, span):
    narrow = pl.BlockSpec((rows, 2 * GROUP), lambda k: (0, k))
    tall = pl.BlockSpec((span, 2 * GROUP), lambda k: (0, k))
    lse = pl.BlockSpec((1, 2, 2 * GROUP), lambda k: (k, 0, 0))
    square = pl.BlockSpec((4, rows, rows), lambda k: (k, 0, 0))
    return narrow, tall, lse, square


def kernel_call(kernel, name, blocks, specs, outs, scratch, cost, arguments, limit=32):
    return pl.pallas_call(
        kernel,
        grid=(blocks,),
        in_specs=specs,
        out_specs=[spec for spec, _, _ in outs],
        out_shape=[jax.ShapeDtypeStruct(shape, kind) for _, shape, kind in outs],
        scratch_shapes=scratch,
        compiler_params=pltpu.CompilerParams(vmem_limit_bytes=limit * 2**20),
        cost_estimate=pl.CostEstimate(flops=cost[0], bytes_accessed=cost[1], transcendentals=cost[2]),
        name=name,
    )(*arguments)


def attention_forward(query, pairs, bias):
    rows, span = query.shape[0], pairs.shape[0]
    blocks = query.shape[1] // (2 * GROUP)
    narrow, tall, lse, square = attention_specs(rows, span)
    cost = (
        16 * rows * span * DH * blocks,
        2 * (2 * query.size + pairs.size),
        4 * rows * span * blocks,
    )
    outs = [
        (narrow, query.shape, jnp.bfloat16),
        (lse, (blocks, 2, 2 * GROUP), jnp.float32),
    ]
    if bias is not None:
        return kernel_call(
            self_forward_kernel,
            "self_forward",
            blocks,
            [narrow, tall, square],
            outs,
            [],
            cost,
            (query, pairs, bias),
        )
    return kernel_call(
        cross_forward_kernel,
        "cross_forward",
        blocks,
        [narrow, tall],
        outs,
        [
            pltpu.VMEM((span, 2 * GROUP), jnp.float32),
            pltpu.VMEM((span, 2 * GROUP), jnp.bfloat16),
        ],
        cost,
        (query, pairs),
    )


def attention_backward(query, dout, out, pairs, lse_value, bias):
    rows, span = query.shape[0], pairs.shape[0]
    blocks = query.shape[1] // (2 * GROUP)
    narrow, tall, lse, square = attention_specs(rows, span)
    cost = (
        40 * rows * span * DH * blocks,
        2 * (4 * query.size + 2 * pairs.size),
        4 * rows * span * blocks,
    )
    outs = [(narrow, query.shape, jnp.bfloat16), (tall, pairs.shape, jnp.bfloat16)]
    if bias is not None:
        return kernel_call(
            self_backward_kernel,
            "self_backward",
            blocks,
            [narrow, narrow, narrow, tall, lse, square],
            outs + [(square, (4 * blocks, rows, rows), jnp.bfloat16)],
            [],
            cost,
            (query, dout, out, pairs, lse_value, bias),
        )
    return kernel_call(
        cross_backward_kernel,
        "cross_backward",
        blocks,
        [narrow, narrow, narrow, tall, lse],
        outs,
        [pltpu.VMEM((span, 4 * GROUP), jnp.bfloat16)] * 2,
        cost,
        (query, dout, out, pairs, lse_value),
    )


def with_index(kernel, name, grid, specs, outs, scratch, cost, index, arguments, limit=32):
    return pl.pallas_call(
        kernel,
        grid_spec=pltpu.PrefetchScalarGridSpec(
            num_scalar_prefetch=1,
            grid=grid,
            in_specs=specs,
            out_specs=[spec for spec, _, _ in outs],
            scratch_shapes=scratch,
        ),
        out_shape=[jax.ShapeDtypeStruct(shape, kind) for _, shape, kind in outs],
        compiler_params=pltpu.CompilerParams(vmem_limit_bytes=limit * 2**20),
        cost_estimate=pl.CostEstimate(flops=cost[0], bytes_accessed=cost[1], transcendentals=0),
        name=name,
    )(index, *arguments)


def unpack_heads(index, near, far, depth, top, rows_first, width, extra):
    tp = near[0].shape[0]
    listed = isinstance(far[0], list)
    seq = (far[0][0].shape[0] if listed else far[0].shape[1]) + 1
    shard = width // (2 * seq)
    sides = tuple(far[0]) + tuple(far[1]) if listed else tuple(far)

    def kernel(index_ref, *refs):
        near_refs, far_refs = refs[0:2], refs[2 : 2 + len(sides)]
        outs = refs[2 + len(sides) :]

        def place(q, side, read):
            row = 2 * (index_ref[0] ^ q) + (index_ref[2] ^ side)
            at = pl.ds(pl.multiple_of(row * shard, shard), shard)
            for entry, (out, down) in enumerate(zip(outs, rows_first)):
                start = entry * 2 * shard
                if down:
                    out[:, at] = read(start, 2 * shard)
                else:
                    for b in range(2):
                        out[at, b * GROUP : (b + 1) * GROUP] = read(start + b * shard, shard)
            if extra:
                outs[-1][0, row] = read(depth - extra, extra)

        for side in range(2):
            place(0, side, lambda start, size: near_refs[side][0, top + start : top + start + size, :])
            for q in range(1, seq):
                if listed:
                    for k in range(tp):

                        @pl.when(pl.program_id(0) == k)
                        def _():
                            ref = far_refs[side * tp + k]
                            place(q, side, lambda start, size: ref[q - 1, start : start + size, :])

                else:
                    place(
                        q,
                        side,
                        lambda start, size: far_refs[side][0, q - 1, start : start + size, :],
                    )

    specs = [pl.BlockSpec((1,) + near[0].shape[1:], lambda k, index: (k ^ index[1], 0, 0))] * 2
    for value in sides:
        if listed:
            specs.append(pl.BlockSpec(value.shape, lambda k, index: (0, 0, 0)))
        else:
            specs.append(
                pl.BlockSpec((1,) + value.shape[1:], lambda k, index: (k ^ index[1], 0, 0, 0))
            )
    outs = []
    for down in rows_first:
        if down:
            spec = pl.BlockSpec((2 * GROUP, width), lambda k, index: (k, 0))
            outs.append((spec, (tp * 2 * GROUP, width), jnp.bfloat16))
        else:
            spec = pl.BlockSpec((width, 2 * GROUP), lambda k, index: (0, k))
            outs.append((spec, (width, tp * 2 * GROUP), jnp.bfloat16))
    if extra:
        spec = pl.BlockSpec((1, 2 * seq, extra, GROUP), lambda k, index: (k, 0, 0, 0))
        outs.append((spec, (tp, 2 * seq, extra, GROUP), jnp.bfloat16))
    return with_index(
        kernel,
        "unpack_heads",
        (tp,),
        specs,
        outs,
        [],
        (0, 8 * tp * seq * depth * GROUP),
        index,
        (*near, *sides),
    )


def unpack_hidden(value, width, hidden_width):
    count = value.shape[0]
    shard = width // count
    columns = 2 * hidden_width // GROUP

    def kernel(in_ref, gate_up_ref, down_ref):
        for b in range(columns):
            gate_up_ref[:, b * GROUP : (b + 1) * GROUP] = in_ref[0, b * shard : (b + 1) * shard, :]
        down_ref[...] = in_ref[0, columns * shard :, :]

    return kernel_call(
        kernel,
        "unpack_hidden",
        count,
        [pl.BlockSpec((1, value.shape[1], GROUP), lambda k: (k, 0, 0))],
        [
            (
                pl.BlockSpec((shard, 2 * hidden_width), lambda k: (k, 0)),
                (width, 2 * hidden_width),
                jnp.bfloat16,
            ),
            (
                pl.BlockSpec((hidden_width, shard), lambda k: (0, k)),
                (hidden_width, width),
                jnp.bfloat16,
            ),
        ],
        [],
        (0, 4 * value.size, 0),
        (value,),
    )


def memory_terms(index, seq, memory, pairs, weight, tp):
    rows, width = pairs.shape
    shard = width // (2 * seq)
    features = weight.shape[0] // tp
    steps = 2 * seq
    block = rows // steps
    early = max(steps // 4, 1)

    def row_of(step, index):
        return 2 * (index[0] ^ (step % seq)) + (index[2] ^ (1 - step // seq))

    def kernel(index_ref, memory_ref, pairs_ref, weight_ref, sent_ref, kept_ref, *outs):
        step = pl.program_id(0)
        part = t_dot(memory_ref[0], pairs_ref[...])

        @pl.when(step < seq)
        def _():
            sent_ref[0] = low(part)

        @pl.when(step >= seq)
        def _():
            kept_ref[0] = part

        values = pairs_ref[pl.ds(pl.multiple_of(step * block, block), block), :]
        for k in range(tp):
            at = pl.multiple_of((index_ref[1] ^ k) * features, features)
            outs[tp + k][...] = low(dot_t(values, weight_ref[pl.ds(at, features), :]))

        @pl.when(step < early)
        def _():
            for k in range(tp):
                outs[k][...] = outs[tp + k][...]

    shape = (seq, shard, width)
    first = pl.BlockSpec((block, features), lambda s, index: (jnp.minimum(s, early - 1), 0))
    second = pl.BlockSpec((block, features), lambda s, index: (jnp.maximum(s - early, 0), 0))
    return with_index(
        kernel,
        "memory_terms",
        (steps,),
        [
            pl.BlockSpec((1, rows, shard), lambda s, index: (index[1], 0, row_of(s, index))),
            pl.BlockSpec(pairs.shape, lambda s, index: (0, 0)),
            pl.BlockSpec(weight.shape, lambda s, index: (0, 0)),
        ],
        [
            (
                pl.BlockSpec((1, shard, width), lambda s, index: (jnp.minimum(s, seq - 1), 0, 0)),
                shape,
                jnp.bfloat16,
            ),
            (
                pl.BlockSpec((1, shard, width), lambda s, index: (jnp.maximum(s - seq, 0), 0, 0)),
                shape,
                jnp.float32,
            ),
        ]
        + [(first, (early * block, features), jnp.bfloat16)] * tp
        + [(second, (rows - early * block, features), jnp.bfloat16)] * tp,
        [],
        (4 * rows * width * width, 6 * pairs.size),
        index,
        (memory, pairs, weight),
    )


def hidden_out(index, hidden, weight, values, tp):
    rows = hidden.shape[0] // tp
    width = weight.shape[1]

    def kernel(index_ref, hidden_ref, weight_ref, values_ref, out_ref):
        part = dot(hidden_ref[...], weight_ref[...])

        @pl.when(pl.program_id(0) == 0)
        def _():
            out_ref[0] = low(part + values_ref[...])

        @pl.when(pl.program_id(0) != 0)
        def _():
            out_ref[0] = low(part)

    return with_index(
        kernel,
        "hidden_out",
        (tp,),
        [
            pl.BlockSpec((rows, hidden.shape[1]), lambda k, index: (k, 0)),
            pl.BlockSpec(weight.shape, lambda k, index: (0, 0)),
            pl.BlockSpec(values.shape, lambda k, index: (0, 0)),
        ],
        [
            (
                pl.BlockSpec((1, rows, width), lambda k, index: (k ^ index[1], 0, 0)),
                (tp, rows, width),
                jnp.bfloat16,
            )
        ],
        [],
        (2 * hidden.size * width, 2 * (hidden.size + weight.size + tp * rows * width)),
        index,
        (hidden, weight, values),
    )[0]


def row_terms(index, seq, name, pairs):
    width = pairs[0][0][0].shape[-1] if isinstance(pairs[0][0], list) else pairs[0][0].shape[-1]
    shard = width // (2 * seq)
    columns = sum(right[0][2] - right[0][1] for _, right in pairs)

    def row_of(step, index):
        return 2 * (index[0] ^ (step % seq)) + (index[2] ^ (1 - step // seq))

    def kernel(index_ref, *refs):
        sent_ref, kept_ref = refs[-2:]
        parts = []
        at = 0
        for left, right in pairs:
            if isinstance(left, list):
                value = jnp.concatenate([ref[...] for ref in refs[at : at + len(left)]], axis=0)
                at += len(left)
            else:
                value = refs[at][0]
                at += 1
            other = [ref[:, low_at:high_at] for ref, (_, low_at, high_at) in zip(refs[at:], right)]
            at += len(right)
            parts.append(t_dot(value, jnp.concatenate(other, axis=0)))

        def put(ref, kind):
            at = 0
            for part in parts:
                ref[0, :, at : at + part.shape[1]] = part.astype(kind)
                at += part.shape[1]

        @pl.when(pl.program_id(0) < seq)
        def _():
            put(sent_ref, jnp.bfloat16)

        @pl.when(pl.program_id(0) >= seq)
        def _():
            put(kept_ref, jnp.float32)

    specs = []
    arguments = []
    depth = 0
    for left, right in pairs:
        if isinstance(left, list):
            for part in left:
                rows = part.shape[0]
                specs.append(pl.BlockSpec((rows, shard), lambda s, index: (0, row_of(s, index))))
                arguments.append(part)
        else:
            specs.append(
                pl.BlockSpec(
                    (1, left.shape[1], shard), lambda s, index: (index[1], 0, row_of(s, index))
                )
            )
            arguments.append(left)
        for part, _, _ in right:
            specs.append(pl.BlockSpec(part.shape, lambda s, index: (0, 0)))
            arguments.append(part)
        depth = max(depth, sum(part.shape[0] for part, _, _ in right))
    shape = (seq, shard, columns)
    block = (1, shard, columns)
    return with_index(
        kernel,
        name,
        (2 * seq,),
        specs,
        [
            (
                pl.BlockSpec(block, lambda s, index: (jnp.minimum(s, seq - 1), 0, 0)),
                shape,
                jnp.bfloat16,
            ),
            (
                pl.BlockSpec(block, lambda s, index: (jnp.maximum(s - seq, 0), 0, 0)),
                shape,
                jnp.float32,
            ),
        ],
        [],
        (2 * depth * width * columns, 2 * depth * (width + columns) + 3 * width * columns),
        index,
        tuple(arguments),
        limit=56,
    )


def hidden_terms(normed, grad_joined, rounded, hidden):
    rows, width = normed.shape
    columns = grad_joined.shape[1] + hidden.shape[1]
    split = grad_joined.shape[1]
    steps = width // GROUP

    def kernel(normed_ref, joined_ref, rounded_ref, hidden_ref, out_ref):
        out_ref[:, :split] = low(t_dot(normed_ref[...], joined_ref[...]))
        out_ref[:, split:] = low(t_dot(rounded_ref[...], hidden_ref[...]))

    left = pl.BlockSpec((rows, GROUP), lambda k: (0, k))
    return kernel_call(
        kernel,
        "hidden_terms",
        steps,
        [
            left,
            pl.BlockSpec(grad_joined.shape, lambda k: (0, 0)),
            left,
            pl.BlockSpec(hidden.shape, lambda k: (0, 0)),
        ],
        [(pl.BlockSpec((GROUP, columns), lambda k: (k, 0)), (width, columns), jnp.bfloat16)],
        [],
        (2 * rows * width * columns, 4 * rows * (width + columns) + 2 * width * columns, 0),
        (normed, grad_joined, rounded, hidden),
    )[0]


def one_each(seq, tp):
    everyone = ("seq", "tp", "fsdp")

    def after(value, *earlier):
        return lax.optimization_barrier((value, earlier))[0]

    def together(*values):
        return lax.optimization_barrier(values)

    def swap(value, axis, flip):
        size = {"seq": seq, "tp": tp, "fsdp": 2}[axis]
        return lax.ppermute(value, axis, [(place, place ^ flip) for place in range(size)])

    def gather(value, axis, size):
        return [value] + [swap(value, axis, flip) for flip in range(1, size)]

    def exchange(parts, axis):
        return [parts[0]] + [swap(parts[k], axis, k) for k in range(1, len(parts))]

    def exchange_all(value):
        return lax.all_to_all(value, "tp", 0, 0, tiled=True)

    def to_everyone(value):
        return exchange_all(jnp.broadcast_to(value[None], (tp,) + value.shape))

    def total(parts):
        result = high(parts[0])
        for part in parts[1:]:
            result = result + high(part)
        return result

    def run(
        decoder_in,
        memory,
        buckets,
        norm_gains,
        rel_bias,
        self_q,
        self_kv,
        self_out,
        cross_q,
        cross_kv,
        cross_out,
        gate_up,
        down,
        cotangent,
    ):
        count, rows, width = decoder_in.shape
        z = lax.axis_index("seq")
        t = lax.axis_index("tp")
        c = lax.axis_index("fsdp")
        index = jnp.stack([z, t, c]).astype(jnp.int32)
        cores = 2
        shard = self_q.shape[0]
        tables = rel_bias.shape[0]
        heads = rel_bias.shape[1]
        hidden_width = down.shape[0]
        extra = 16

        def own(value):
            return lax.dynamic_index_in_dim(value, t, 0, keepdims=False)

        def from_here(value):
            return [
                lax.dynamic_index_in_dim(value, t ^ k, 0, keepdims=False) for k in range(tp)
            ]

        def in_order(parts, kind):
            result = jnp.zeros((count,) + parts[0].shape, kind)
            for k, part in enumerate(parts):
                result = lax.dynamic_update_index_in_dim(result, part.astype(kind), t ^ k, 0)
            return result

        def head_blocks(value):
            size = value.shape[1] // tp
            return [value[:, k * size : (k + 1) * size] for k in range(tp)]

        small = jnp.concatenate(
            [
                norm_gains,
                jnp.pad(rel_bias.reshape(1, -1), ((0, 0), (0, GROUP - rel_bias.size))),
                jnp.zeros((extra - 4, GROUP), jnp.bfloat16),
            ],
            axis=0,
        )
        pack_a = jnp.concatenate(
            [lane_blocks(flatten(cross_kv)), lane_blocks(self_q), lane_blocks(flatten(self_kv)), small],
            axis=0,
        )
        pack_b = jnp.concatenate([self_out, lane_blocks(cross_q), cross_out], axis=0)
        pack_f = jnp.concatenate([lane_blocks(flatten(gate_up)), down], axis=0)

        depth_a, depth_b = pack_a.shape[0], pack_b.shape[0]
        near = to_everyone(jnp.concatenate([pack_a, pack_b], axis=0))
        ring_a = gather(pack_a, "seq", seq)
        ring_b = gather(after(pack_b, *ring_a), "seq", seq)
        far_a = to_everyone(after(jnp.stack(ring_a[1:]), near))
        far_b = after(jnp.stack(ring_b[1:]), far_a)
        buckets, decoder_in, cotangent = after((buckets, decoder_in, cotangent), far_b)
        far_b = gather(far_b, "tp", tp)
        full_f = lax.all_gather(after(pack_f, *ring_b), ("seq", "fsdp"), axis=0, tiled=True)
        near = [near, swap(near, "fsdp", 1)]
        far_a = [far_a, swap(far_a, "fsdp", 1)]

        cross_pairs, weight_self_q, weight_self_kv, smalls = unpack_heads(
            index, near, far_a, depth_a, 0, (False, False, False), width, extra
        )
        weight_gate_up, weight_down = unpack_hidden(
            full_f.reshape(seq * cores, -1, GROUP), width, hidden_width
        )
        gain_rows = high(smalls[0, :, 0:3].transpose(1, 0, 2).reshape(3, width))
        table = smalls[:, :, 3, 0 : tables * heads].reshape(tp, seq * cores, tables, heads)
        table = table.transpose(1, 2, 0, 3).reshape(NB, tp * heads)
        onehot = (
            buckets.T[:, :, None] == jnp.arange(NB, dtype=jnp.int32)[None, None, :]
        ).astype(jnp.bfloat16)
        bias = jnp.einsum("jin,nh->hji", onehot, table, preferred_element_type=jnp.float32)

        pairs = low(dot(own(memory), cross_pairs))
        start = high(own(decoder_in))
        scale = DH ** (-0.5)

        normed_self = low(rms_norm(start, gain_rows[0]))
        query_self = low(dot(normed_self, weight_self_q) * scale)
        pair_self = low(dot(normed_self, weight_self_kv))
        mixed_self, log_self = attention_forward(query_self, pair_self, bias)
        far_b = [after(part, mixed_self, pairs) for part in far_b]
        far_b = [far_b, [swap(part, "fsdp", 1) for part in far_b]]
        weight_self_out, weight_cross_q, weight_cross_out = unpack_heads(
            index, near, far_b, depth_b, depth_a, (True, False, True), width, 0
        )
        after_self = start + dot(mixed_self, weight_self_out)

        normed_cross = low(rms_norm(after_self, gain_rows[1]))
        query_cross = low(dot(normed_cross, weight_cross_q) * scale)
        mixed_cross, log_cross = attention_forward(query_cross, pairs, None)
        after_cross = after_self + dot(mixed_cross, weight_cross_out)
        normed_ffn = low(rms_norm(after_cross, gain_rows[2]))

        all_cross = lax.all_gather(normed_cross, "tp", axis=0, tiled=True)
        all_normed = jnp.concatenate(gather(normed_ffn, "tp", tp), axis=0)
        rounded = jnp.concatenate(from_here(cotangent), axis=0)
        joined = dot(all_normed, weight_gate_up)
        gate = joined[:, :hidden_width]
        up = joined[:, hidden_width:]
        grad_hidden = dot_t(rounded, weight_down)
        hidden = low(gelu_product(gate, up))
        _, pull = jax.vjp(gelu_product, gate, up)
        grad_gate, grad_up = pull(grad_hidden)
        grad_joined = low(jnp.concatenate([grad_gate, grad_up], axis=-1))

        def row_parts(value):
            return [value[k * rows : (k + 1) * rows] for k in range(tp)]

        partial_normed = row_parts(low(dot_t(grad_joined, weight_gate_up)))
        grad_parts = exchange(partial_normed, "tp")
        all_normed, grad_joined, rounded, hidden, o_self, o_cross = after(
            (all_normed, grad_joined, rounded, hidden, mixed_self, mixed_cross), partial_normed
        )
        hidden_grads = hidden_terms(all_normed, grad_joined, rounded, hidden)
        partial_out = hidden_out(index, hidden, weight_down, after_cross, tp)
        o_blocks = [
            jnp.concatenate(blocks, axis=1)
            for blocks in zip(head_blocks(o_self), head_blocks(o_cross))
        ]
        grad_parts, hidden_grads, partial_out, o_blocks = together(
            grad_parts, hidden_grads, partial_out, o_blocks
        )
        hidden_grads = high(
            lax.psum_scatter(hidden_grads, ("seq", "fsdp"), scatter_dimension=0, tiled=True)
        )

        grad_normed = total(grad_parts)
        grad_residual, gain_ffn = norm_backward(after_cross, gain_rows[2], grad_normed)
        grad_cross = high(own(cotangent)) + grad_residual
        rounded_cross = low(grad_cross)
        cross_operands = [jnp.concatenate([rounded_cross, block], axis=1) for block in o_blocks]
        cross_parts = exchange(cross_operands, "tp")
        grad_mixed = low(dot_t(after(rounded_cross, cross_operands), weight_cross_out))
        grad_query, grad_pairs = attention_backward(
            query_cross, grad_mixed, mixed_cross, pairs, log_cross, None
        )
        cross_parts, grad_query, grad_pairs = together(cross_parts, grad_query, grad_pairs)
        grad_normed = dot_t(grad_query, weight_cross_q)
        grad_residual, gain_cross = norm_backward(after_self, gain_rows[1], grad_normed)
        grad_self = grad_cross + grad_residual
        rounded_self = low(grad_self)
        self_operands = [
            jnp.concatenate([rounded_self, block], axis=1) for block in head_blocks(grad_query)
        ]
        self_parts = exchange(self_operands, "tp")

        grad_mixed_self = low(dot_t(after(rounded_self, self_operands), weight_self_out))
        grad_query_self, grad_pair_self, grad_scores = attention_backward(
            query_self, grad_mixed_self, mixed_self, pair_self, log_self, bias
        )
        grad_normed = dot_t(grad_query_self, weight_self_q) + dot_t(grad_pair_self, weight_self_kv)
        grad_residual, gain_self = norm_backward(start, gain_rows[0], grad_normed)
        grad_tokens = low(grad_self + grad_residual)
        last_operands = [
            jnp.concatenate([grad_tokens, q_block, kv_block], axis=1)
            for q_block, kv_block in zip(head_blocks(grad_query_self), head_blocks(grad_pair_self))
        ]
        self_parts, last_operands, memory_pairs, decoder_in, gains, grad_scores = together(
            self_parts,
            last_operands,
            grad_pairs,
            decoder_in,
            (gain_self, gain_cross, gain_ffn),
            grad_scores,
        )
        last_parts = exchange(last_operands, "tp")

        kv_sent, kv_rows, *memory_parts = memory_terms(
            index, seq, memory, memory_pairs, cross_pairs, tp
        )
        last_parts, kv_sent, kv_rows, memory_parts, gains, grad_scores, partial_out = together(
            last_parts, kv_sent, kv_rows, memory_parts, gains, grad_scores, partial_out
        )
        decoder_out = lax.psum(partial_out, "tp")
        first_parts = exchange(memory_parts[:tp], "tp")
        kv_rows = kv_rows + high(swap(kv_sent, "fsdp", 1))

        def span_of(parts, first, last):
            return [(part, first, last) for part in parts]

        all_start = [
            low(rms_norm(high(part), gain_rows[0])) for part in from_here(decoder_in)
        ]
        both_sent, both_kept = row_terms(
            index,
            seq,
            "head_weights",
            [
                (
                    from_here(all_cross.reshape(tp, rows, width)),
                    span_of(self_parts, width, width + 2 * GROUP),
                ),
                (cross_parts, span_of(cross_parts, width + 2 * GROUP, width + 4 * GROUP)),
                (all_start, span_of(last_parts, width, width + 4 * GROUP)),
                (self_parts, span_of(cross_parts, width, width + 2 * GROUP)),
            ],
        )
        kv_far = low(kv_rows[seq // 2 :])
        first_parts, kv_far, kv_rows, both_sent, both_kept, second_parts = together(
            first_parts, kv_far, kv_rows, both_sent, both_kept, memory_parts[tp:]
        )
        kv_far = swap(kv_far, "seq", seq // 2)
        second_parts = exchange(second_parts, "tp")
        both_grads = low(both_kept + high(swap(both_sent, "fsdp", 1)))
        both_grads = jnp.concatenate(
            [
                lax.dynamic_index_in_dim(both_grads, z ^ k, 0, keepdims=True) for k in range(seq)
            ],
            axis=0,
        )
        gains, grad_scores, last_parts, kv_far, second_parts, hidden_grads = after(
            (gains, grad_scores, last_parts, kv_far, second_parts, hidden_grads), both_grads
        )
        gate_up_grad = hidden_grads[:, : 2 * hidden_width].reshape(gate_up.shape)
        down_grad = hidden_grads[:, 2 * hidden_width :].T
        both_grads = lax.all_to_all(both_grads, "seq", 0, 0, tiled=True)
        kv_rows = kv_rows[: seq // 2] + high(kv_far)
        step = seq // 4
        while step:
            kv_rows = kv_rows[:step] + high(swap(low(kv_rows[step:]), "seq", step))
            step //= 2
        kv_rows = kv_rows[0]
        memory_grad = jnp.zeros((count, memory.shape[1], first_parts[0].shape[1]), jnp.bfloat16)
        cut = first_parts[0].shape[0]
        for at, parts in ((0, first_parts), (cut, second_parts)):
            for k in range(tp):
                memory_grad = lax.dynamic_update_slice(
                    memory_grad, parts[k][None], (t ^ k, at, 0)
                )
        decoder_grad = in_order([part[:, :width] for part in last_parts], jnp.float32)

        table_grad = jnp.einsum(
            "jin,hji->nh", onehot, grad_scores, preferred_element_type=jnp.float32
        )
        gain_parts = jnp.stack([gain.reshape(-1, GROUP) for gain in gains], axis=1)
        table_parts = jnp.pad(
            table_grad.reshape(seq * cores, 1, -1),
            ((0, 0), (0, 0), (0, GROUP - tables * tp * heads)),
        )
        little = low(jnp.concatenate([gain_parts, table_parts], axis=1))
        little = jnp.broadcast_to(
            little.reshape(seq, 1, cores, 4, GROUP), (seq, tp, cores, 4, GROUP)
        )
        both_grads, little, gate_up_grad, down_grad, decoder_grad, kv_rows, memory_grad = together(
            both_grads, little, gate_up_grad, down_grad, decoder_grad, kv_rows, memory_grad
        )
        cross_kv_grad = total(
            exchange([kv_rows[:, : 2 * GROUP]] + head_blocks(low(kv_rows))[1:], "tp")
        )
        little = lax.all_to_all(little.reshape(-1, 4, GROUP), everyone, 0, 0, tiled=True)
        little = jnp.sum(high(little).reshape(seq, tp, cores, 4, GROUP), axis=(0, 2))
        sender = jnp.arange(tp, dtype=jnp.int32)
        chosen = (sender[:, None] ^ sender[None, :]) == t
        table_sum = little[:, 3, : tables * tp * heads].reshape(tp, tables, tp, heads)
        table_sum = jnp.sum(jnp.where(chosen[:, None, :, None], table_sum, 0.0), axis=(0, 2))
        little = jnp.sum(little, axis=0)
        both_grads = jnp.sum(high(both_grads), axis=0)
        cross_grads = both_grads[:, : 4 * GROUP]
        self_grads = both_grads[:, 4 * GROUP :]

        return (
            decoder_out,
            decoder_grad,
            memory_grad,
            little[0:3],
            table_sum,
            self_grads[:, 0 : 2 * GROUP],
            self_grads[:, 2 * GROUP : 4 * GROUP].reshape(self_kv.shape),
            self_grads[:, 4 * GROUP :].T,
            cross_grads[:, 0 : 2 * GROUP],
            cross_kv_grad.reshape(cross_kv.shape),
            cross_grads[:, 2 * GROUP :].T,
            gate_up_grad,
            down_grad,
        )

    return run


def plan_of(mesh):
    seq, tp, cores = (mesh.shape[axis] for axis in ("seq", "tp", "fsdp"))

    def chosen(*arrays):
        count, rows, width = arrays[0].shape
        fits = (
            cores == 2
            and seq & (seq - 1) == 0
            and tp & (tp - 1) == 0
            and count == tp
            and rows == GROUP
            and width == 2 * seq * GROUP
            and arrays[5].shape[1] == 4 * DH
            and arrays[6].shape[2] == 2 * DH
            and tp * arrays[4].size <= GROUP
            and 2 * arrays[12].shape[0] % GROUP == 0
        )
        return (one_each(seq, tp) if fits else per_device)(*arrays)

    return chosen


def solution(mesh):
    return jax.shard_map(
        plan_of(mesh),
        mesh=mesh,
        in_specs=(
            P(("seq", "fsdp"), None, None),
            P(("seq", "fsdp"), None, None),
            P(),
            P(None, ("seq", "fsdp")),
            P(("seq", "fsdp"), "tp"),
            P(("seq", "fsdp"), "tp"),
            P(("seq", "fsdp"), None, "tp"),
            P("tp", ("seq", "fsdp")),
            P(("seq", "fsdp"), "tp"),
            P(("seq", "fsdp"), None, "tp"),
            P("tp", ("seq", "fsdp")),
            P(("seq", "fsdp"), None, "tp"),
            P("tp", ("seq", "fsdp")),
            P(("seq", "fsdp"), None, None),
        ),
        out_specs=(
            P(("seq", "fsdp"), None, None),
            P(("seq", "fsdp"), None, None),
            P(("seq", "fsdp"), None, "tp"),
            P(None, ("seq", "fsdp")),
            P(("seq", "fsdp"), "tp"),
            P(("seq", "fsdp"), "tp"),
            P(("seq", "fsdp"), None, "tp"),
            P("tp", ("seq", "fsdp")),
            P(("seq", "fsdp"), "tp"),
            P(("seq", "fsdp"), None, "tp"),
            P("tp", ("seq", "fsdp")),
            P(("seq", "fsdp"), None, "tp"),
            P("tp", ("seq", "fsdp")),
        ),
        check_vma=False,
    )
```

```python
import jax
import jax.numpy as jnp
from jax import lax
from jax.experimental import pallas as pl
from jax.experimental.pallas import tpu as pltpu
from jax.sharding import PartitionSpec as P

DH = 64
NB = 32
MICRO = 2


EPSILON = 1e-06
MASKED = -1e30


def rms_norm(values, gain):
    return values * lax.rsqrt(jnp.mean(values * values, axis=-1, keepdims=True) + EPSILON) * gain


def gelu_product(gate, up):
    return jax.nn.gelu(gate, approximate=True) * up


def flatten(weight):
    return weight.reshape(weight.shape[0], -1)


def gather_weights(
    gains, table, self_q, self_kv, self_out, cross_q, cross_kv, cross_out, gate_up, down
):
    return (
        lax.all_gather(gains, ("seq", "fsdp"), axis=1, tiled=True),
        lax.all_gather(table, ("seq", "fsdp"), axis=0, tiled=True),
        lax.all_gather(self_q, ("seq", "fsdp"), axis=0, tiled=True),
        lax.all_gather(self_kv, ("seq", "fsdp"), axis=0, tiled=True),
        lax.all_gather(self_out, ("seq", "fsdp"), axis=1, tiled=True),
        lax.all_gather(cross_q, ("seq", "fsdp"), axis=0, tiled=True),
        lax.all_gather(cross_kv, ("seq", "fsdp"), axis=0, tiled=True),
        lax.all_gather(cross_out, ("seq", "fsdp"), axis=1, tiled=True),
        lax.all_gather(gate_up, ("seq", "fsdp"), axis=0, tiled=True),
        lax.all_gather(down, ("seq", "fsdp"), axis=1, tiled=True),
    )


def branch_total(partial_value):
    return lax.psum(partial_value.astype(jnp.bfloat16), "tp").astype(jnp.float32)


def input_total(partial_value):
    return lax.psum(partial_value.astype(jnp.bfloat16), "tp").astype(jnp.float32)


def split_heads(query, keys, values):
    batch, rows, width = query.shape
    span = keys.shape[1]
    groups = keys.shape[2] // DH
    ratio = width // DH // groups
    return (
        query.reshape(batch, rows, groups, ratio, DH),
        keys.reshape(batch, span, groups, DH),
        values.reshape(batch, span, groups, DH),
    )


def scores_of(query_heads, key_heads, bias, causal):
    scores = jnp.einsum(
        "bigrd,bjgd->bgrij", query_heads, key_heads, preferred_element_type=jnp.float32
    ) * DH ** (-0.5)
    if bias is not None:
        scores = scores + bias
    if causal is not None:
        scores = jnp.where(causal, scores, MASKED)
    return scores


def attend_forward(query, keys, values, bias, causal):
    query_heads, key_heads, value_heads = split_heads(query, keys, values)
    scores = scores_of(query_heads, key_heads, bias, causal)
    row_max = jnp.max(scores, axis=-1, keepdims=True)
    exponent = jnp.exp(scores - row_max)
    total = jnp.sum(exponent, axis=-1, keepdims=True)
    probs = (exponent / total).astype(jnp.bfloat16)
    mixed = jnp.einsum("bgrij,bjgd->bigrd", probs, value_heads, preferred_element_type=jnp.float32)
    return (mixed.reshape(query.shape).astype(jnp.bfloat16), row_max + jnp.log(total))


def attend_backward(query, keys, values, bias, causal, log_total, grad_mixed):
    query_heads, key_heads, value_heads = split_heads(query, keys, values)
    probs = jnp.exp(scores_of(query_heads, key_heads, bias, causal) - log_total)
    grad_heads = grad_mixed.reshape(query_heads.shape)
    grad_probs = jnp.einsum(
        "bigrd,bjgd->bgrij", grad_heads, value_heads, preferred_element_type=jnp.float32
    )
    inner = jnp.sum(probs * grad_probs, axis=-1, keepdims=True)
    grad_scores = (probs * (grad_probs - inner)).astype(jnp.bfloat16)
    scale = DH ** (-0.5)
    grad_query = (
        jnp.einsum("bgrij,bjgd->bigrd", grad_scores, key_heads, preferred_element_type=jnp.float32)
        * scale
    ).astype(jnp.bfloat16)
    grad_keys = (
        jnp.einsum(
            "bgrij,bigrd->bjgd", grad_scores, query_heads, preferred_element_type=jnp.float32
        )
        * scale
    ).astype(jnp.bfloat16)
    grad_values = jnp.einsum(
        "bgrij,bigrd->bjgd",
        probs.astype(jnp.bfloat16),
        grad_heads,
        preferred_element_type=jnp.float32,
    ).astype(jnp.bfloat16)
    return (
        grad_query.reshape(query.shape),
        grad_keys.reshape(keys.shape),
        grad_values.reshape(values.shape),
        grad_scores,
    )


def forward(tokens, memory, weights, onehot, causal):
    gains, table, self_q, self_kv, self_out, cross_q, cross_kv, cross_out, gate_up, down = weights
    gain_rows = gains.astype(jnp.float32)
    start = tokens.astype(jnp.float32)
    normed_self = rms_norm(start, gain_rows[0]).astype(jnp.bfloat16)
    query_self = jnp.dot(normed_self, self_q, preferred_element_type=jnp.float32).astype(
        jnp.bfloat16
    )
    pair_self = jnp.dot(normed_self, flatten(self_kv), preferred_element_type=jnp.float32).astype(
        jnp.bfloat16
    )
    half = pair_self.shape[-1] // 2
    keys_self = pair_self[..., :half]
    values_self = pair_self[..., half:]
    groups = half // DH
    heads = table.shape[1]
    rows = tokens.shape[1]
    bias = jnp.einsum("ijn,nh->hij", onehot, table, preferred_element_type=jnp.float32).reshape(
        groups, heads // groups, rows, rows
    )
    mixed_self, log_self = attend_forward(query_self, keys_self, values_self, bias, causal)
    after_self = start + branch_total(
        jnp.dot(mixed_self, self_out, preferred_element_type=jnp.float32)
    )
    normed_cross = rms_norm(after_self, gain_rows[1]).astype(jnp.bfloat16)
    query_cross = jnp.dot(normed_cross, cross_q, preferred_element_type=jnp.float32).astype(
        jnp.bfloat16
    )
    pair_cross = jnp.dot(memory, flatten(cross_kv), preferred_element_type=jnp.float32).astype(
        jnp.bfloat16
    )
    keys_cross = pair_cross[..., :half]
    values_cross = pair_cross[..., half:]
    mixed_cross, log_cross = attend_forward(query_cross, keys_cross, values_cross, None, None)
    after_cross = after_self + branch_total(
        jnp.dot(mixed_cross, cross_out, preferred_element_type=jnp.float32)
    )
    normed_ffn = rms_norm(after_cross, gain_rows[2]).astype(jnp.bfloat16)
    joined = jnp.dot(normed_ffn, flatten(gate_up), preferred_element_type=jnp.float32)
    hidden_width = joined.shape[-1] // 2
    gate = joined[..., :hidden_width]
    up = joined[..., hidden_width:]
    hidden = gelu_product(gate, up).astype(jnp.bfloat16)
    output = after_cross + branch_total(jnp.dot(hidden, down, preferred_element_type=jnp.float32))
    saved = (
        start,
        after_self,
        after_cross,
        normed_self,
        query_self,
        keys_self,
        values_self,
        bias,
        mixed_self,
        log_self,
        normed_cross,
        query_cross,
        keys_cross,
        values_cross,
        mixed_cross,
        log_cross,
        normed_ffn,
        gate,
        up,
        hidden,
    )
    return (output, saved)


def backward(saved, grad_out, memory, weights, onehot, causal):
    (
        start,
        after_self,
        after_cross,
        normed_self,
        query_self,
        keys_self,
        values_self,
        bias,
        mixed_self,
        log_self,
        normed_cross,
        query_cross,
        keys_cross,
        values_cross,
        mixed_cross,
        log_cross,
        normed_ffn,
        gate,
        up,
        hidden,
    ) = saved
    gains, table, self_q, self_kv, self_out, cross_q, cross_kv, cross_out, gate_up, down = weights
    gain_rows = gains.astype(jnp.float32)
    grad_ffn = grad_out.astype(jnp.float32)
    rounded = grad_ffn.astype(jnp.bfloat16)
    down_grad = jnp.einsum("blf,bld->fd", hidden, rounded, preferred_element_type=jnp.float32)
    grad_hidden = jnp.einsum("bld,fd->blf", rounded, down, preferred_element_type=jnp.float32)
    _, pull = jax.vjp(gelu_product, gate, up)
    grad_gate, grad_up = pull(grad_hidden)
    grad_joined = jnp.concatenate([grad_gate, grad_up], axis=-1).astype(jnp.bfloat16)
    gate_up_grad = jnp.einsum(
        "bld,blf->df", normed_ffn, grad_joined, preferred_element_type=jnp.float32
    ).reshape(gate_up.shape)
    grad_normed = input_total(
        jnp.einsum("blf,df->bld", grad_joined, flatten(gate_up), preferred_element_type=jnp.float32)
    )
    _, pull = jax.vjp(rms_norm, after_cross, gain_rows[2])
    grad_residual, gain_ffn = pull(grad_normed)
    grad_cross = grad_ffn + grad_residual
    rounded = grad_cross.astype(jnp.bfloat16)
    cross_out_grad = jnp.einsum(
        "blh,bld->hd", mixed_cross, rounded, preferred_element_type=jnp.float32
    )
    grad_mixed = jnp.einsum(
        "bld,hd->blh", rounded, cross_out, preferred_element_type=jnp.float32
    ).astype(jnp.bfloat16)
    grad_query, grad_keys, grad_values, _ = attend_backward(
        query_cross, keys_cross, values_cross, None, None, log_cross, grad_mixed
    )
    grad_pair_cross = jnp.concatenate([grad_keys, grad_values], axis=-1)
    cross_q_grad = jnp.einsum(
        "bld,blh->dh", normed_cross, grad_query, preferred_element_type=jnp.float32
    )
    cross_kv_grad = jnp.einsum(
        "bsd,bsw->dw", memory, grad_pair_cross, preferred_element_type=jnp.float32
    ).reshape(cross_kv.shape)
    grad_normed = input_total(
        jnp.einsum("blh,dh->bld", grad_query, cross_q, preferred_element_type=jnp.float32)
    )
    _, pull = jax.vjp(rms_norm, after_self, gain_rows[1])
    grad_residual, gain_cross = pull(grad_normed)
    grad_self = grad_cross + grad_residual
    rounded = grad_self.astype(jnp.bfloat16)
    self_out_grad = jnp.einsum(
        "blh,bld->hd", mixed_self, rounded, preferred_element_type=jnp.float32
    )
    grad_mixed = jnp.einsum(
        "bld,hd->blh", rounded, self_out, preferred_element_type=jnp.float32
    ).astype(jnp.bfloat16)
    grad_query, grad_keys, grad_values, grad_scores = attend_backward(
        query_self, keys_self, values_self, bias, causal, log_self, grad_mixed
    )
    batch = grad_scores.shape[0]
    rows = grad_scores.shape[-1]
    table_grad = jnp.einsum(
        "ijn,bhij->nh",
        onehot,
        grad_scores.reshape(batch, -1, rows, rows),
        preferred_element_type=jnp.float32,
    )
    grad_pair = jnp.concatenate([grad_keys, grad_values], axis=-1)
    self_q_grad = jnp.einsum(
        "bld,blh->dh", normed_self, grad_query, preferred_element_type=jnp.float32
    )
    self_kv_grad = jnp.einsum(
        "bld,blw->dw", normed_self, grad_pair, preferred_element_type=jnp.float32
    ).reshape(self_kv.shape)
    grad_normed = input_total(
        jnp.einsum("blh,dh->bld", grad_query, self_q, preferred_element_type=jnp.float32)
        + jnp.einsum("blw,dw->bld", grad_pair, flatten(self_kv), preferred_element_type=jnp.float32)
    )
    _, pull = jax.vjp(rms_norm, start, gain_rows[0])
    grad_residual, gain_self = pull(grad_normed)
    grad_tokens = grad_self + grad_residual
    gains_grad = jnp.stack([gain_self, gain_cross, gain_ffn])
    grads = (
        gains_grad,
        table_grad,
        self_q_grad,
        self_kv_grad,
        self_out_grad,
        cross_q_grad,
        cross_kv_grad,
        cross_out_grad,
        gate_up_grad,
        down_grad,
    )
    return (grad_tokens, grad_pair_cross, grads)


def per_device(
    decoder_in,
    memory,
    buckets,
    norm_gains,
    rel_bias,
    self_q,
    self_kv,
    self_out,
    cross_q,
    cross_kv,
    cross_out,
    gate_up,
    down,
    cotangent,
):
    local = decoder_in.shape[0]
    rows = decoder_in.shape[1]
    per_batch = local // MICRO
    positions = jnp.arange(rows, dtype=jnp.int32)
    causal = positions[:, None] >= positions[None, :]
    onehot = (buckets[:, :, None] == jnp.arange(NB, dtype=jnp.int32)[None, None, :]).astype(
        jnp.bfloat16
    )
    weights = gather_weights(
        norm_gains, rel_bias, self_q, self_kv, self_out, cross_q, cross_kv, cross_out, gate_up, down
    )
    outputs = []
    token_grads = []
    memory_grads = []
    totals = None
    for index in range(MICRO):
        lower = index * per_batch
        upper = lower + per_batch
        memory_part = memory[lower:upper]
        output, saved = forward(decoder_in[lower:upper], memory_part, weights, onehot, causal)
        grad_tokens, grad_pair_cross, grads = backward(
            saved, cotangent[lower:upper], memory_part, weights, onehot, causal
        )
        memory_term = jnp.einsum(
            "bsw,dw->bsd", grad_pair_cross, flatten(weights[6]), preferred_element_type=jnp.float32
        )
        memory_part_grad = lax.psum_scatter(
            memory_term.astype(jnp.bfloat16), "tp", scatter_dimension=2, tiled=True
        )
        memory_grads.append(memory_part_grad)
        outputs.append(output.astype(jnp.bfloat16))
        token_grads.append(grad_tokens)
        grads = (
            lax.psum_scatter(
                grads[0].astype(jnp.bfloat16), ("seq", "fsdp"), scatter_dimension=1, tiled=True
            ).astype(jnp.float32),
            lax.psum_scatter(
                grads[1].astype(jnp.bfloat16), ("seq", "fsdp"), scatter_dimension=0, tiled=True
            ).astype(jnp.float32),
            lax.psum_scatter(
                grads[2].astype(jnp.bfloat16), ("seq", "fsdp"), scatter_dimension=0, tiled=True
            ).astype(jnp.float32),
            lax.psum_scatter(
                grads[3].astype(jnp.bfloat16), ("seq", "fsdp"), scatter_dimension=0, tiled=True
            ).astype(jnp.float32),
            lax.psum_scatter(
                grads[4].astype(jnp.bfloat16), ("seq", "fsdp"), scatter_dimension=1, tiled=True
            ).astype(jnp.float32),
            lax.psum_scatter(
                grads[5].astype(jnp.bfloat16), ("seq", "fsdp"), scatter_dimension=0, tiled=True
            ).astype(jnp.float32),
            lax.psum_scatter(
                grads[6].astype(jnp.bfloat16), ("seq", "fsdp"), scatter_dimension=0, tiled=True
            ).astype(jnp.float32),
            lax.psum_scatter(
                grads[7].astype(jnp.bfloat16), ("seq", "fsdp"), scatter_dimension=1, tiled=True
            ).astype(jnp.float32),
            lax.psum_scatter(
                grads[8].astype(jnp.bfloat16), ("seq", "fsdp"), scatter_dimension=0, tiled=True
            ).astype(jnp.float32),
            lax.psum_scatter(
                grads[9].astype(jnp.bfloat16), ("seq", "fsdp"), scatter_dimension=1, tiled=True
            ).astype(jnp.float32),
        )
        totals = grads if totals is None else jax.tree.map(jnp.add, totals, grads)
    return (
        jnp.concatenate(outputs, axis=0),
        jnp.concatenate(token_grads, axis=0),
        jnp.concatenate(memory_grads, axis=0),
        totals[0],
        totals[1],
        totals[2],
        totals[3],
        totals[4],
        totals[5],
        totals[6],
        totals[7],
        totals[8],
        totals[9],
    )


GROUP = 128


def lane_blocks(value):
    count = value.shape[1] // GROUP
    return jnp.concatenate(
        [value[:, b * GROUP : (b + 1) * GROUP] for b in range(count)], axis=0
    )


def dot(left, right):
    return jnp.dot(left, right, preferred_element_type=jnp.float32)


def dot_t(left, right):
    return lax.dot_general(left, right, (((1,), (1,)), ((), ())), preferred_element_type=jnp.float32)


def t_dot(left, right):
    return lax.dot_general(left, right, (((0,), (0,)), ((), ())), preferred_element_type=jnp.float32)


def low(value):
    return value.astype(jnp.bfloat16)


def high(value):
    return value.astype(jnp.float32)


def norm_backward(values, gain, cotangent):
    _, pull = jax.vjp(rms_norm, values, gain)
    return pull(cotangent)


def stacked(block, pair, lanes):
    block = high(block[:, pair * GROUP : (pair + 1) * GROUP])
    other = pltpu.roll(block, DH, 1)
    if pair == 0:
        rows = jnp.concatenate([block, other], axis=0)
        keep = lanes < DH
    else:
        rows = jnp.concatenate([other, block], axis=0)
        keep = lanes >= DH
    return low(jnp.where(keep, rows, 0.0))


def unstacked(parts):
    heads = []
    for pair, value in enumerate(parts):
        half = value[:, pair * DH : (pair + 1) * DH]
        heads += [half[0:GROUP], half[GROUP : 2 * GROUP]]
    return jnp.concatenate(heads, axis=1)


def all_stacked(block):
    lanes = lax.broadcasted_iota(jnp.int32, (1, GROUP), 1)
    return jnp.concatenate([stacked(block, 0, lanes), stacked(block, 1, lanes)], axis=0)


def all_unstacked(value):
    return low(unstacked([value[0 : 2 * GROUP], value[2 * GROUP :]]))


def pieces(span):
    return [slice(at, at + 512) for at in range(0, span, 512)]


def cross_forward_kernel(q_ref, kv_ref, o_ref, lse_ref, scores):
    query = all_stacked(q_ref[...])
    best = jnp.full((1, 4 * GROUP), MASKED, jnp.float32)
    for rows in pieces(kv_ref.shape[0]):
        part = dot_t(kv_ref[rows, 0:GROUP], query)
        scores[rows, :] = part
        best = jnp.maximum(best, jnp.max(part, axis=0, keepdims=True))
    total = jnp.zeros((1, 4 * GROUP), jnp.float32)
    mixed = jnp.zeros((GROUP, 4 * GROUP), jnp.float32)
    for rows in pieces(kv_ref.shape[0]):
        part = jnp.exp(scores[rows, :] - best)
        total = total + jnp.sum(part, axis=0, keepdims=True)
        mixed = mixed + t_dot(kv_ref[rows, GROUP : 2 * GROUP], low(part))
    o_ref[...] = all_unstacked((mixed / total).T)
    lse = best + jnp.log(total)
    lse_ref[0, 0:1, :] = lse[:, 0 : 2 * GROUP]
    lse_ref[0, 1:2, :] = lse[:, 2 * GROUP :]


def inner_of(dout, out):
    return jnp.sum((high(dout) * high(out)).T, axis=0, keepdims=True)


def cross_backward_kernel(q_ref, do_ref, o_ref, kv_ref, lse_ref, dq_ref, dkv_ref):
    query = all_stacked(q_ref[...])
    dout = all_stacked(do_ref[...])
    inner = inner_of(dout, all_stacked(o_ref[...]))
    lse = jnp.concatenate([lse_ref[0, 0:1, :], lse_ref[0, 1:2, :]], axis=1)
    dq = jnp.zeros((GROUP, 4 * GROUP), jnp.float32)
    for rows in pieces(kv_ref.shape[0]):
        keys = kv_ref[rows, 0:GROUP]
        prob = jnp.exp(dot_t(keys, query) - lse)
        grad = low(prob * (dot_t(kv_ref[rows, GROUP : 2 * GROUP], dout) - inner))
        dkv_ref[rows, 0:GROUP] = low(dot(grad, query))
        dkv_ref[rows, GROUP : 2 * GROUP] = low(dot(low(prob), dout))
        dq = dq + t_dot(keys, grad)
    dq_ref[...] = all_unstacked((dq * DH ** (-0.5)).T)


def self_scores(kv_ref, query, bias_ref, pair):
    rows = kv_ref.shape[0]
    scores = dot_t(kv_ref[:, 0:GROUP], query)
    scores = scores + jnp.concatenate([bias_ref[2 * pair], bias_ref[2 * pair + 1]], axis=1)
    key_at = lax.broadcasted_iota(jnp.int32, scores.shape, 0)
    query_at = lax.broadcasted_iota(jnp.int32, scores.shape, 1) % rows
    return scores, key_at <= query_at


def self_forward_kernel(q_ref, kv_ref, bias_ref, o_ref, lse_ref):
    lanes = lax.broadcasted_iota(jnp.int32, (1, GROUP), 1)
    outs = []
    for pair in range(2):
        query = stacked(q_ref[...], pair, lanes)
        scores, seen = self_scores(kv_ref, query, bias_ref, pair)
        scores = jnp.where(seen, scores, MASKED)
        best = jnp.max(scores, axis=0, keepdims=True)
        part = jnp.exp(scores - best)
        total = jnp.sum(part, axis=0, keepdims=True)
        mixed = t_dot(kv_ref[:, GROUP : 2 * GROUP], low(part / total))
        outs.append(mixed.T)
        lse_ref[0, pair : pair + 1, :] = best + jnp.log(total)
    o_ref[...] = low(unstacked(outs))


def self_backward_kernel(
    q_ref, do_ref, o_ref, kv_ref, lse_ref, bias_ref, dq_ref, dkv_ref, ds_ref
):
    lanes = lax.broadcasted_iota(jnp.int32, (1, GROUP), 1)
    dqs = []
    dk = 0.0
    dv = 0.0
    for pair in range(2):
        query = stacked(q_ref[...], pair, lanes)
        dout = stacked(do_ref[...], pair, lanes)
        inner = inner_of(dout, stacked(o_ref[...], pair, lanes))
        scores, seen = self_scores(kv_ref, query, bias_ref, pair)
        prob = jnp.exp(jnp.where(seen, scores - lse_ref[0, pair : pair + 1, :], MASKED))
        grad = low(prob * (dot_t(kv_ref[:, GROUP : 2 * GROUP], dout) - inner))
        ds_ref[2 * pair] = grad[:, 0:GROUP]
        ds_ref[2 * pair + 1] = grad[:, GROUP : 2 * GROUP]
        dk = dk + dot(grad, query)
        dv = dv + dot(low(prob), dout)
        dqs.append((t_dot(kv_ref[:, 0:GROUP], grad) * DH ** (-0.5)).T)
    dkv_ref[:, 0:GROUP] = low(dk)
    dkv_ref[:, GROUP : 2 * GROUP] = low(dv)
    dq_ref[...] = low(unstacked(dqs))


def attention_specs(rows, span):
    narrow = pl.BlockSpec((rows, 2 * GROUP), lambda k: (0, k))
    tall = pl.BlockSpec((span, 2 * GROUP), lambda k: (0, k))
    lse = pl.BlockSpec((1, 2, 2 * GROUP), lambda k: (k, 0, 0))
    square = pl.BlockSpec((4, rows, rows), lambda k: (k, 0, 0))
    return narrow, tall, lse, square


def kernel_call(kernel, name, blocks, specs, outs, scratch, cost, arguments, limit=32):
    return pl.pallas_call(
        kernel,
        grid=(blocks,),
        in_specs=specs,
        out_specs=[spec for spec, _, _ in outs],
        out_shape=[jax.ShapeDtypeStruct(shape, kind) for _, shape, kind in outs],
        scratch_shapes=scratch,
        compiler_params=pltpu.CompilerParams(vmem_limit_bytes=limit * 2**20),
        cost_estimate=pl.CostEstimate(flops=cost[0], bytes_accessed=cost[1], transcendentals=cost[2]),
        name=name,
    )(*arguments)


def attention_forward(query, pairs, bias):
    rows, span = query.shape[0], pairs.shape[0]
    blocks = query.shape[1] // (2 * GROUP)
    narrow, tall, lse, square = attention_specs(rows, span)
    cost = (
        16 * rows * span * DH * blocks,
        2 * (2 * query.size + pairs.size),
        4 * rows * span * blocks,
    )
    outs = [
        (narrow, query.shape, jnp.bfloat16),
        (lse, (blocks, 2, 2 * GROUP), jnp.float32),
    ]
    if bias is not None:
        return kernel_call(
            self_forward_kernel,
            "self_forward",
            blocks,
            [narrow, tall, square],
            outs,
            [],
            cost,
            (query, pairs, bias),
        )
    return kernel_call(
        cross_forward_kernel,
        "cross_forward",
        blocks,
        [narrow, tall],
        outs,
        [pltpu.VMEM((span, 4 * GROUP), jnp.float32)],
        cost,
        (query, pairs),
    )


def attention_backward(query, dout, out, pairs, lse_value, bias):
    rows, span = query.shape[0], pairs.shape[0]
    blocks = query.shape[1] // (2 * GROUP)
    narrow, tall, lse, square = attention_specs(rows, span)
    cost = (
        40 * rows * span * DH * blocks,
        2 * (4 * query.size + 2 * pairs.size),
        4 * rows * span * blocks,
    )
    outs = [(narrow, query.shape, jnp.bfloat16), (tall, pairs.shape, jnp.bfloat16)]
    if bias is not None:
        return kernel_call(
            self_backward_kernel,
            "self_backward",
            blocks,
            [narrow, narrow, narrow, tall, lse, square],
            outs + [(square, (4 * blocks, rows, rows), jnp.bfloat16)],
            [],
            cost,
            (query, dout, out, pairs, lse_value, bias),
        )
    return kernel_call(
        cross_backward_kernel,
        "cross_backward",
        blocks,
        [narrow, narrow, narrow, tall, lse],
        outs,
        [],
        cost,
        (query, dout, out, pairs, lse_value),
    )


def with_index(kernel, name, grid, specs, outs, scratch, cost, index, arguments, limit=32):
    return pl.pallas_call(
        kernel,
        grid_spec=pltpu.PrefetchScalarGridSpec(
            num_scalar_prefetch=1,
            grid=grid,
            in_specs=specs,
            out_specs=[spec for spec, _, _ in outs],
            scratch_shapes=scratch,
        ),
        out_shape=[jax.ShapeDtypeStruct(shape, kind) for _, shape, kind in outs],
        compiler_params=pltpu.CompilerParams(vmem_limit_bytes=limit * 2**20),
        cost_estimate=pl.CostEstimate(flops=cost[0], bytes_accessed=cost[1], transcendentals=0),
        name=name,
    )(index, *arguments)


def pack_shards(tp, cross_kv, self_q, self_kv, small, self_out, cross_q, cross_out):
    groups = [[cross_kv, self_q, self_kv, small], [self_out, cross_q, cross_out]]
    depths = [sum(part.size // GROUP for part in parts) for parts in groups]
    arguments = [part for parts in groups for part in parts]

    def kernel(*refs):
        ins, (near, *packs) = refs[: len(arguments)], refs[len(arguments) :]
        taken = 0
        above = 0
        for parts, pack, depth in zip(groups, packs, depths):
            at = 0
            for part in parts:
                rows = part.shape[0]
                for b in range(part.size // GROUP // rows):
                    if part.ndim == 3:
                        pack[at : at + rows, :] = ins[taken][:, b, :]
                    else:
                        pack[at : at + rows, :] = ins[taken][:, b * GROUP : (b + 1) * GROUP]
                    at += rows
                taken += 1
            for k in range(tp):
                near[k, above : above + depth, :] = pack[...]
            above += depth

    shapes = [(tp, depths[0] + depths[1], GROUP)] + [(depth, GROUP) for depth in depths]
    whole = [
        pl.BlockSpec(shape, lambda k, nothing=(0,) * len(shape): nothing) for shape in shapes
    ]
    return kernel_call(
        kernel,
        "pack_shards",
        1,
        [pl.BlockSpec(part.shape, lambda k, at=(0,) * part.ndim: at) for part in arguments],
        [(spec, shape, jnp.bfloat16) for spec, shape in zip(whole, shapes)],
        [],
        (0, 4 * sum(depths) * GROUP, 0),
        tuple(arguments),
        limit=56,
    )


def unpack_heads(index, near, far, depth, top, rows_first, width, extra):
    tp = near[0].shape[0]
    listed = isinstance(far[0], list)
    seq = (far[0][0].shape[0] if listed else far[0].shape[1]) + 1
    shard = width // (2 * seq)
    sides = tuple(far[0]) + tuple(far[1]) if listed else tuple(far)

    def kernel(index_ref, *refs):
        near_refs, far_refs = refs[0:2], refs[2 : 2 + len(sides)]
        outs = refs[2 + len(sides) :]

        def place(q, side, read):
            row = 2 * (index_ref[0] ^ q) + (index_ref[2] ^ side)
            at = pl.ds(pl.multiple_of(row * shard, shard), shard)
            for entry, (out, down) in enumerate(zip(outs, rows_first)):
                start = entry * 2 * shard
                if down:
                    out[:, at] = read(start, 2 * shard)
                else:
                    for b in range(2):
                        out[at, b * GROUP : (b + 1) * GROUP] = read(start + b * shard, shard)
            if extra:
                outs[-1][0, row] = read(depth - extra, extra)

        for side in range(2):
            place(0, side, lambda start, size: near_refs[side][0, top + start : top + start + size, :])
            for q in range(1, seq):
                if listed:
                    for k in range(tp):

                        @pl.when(pl.program_id(0) == k)
                        def _():
                            ref = far_refs[side * tp + k]
                            place(q, side, lambda start, size: ref[q - 1, start : start + size, :])

                else:
                    place(
                        q,
                        side,
                        lambda start, size: far_refs[side][0, q - 1, start : start + size, :],
                    )

    specs = [pl.BlockSpec((1,) + near[0].shape[1:], lambda k, index: (k ^ index[1], 0, 0))] * 2
    for value in sides:
        if listed:
            specs.append(pl.BlockSpec(value.shape, lambda k, index: (0, 0, 0)))
        else:
            specs.append(
                pl.BlockSpec((1,) + value.shape[1:], lambda k, index: (k ^ index[1], 0, 0, 0))
            )
    outs = []
    for down in rows_first:
        if down:
            spec = pl.BlockSpec((2 * GROUP, width), lambda k, index: (k, 0))
            outs.append((spec, (tp * 2 * GROUP, width), jnp.bfloat16))
        else:
            spec = pl.BlockSpec((width, 2 * GROUP), lambda k, index: (0, k))
            outs.append((spec, (width, tp * 2 * GROUP), jnp.bfloat16))
    if extra:
        spec = pl.BlockSpec((1, 2 * seq, extra, GROUP), lambda k, index: (k, 0, 0, 0))
        outs.append((spec, (tp, 2 * seq, extra, GROUP), jnp.bfloat16))
    return with_index(
        kernel,
        "unpack_heads",
        (tp,),
        specs,
        outs,
        [],
        (0, 8 * tp * seq * depth * GROUP),
        index,
        (*near, *sides),
    )


def unpack_hidden(value, width, hidden_width):
    count = value.shape[0]
    shard = width // count
    columns = 2 * hidden_width // GROUP

    def kernel(in_ref, gate_up_ref, down_ref):
        for b in range(columns):
            gate_up_ref[:, b * GROUP : (b + 1) * GROUP] = in_ref[0, b * shard : (b + 1) * shard, :]
        down_ref[...] = in_ref[0, columns * shard :, :]

    return kernel_call(
        kernel,
        "unpack_hidden",
        count,
        [pl.BlockSpec((1, value.shape[1], GROUP), lambda k: (k, 0, 0))],
        [
            (
                pl.BlockSpec((shard, 2 * hidden_width), lambda k: (k, 0)),
                (width, 2 * hidden_width),
                jnp.bfloat16,
            ),
            (
                pl.BlockSpec((hidden_width, shard), lambda k: (0, k)),
                (hidden_width, width),
                jnp.bfloat16,
            ),
        ],
        [],
        (0, 4 * value.size, 0),
        (value,),
    )


def memory_terms(index, seq, memory, pairs, weight, tp):
    rows, width = pairs.shape
    shard = width // (2 * seq)
    features = weight.shape[0] // tp
    steps = 2 * seq
    block = rows // steps
    early = max(steps // 4, 1)

    def row_of(step, index):
        return 2 * (index[0] ^ (step % seq)) + (index[2] ^ (1 - step // seq))

    def kernel(index_ref, memory_ref, pairs_ref, weight_ref, sent_ref, kept_ref, *outs):
        step = pl.program_id(0)
        part = t_dot(memory_ref[0], pairs_ref[...])

        @pl.when(step < seq)
        def _():
            sent_ref[0] = low(part)

        @pl.when(step >= seq)
        def _():
            kept_ref[0] = part

        values = pairs_ref[pl.ds(pl.multiple_of(step * block, block), block), :]
        for k in range(tp):
            at = pl.multiple_of((index_ref[1] ^ k) * features, features)
            outs[tp + k][...] = low(dot_t(values, weight_ref[pl.ds(at, features), :]))

        @pl.when(step < early)
        def _():
            for k in range(tp):
                outs[k][...] = outs[tp + k][...]

    shape = (seq, shard, width)
    first = pl.BlockSpec((block, features), lambda s, index: (jnp.minimum(s, early - 1), 0))
    second = pl.BlockSpec((block, features), lambda s, index: (jnp.maximum(s - early, 0), 0))
    return with_index(
        kernel,
        "memory_terms",
        (steps,),
        [
            pl.BlockSpec((1, rows, shard), lambda s, index: (index[1], 0, row_of(s, index))),
            pl.BlockSpec(pairs.shape, lambda s, index: (0, 0)),
            pl.BlockSpec(weight.shape, lambda s, index: (0, 0)),
        ],
        [
            (
                pl.BlockSpec((1, shard, width), lambda s, index: (jnp.minimum(s, seq - 1), 0, 0)),
                shape,
                jnp.bfloat16,
            ),
            (
                pl.BlockSpec((1, shard, width), lambda s, index: (jnp.maximum(s - seq, 0), 0, 0)),
                shape,
                jnp.float32,
            ),
        ]
        + [(first, (early * block, features), jnp.bfloat16)] * tp
        + [(second, (rows - early * block, features), jnp.bfloat16)] * tp,
        [],
        (4 * rows * width * width, 6 * pairs.size),
        index,
        (memory, pairs, weight),
    )


def hidden_out(index, hidden, weight, values, tp):
    rows = hidden.shape[0] // tp
    width = weight.shape[1]

    def kernel(index_ref, hidden_ref, weight_ref, values_ref, out_ref):
        part = dot(hidden_ref[...], weight_ref[...])

        @pl.when(pl.program_id(0) == 0)
        def _():
            out_ref[0] = low(part + values_ref[...])

        @pl.when(pl.program_id(0) != 0)
        def _():
            out_ref[0] = low(part)

    return with_index(
        kernel,
        "hidden_out",
        (tp,),
        [
            pl.BlockSpec((rows, hidden.shape[1]), lambda k, index: (k, 0)),
            pl.BlockSpec(weight.shape, lambda k, index: (0, 0)),
            pl.BlockSpec(values.shape, lambda k, index: (0, 0)),
        ],
        [
            (
                pl.BlockSpec((1, rows, width), lambda k, index: (k ^ index[1], 0, 0)),
                (tp, rows, width),
                jnp.bfloat16,
            )
        ],
        [],
        (2 * hidden.size * width, 2 * (hidden.size + weight.size + tp * rows * width)),
        index,
        (hidden, weight, values),
    )[0]


def row_terms(index, seq, name, pairs):
    width = pairs[0][0][0].shape[-1] if isinstance(pairs[0][0], list) else pairs[0][0].shape[-1]
    shard = width // (2 * seq)
    columns = sum(right[0][2] - right[0][1] for _, right in pairs)

    def row_of(step, index):
        return 2 * (index[0] ^ (step % seq)) + (index[2] ^ (1 - step // seq))

    def kernel(index_ref, *refs):
        sent_ref, kept_ref = refs[-2:]
        parts = []
        at = 0
        for left, right in pairs:
            if isinstance(left, list):
                value = jnp.concatenate([ref[...] for ref in refs[at : at + len(left)]], axis=0)
                at += len(left)
            else:
                value = refs[at][0]
                at += 1
            other = [ref[:, low_at:high_at] for ref, (_, low_at, high_at) in zip(refs[at:], right)]
            at += len(right)
            parts.append(t_dot(value, jnp.concatenate(other, axis=0)))

        def put(ref, kind):
            at = 0
            for part in parts:
                ref[0, :, at : at + part.shape[1]] = part.astype(kind)
                at += part.shape[1]

        @pl.when(pl.program_id(0) < seq)
        def _():
            put(sent_ref, jnp.bfloat16)

        @pl.when(pl.program_id(0) >= seq)
        def _():
            put(kept_ref, jnp.float32)

    specs = []
    arguments = []
    depth = 0
    for left, right in pairs:
        if isinstance(left, list):
            for part in left:
                rows = part.shape[0]
                specs.append(pl.BlockSpec((rows, shard), lambda s, index: (0, row_of(s, index))))
                arguments.append(part)
        else:
            specs.append(
                pl.BlockSpec(
                    (1, left.shape[1], shard), lambda s, index: (index[1], 0, row_of(s, index))
                )
            )
            arguments.append(left)
        for part, _, _ in right:
            specs.append(pl.BlockSpec(part.shape, lambda s, index: (0, 0)))
            arguments.append(part)
        depth = max(depth, sum(part.shape[0] for part, _, _ in right))
    shape = (seq, shard, columns)
    block = (1, shard, columns)
    return with_index(
        kernel,
        name,
        (2 * seq,),
        specs,
        [
            (
                pl.BlockSpec(block, lambda s, index: (jnp.minimum(s, seq - 1), 0, 0)),
                shape,
                jnp.bfloat16,
            ),
            (
                pl.BlockSpec(block, lambda s, index: (jnp.maximum(s - seq, 0), 0, 0)),
                shape,
                jnp.float32,
            ),
        ],
        [],
        (2 * depth * width * columns, 2 * depth * (width + columns) + 3 * width * columns),
        index,
        tuple(arguments),
        limit=56,
    )


def hidden_terms(normed, grad_joined, rounded, hidden):
    rows, width = normed.shape
    columns = grad_joined.shape[1] + hidden.shape[1]
    split = grad_joined.shape[1]
    steps = width // GROUP

    def kernel(normed_ref, joined_ref, rounded_ref, hidden_ref, out_ref):
        out_ref[:, :split] = low(t_dot(normed_ref[...], joined_ref[...]))
        out_ref[:, split:] = low(t_dot(rounded_ref[...], hidden_ref[...]))

    left = pl.BlockSpec((rows, GROUP), lambda k: (0, k))
    return kernel_call(
        kernel,
        "hidden_terms",
        steps,
        [
            left,
            pl.BlockSpec(grad_joined.shape, lambda k: (0, 0)),
            left,
            pl.BlockSpec(hidden.shape, lambda k: (0, 0)),
        ],
        [(pl.BlockSpec((GROUP, columns), lambda k: (k, 0)), (width, columns), jnp.bfloat16)],
        [],
        (2 * rows * width * columns, 4 * rows * (width + columns) + 2 * width * columns, 0),
        (normed, grad_joined, rounded, hidden),
    )[0]


def one_each(seq, tp):
    everyone = ("seq", "tp", "fsdp")

    def after(value, *earlier):
        return lax.optimization_barrier((value, earlier))[0]

    def together(*values):
        return lax.optimization_barrier(values)

    def swap(value, axis, flip):
        size = {"seq": seq, "tp": tp, "fsdp": 2}[axis]
        return lax.ppermute(value, axis, [(place, place ^ flip) for place in range(size)])

    def gather(value, axis, size):
        return [value] + [swap(value, axis, flip) for flip in range(1, size)]

    def exchange(parts, axis):
        return [parts[0]] + [swap(parts[k], axis, k) for k in range(1, len(parts))]

    def exchange_all(value):
        return lax.all_to_all(value, "tp", 0, 0, tiled=True)

    def to_everyone(value):
        return exchange_all(jnp.broadcast_to(value[None], (tp,) + value.shape))

    def total(parts):
        result = high(parts[0])
        for part in parts[1:]:
            result = result + high(part)
        return result

    def run(
        decoder_in,
        memory,
        buckets,
        norm_gains,
        rel_bias,
        self_q,
        self_kv,
        self_out,
        cross_q,
        cross_kv,
        cross_out,
        gate_up,
        down,
        cotangent,
    ):
        count, rows, width = decoder_in.shape
        z = lax.axis_index("seq")
        t = lax.axis_index("tp")
        c = lax.axis_index("fsdp")
        index = jnp.stack([z, t, c]).astype(jnp.int32)
        cores = 2
        shard = self_q.shape[0]
        tables = rel_bias.shape[0]
        heads = rel_bias.shape[1]
        hidden_width = down.shape[0]
        extra = 16

        def own(value):
            return lax.dynamic_index_in_dim(value, t, 0, keepdims=False)

        def from_here(value):
            return [
                lax.dynamic_index_in_dim(value, t ^ k, 0, keepdims=False) for k in range(tp)
            ]

        def in_order(parts, kind):
            result = jnp.zeros((count,) + parts[0].shape, kind)
            for k, part in enumerate(parts):
                result = lax.dynamic_update_index_in_dim(result, part.astype(kind), t ^ k, 0)
            return result

        def head_blocks(value):
            size = value.shape[1] // tp
            return [value[:, k * size : (k + 1) * size] for k in range(tp)]

        small = jnp.concatenate(
            [
                norm_gains,
                jnp.pad(rel_bias.reshape(1, -1), ((0, 0), (0, GROUP - rel_bias.size))),
                jnp.zeros((extra - 4, GROUP), jnp.bfloat16),
            ],
            axis=0,
        )
        near, pack_a, pack_b = pack_shards(
            tp, cross_kv, self_q, self_kv, small, self_out, cross_q, cross_out
        )
        gate_up, down = after((gate_up, down), near)
        pack_f = jnp.concatenate([lane_blocks(flatten(gate_up)), down], axis=0)

        depth_a, depth_b = pack_a.shape[0], pack_b.shape[0]
        near = exchange_all(near)
        ring_a = gather(pack_a, "seq", seq)
        ring_b = gather(after(pack_b, *ring_a), "seq", seq)
        far_a = to_everyone(after(jnp.stack(ring_a[1:]), near))
        far_b = after(jnp.stack(ring_b[1:]), far_a)
        buckets, decoder_in, cotangent = after((buckets, decoder_in, cotangent), far_b)
        far_b = gather(far_b, "tp", tp)
        full_f = lax.all_gather(after(pack_f, *ring_b), ("seq", "fsdp"), axis=0, tiled=True)
        near = [near, swap(near, "fsdp", 1)]
        far_a = [far_a, swap(far_a, "fsdp", 1)]

        cross_pairs, weight_self_q, weight_self_kv, smalls = unpack_heads(
            index, near, far_a, depth_a, 0, (False, False, False), width, extra
        )
        weight_gate_up, weight_down = unpack_hidden(
            full_f.reshape(seq * cores, -1, GROUP), width, hidden_width
        )
        gain_rows = high(smalls[0, :, 0:3].transpose(1, 0, 2).reshape(3, width))
        table = smalls[:, :, 3, 0 : tables * heads].reshape(tp, seq * cores, tables, heads)
        table = table.transpose(1, 2, 0, 3).reshape(NB, tp * heads)
        onehot = (
            buckets.T[:, :, None] == jnp.arange(NB, dtype=jnp.int32)[None, None, :]
        ).astype(jnp.bfloat16)
        bias = jnp.einsum("jin,nh->hji", onehot, table, preferred_element_type=jnp.float32)

        pairs = low(dot(own(memory), cross_pairs))
        start = high(own(decoder_in))
        scale = DH ** (-0.5)

        normed_self = low(rms_norm(start, gain_rows[0]))
        query_self = low(dot(normed_self, weight_self_q) * scale)
        pair_self = low(dot(normed_self, weight_self_kv))
        mixed_self, log_self = attention_forward(query_self, pair_self, bias)
        far_b = [after(part, mixed_self, pairs) for part in far_b]
        far_b = [far_b, [swap(part, "fsdp", 1) for part in far_b]]
        weight_self_out, weight_cross_q, weight_cross_out = unpack_heads(
            index, near, far_b, depth_b, depth_a, (True, False, True), width, 0
        )
        after_self = start + dot(mixed_self, weight_self_out)

        normed_cross = low(rms_norm(after_self, gain_rows[1]))
        query_cross = low(dot(normed_cross, weight_cross_q) * scale)
        mixed_cross, log_cross = attention_forward(query_cross, pairs, None)
        after_cross = after_self + dot(mixed_cross, weight_cross_out)
        normed_ffn = low(rms_norm(after_cross, gain_rows[2]))

        all_cross = lax.all_gather(normed_cross, "tp", axis=0, tiled=True)
        normed_parts, weight_gate_up, weight_down, own_cotangent, rounded = together(
            gather(normed_ffn, "tp", tp),
            weight_gate_up,
            weight_down,
            own(cotangent),
            jnp.concatenate(from_here(cotangent), axis=0),
        )
        all_normed = jnp.concatenate(normed_parts, axis=0)
        joined = dot(all_normed, weight_gate_up)
        gate = joined[:, :hidden_width]
        up = joined[:, hidden_width:]
        grad_hidden = dot_t(rounded, weight_down)
        hidden = low(gelu_product(gate, up))
        _, pull = jax.vjp(gelu_product, gate, up)
        grad_gate, grad_up = pull(grad_hidden)
        grad_joined = low(jnp.concatenate([grad_gate, grad_up], axis=-1))

        def row_parts(value):
            return [value[k * rows : (k + 1) * rows] for k in range(tp)]

        partial_normed = row_parts(low(dot_t(grad_joined, weight_gate_up)))
        grad_parts = exchange(partial_normed, "tp")
        all_normed, grad_joined, rounded, hidden, o_self, o_cross = after(
            (all_normed, grad_joined, rounded, hidden, mixed_self, mixed_cross), partial_normed
        )
        hidden_grads = hidden_terms(all_normed, grad_joined, rounded, hidden)
        partial_out = hidden_out(index, hidden, weight_down, after_cross, tp)
        o_blocks = [
            jnp.concatenate(blocks, axis=1)
            for blocks in zip(head_blocks(o_self), head_blocks(o_cross))
        ]
        grad_parts, hidden_grads, partial_out, o_blocks = together(
            grad_parts, hidden_grads, partial_out, o_blocks
        )
        hidden_grads = high(
            lax.psum_scatter(hidden_grads, ("seq", "fsdp"), scatter_dimension=0, tiled=True)
        )

        grad_normed = total(grad_parts)
        grad_residual, gain_ffn = norm_backward(after_cross, gain_rows[2], grad_normed)
        grad_cross = high(own_cotangent) + grad_residual
        rounded_cross = low(grad_cross)
        cross_operands = [jnp.concatenate([rounded_cross, block], axis=1) for block in o_blocks]
        cross_parts = exchange(cross_operands, "tp")
        grad_mixed = low(dot_t(after(rounded_cross, cross_operands), weight_cross_out))
        grad_query, grad_pairs = attention_backward(
            query_cross, grad_mixed, mixed_cross, pairs, log_cross, None
        )
        cross_parts, grad_query, grad_pairs = together(cross_parts, grad_query, grad_pairs)
        grad_normed = dot_t(grad_query, weight_cross_q)
        grad_residual, gain_cross = norm_backward(after_self, gain_rows[1], grad_normed)
        grad_self = grad_cross + grad_residual
        rounded_self = low(grad_self)
        self_operands = [
            jnp.concatenate([rounded_self, block], axis=1) for block in head_blocks(grad_query)
        ]
        self_parts = exchange(self_operands, "tp")

        grad_mixed_self = low(dot_t(after(rounded_self, self_operands), weight_self_out))
        grad_query_self, grad_pair_self, grad_scores = attention_backward(
            query_self, grad_mixed_self, mixed_self, pair_self, log_self, bias
        )
        grad_normed = dot_t(grad_query_self, weight_self_q) + dot_t(grad_pair_self, weight_self_kv)
        grad_residual, gain_self = norm_backward(start, gain_rows[0], grad_normed)
        grad_tokens = low(grad_self + grad_residual)
        last_operands = [
            jnp.concatenate([grad_tokens, q_block, kv_block], axis=1)
            for q_block, kv_block in zip(head_blocks(grad_query_self), head_blocks(grad_pair_self))
        ]
        self_parts, last_operands, memory_pairs, decoder_in, gains, grad_scores = together(
            self_parts,
            last_operands,
            grad_pairs,
            decoder_in,
            (gain_self, gain_cross, gain_ffn),
            grad_scores,
        )
        last_parts = exchange(last_operands, "tp")

        kv_sent, kv_rows, *memory_parts = memory_terms(
            index, seq, memory, memory_pairs, cross_pairs, tp
        )
        last_parts, kv_sent, kv_rows, memory_parts, gains, grad_scores, partial_out = together(
            last_parts, kv_sent, kv_rows, memory_parts, gains, grad_scores, partial_out
        )
        decoder_out = lax.psum(partial_out, "tp")
        first_parts = exchange(memory_parts[:tp], "tp")
        kv_rows = kv_rows + high(swap(kv_sent, "fsdp", 1))

        def span_of(parts, first, last):
            return [(part, first, last) for part in parts]

        all_start = [
            low(rms_norm(high(part), gain_rows[0])) for part in from_here(decoder_in)
        ]
        both_sent, both_kept = row_terms(
            index,
            seq,
            "head_weights",
            [
                (
                    from_here(all_cross.reshape(tp, rows, width)),
                    span_of(self_parts, width, width + 2 * GROUP),
                ),
                (cross_parts, span_of(cross_parts, width + 2 * GROUP, width + 4 * GROUP)),
                (all_start, span_of(last_parts, width, width + 4 * GROUP)),
                (self_parts, span_of(cross_parts, width, width + 2 * GROUP)),
            ],
        )
        kv_far = low(kv_rows[seq // 2 :])
        first_parts, kv_far, kv_rows, both_sent, both_kept, second_parts = together(
            first_parts, kv_far, kv_rows, both_sent, both_kept, memory_parts[tp:]
        )
        kv_far = swap(kv_far, "seq", seq // 2)
        second_parts = exchange(second_parts, "tp")
        both_grads = low(both_kept + high(swap(both_sent, "fsdp", 1)))
        both_grads = jnp.concatenate(
            [
                lax.dynamic_index_in_dim(both_grads, z ^ k, 0, keepdims=True) for k in range(seq)
            ],
            axis=0,
        )
        gains, grad_scores, last_parts, kv_far, second_parts, hidden_grads = after(
            (gains, grad_scores, last_parts, kv_far, second_parts, hidden_grads), both_grads
        )
        gate_up_grad = hidden_grads[:, : 2 * hidden_width].reshape(gate_up.shape)
        down_grad = hidden_grads[:, 2 * hidden_width :].T
        both_grads = lax.all_to_all(both_grads, "seq", 0, 0, tiled=True)
        kv_rows = kv_rows[: seq // 2] + high(kv_far)
        step = seq // 4
        while step:
            kv_rows = kv_rows[:step] + high(swap(low(kv_rows[step:]), "seq", step))
            step //= 2
        kv_rows = kv_rows[0]
        memory_grad = jnp.zeros((count, memory.shape[1], first_parts[0].shape[1]), jnp.bfloat16)
        cut = first_parts[0].shape[0]
        for at, parts in ((0, first_parts), (cut, second_parts)):
            for k in range(tp):
                memory_grad = lax.dynamic_update_slice(
                    memory_grad, parts[k][None], (t ^ k, at, 0)
                )
        decoder_grad = in_order([part[:, :width] for part in last_parts], jnp.float32)

        table_grad = jnp.einsum(
            "jin,hji->nh", onehot, grad_scores, preferred_element_type=jnp.float32
        )
        gain_parts = jnp.stack([gain.reshape(-1, GROUP) for gain in gains], axis=1)
        table_parts = jnp.pad(
            table_grad.reshape(seq * cores, 1, -1),
            ((0, 0), (0, 0), (0, GROUP - tables * tp * heads)),
        )
        little = low(jnp.concatenate([gain_parts, table_parts], axis=1))
        little = jnp.broadcast_to(
            little.reshape(seq, 1, cores, 4, GROUP), (seq, tp, cores, 4, GROUP)
        )
        both_grads, little, gate_up_grad, down_grad, decoder_grad, kv_rows, memory_grad = together(
            both_grads, little, gate_up_grad, down_grad, decoder_grad, kv_rows, memory_grad
        )
        cross_kv_grad = total(
            exchange([kv_rows[:, : 2 * GROUP]] + head_blocks(low(kv_rows))[1:], "tp")
        )
        little = lax.all_to_all(little.reshape(-1, 4, GROUP), everyone, 0, 0, tiled=True)
        little = jnp.sum(high(little).reshape(seq, tp, cores, 4, GROUP), axis=(0, 2))
        sender = jnp.arange(tp, dtype=jnp.int32)
        chosen = (sender[:, None] ^ sender[None, :]) == t
        table_sum = little[:, 3, : tables * tp * heads].reshape(tp, tables, tp, heads)
        table_sum = jnp.sum(jnp.where(chosen[:, None, :, None], table_sum, 0.0), axis=(0, 2))
        little = jnp.sum(little, axis=0)
        both_grads = jnp.sum(high(both_grads), axis=0)
        cross_grads = both_grads[:, : 4 * GROUP]
        self_grads = both_grads[:, 4 * GROUP :]

        return (
            decoder_out,
            decoder_grad,
            memory_grad,
            little[0:3],
            table_sum,
            self_grads[:, 0 : 2 * GROUP],
            self_grads[:, 2 * GROUP : 4 * GROUP].reshape(self_kv.shape),
            self_grads[:, 4 * GROUP :].T,
            cross_grads[:, 0 : 2 * GROUP],
            cross_kv_grad.reshape(cross_kv.shape),
            cross_grads[:, 2 * GROUP :].T,
            gate_up_grad,
            down_grad,
        )

    return run


def plan_of(mesh):
    seq, tp, cores = (mesh.shape[axis] for axis in ("seq", "tp", "fsdp"))

    def chosen(*arrays):
        count, rows, width = arrays[0].shape
        fits = (
            cores == 2
            and seq & (seq - 1) == 0
            and tp & (tp - 1) == 0
            and count == tp
            and rows == GROUP
            and arrays[1].shape[1] % 512 == 0
            and width == 2 * seq * GROUP
            and arrays[5].shape[1] == 4 * DH
            and arrays[6].shape[2] == 2 * DH
            and tp * arrays[4].size <= GROUP
            and 2 * arrays[12].shape[0] % GROUP == 0
        )
        return (one_each(seq, tp) if fits else per_device)(*arrays)

    return chosen


def solution(mesh):
    return jax.shard_map(
        plan_of(mesh),
        mesh=mesh,
        in_specs=(
            P(("seq", "fsdp"), None, None),
            P(("seq", "fsdp"), None, None),
            P(),
            P(None, ("seq", "fsdp")),
            P(("seq", "fsdp"), "tp"),
            P(("seq", "fsdp"), "tp"),
            P(("seq", "fsdp"), None, "tp"),
            P("tp", ("seq", "fsdp")),
            P(("seq", "fsdp"), "tp"),
            P(("seq", "fsdp"), None, "tp"),
            P("tp", ("seq", "fsdp")),
            P(("seq", "fsdp"), None, "tp"),
            P("tp", ("seq", "fsdp")),
            P(("seq", "fsdp"), None, None),
        ),
        out_specs=(
            P(("seq", "fsdp"), None, None),
            P(("seq", "fsdp"), None, None),
            P(("seq", "fsdp"), None, "tp"),
            P(None, ("seq", "fsdp")),
            P(("seq", "fsdp"), "tp"),
            P(("seq", "fsdp"), "tp"),
            P(("seq", "fsdp"), None, "tp"),
            P("tp", ("seq", "fsdp")),
            P(("seq", "fsdp"), "tp"),
            P(("seq", "fsdp"), None, "tp"),
            P("tp", ("seq", "fsdp")),
            P(("seq", "fsdp"), None, "tp"),
            P("tp", ("seq", "fsdp")),
        ),
        check_vma=False,
    )
```

```python
import jax
import jax.numpy as jnp
from jax import lax
from jax.experimental import pallas as pl
from jax.experimental.pallas import tpu as pltpu
from jax.sharding import PartitionSpec as P

DH = 64
NB = 32
MICRO = 2


EPSILON = 1e-06
MASKED = -1e30


def rms_norm(values, gain):
    return values * lax.rsqrt(jnp.mean(values * values, axis=-1, keepdims=True) + EPSILON) * gain


def gelu_product(gate, up):
    return jax.nn.gelu(gate, approximate=True) * up


def flatten(weight):
    return weight.reshape(weight.shape[0], -1)


def gather_weights(
    gains, table, self_q, self_kv, self_out, cross_q, cross_kv, cross_out, gate_up, down
):
    return (
        lax.all_gather(gains, ("seq", "fsdp"), axis=1, tiled=True),
        lax.all_gather(table, ("seq", "fsdp"), axis=0, tiled=True),
        lax.all_gather(self_q, ("seq", "fsdp"), axis=0, tiled=True),
        lax.all_gather(self_kv, ("seq", "fsdp"), axis=0, tiled=True),
        lax.all_gather(self_out, ("seq", "fsdp"), axis=1, tiled=True),
        lax.all_gather(cross_q, ("seq", "fsdp"), axis=0, tiled=True),
        lax.all_gather(cross_kv, ("seq", "fsdp"), axis=0, tiled=True),
        lax.all_gather(cross_out, ("seq", "fsdp"), axis=1, tiled=True),
        lax.all_gather(gate_up, ("seq", "fsdp"), axis=0, tiled=True),
        lax.all_gather(down, ("seq", "fsdp"), axis=1, tiled=True),
    )


def branch_total(partial_value):
    return lax.psum(partial_value.astype(jnp.bfloat16), "tp").astype(jnp.float32)


def input_total(partial_value):
    return lax.psum(partial_value.astype(jnp.bfloat16), "tp").astype(jnp.float32)


def split_heads(query, keys, values):
    batch, rows, width = query.shape
    span = keys.shape[1]
    groups = keys.shape[2] // DH
    ratio = width // DH // groups
    return (
        query.reshape(batch, rows, groups, ratio, DH),
        keys.reshape(batch, span, groups, DH),
        values.reshape(batch, span, groups, DH),
    )


def scores_of(query_heads, key_heads, bias, causal):
    scores = jnp.einsum(
        "bigrd,bjgd->bgrij", query_heads, key_heads, preferred_element_type=jnp.float32
    ) * DH ** (-0.5)
    if bias is not None:
        scores = scores + bias
    if causal is not None:
        scores = jnp.where(causal, scores, MASKED)
    return scores


def attend_forward(query, keys, values, bias, causal):
    query_heads, key_heads, value_heads = split_heads(query, keys, values)
    scores = scores_of(query_heads, key_heads, bias, causal)
    row_max = jnp.max(scores, axis=-1, keepdims=True)
    exponent = jnp.exp(scores - row_max)
    total = jnp.sum(exponent, axis=-1, keepdims=True)
    probs = (exponent / total).astype(jnp.bfloat16)
    mixed = jnp.einsum("bgrij,bjgd->bigrd", probs, value_heads, preferred_element_type=jnp.float32)
    return (mixed.reshape(query.shape).astype(jnp.bfloat16), row_max + jnp.log(total))


def attend_backward(query, keys, values, bias, causal, log_total, grad_mixed):
    query_heads, key_heads, value_heads = split_heads(query, keys, values)
    probs = jnp.exp(scores_of(query_heads, key_heads, bias, causal) - log_total)
    grad_heads = grad_mixed.reshape(query_heads.shape)
    grad_probs = jnp.einsum(
        "bigrd,bjgd->bgrij", grad_heads, value_heads, preferred_element_type=jnp.float32
    )
    inner = jnp.sum(probs * grad_probs, axis=-1, keepdims=True)
    grad_scores = (probs * (grad_probs - inner)).astype(jnp.bfloat16)
    scale = DH ** (-0.5)
    grad_query = (
        jnp.einsum("bgrij,bjgd->bigrd", grad_scores, key_heads, preferred_element_type=jnp.float32)
        * scale
    ).astype(jnp.bfloat16)
    grad_keys = (
        jnp.einsum(
            "bgrij,bigrd->bjgd", grad_scores, query_heads, preferred_element_type=jnp.float32
        )
        * scale
    ).astype(jnp.bfloat16)
    grad_values = jnp.einsum(
        "bgrij,bigrd->bjgd",
        probs.astype(jnp.bfloat16),
        grad_heads,
        preferred_element_type=jnp.float32,
    ).astype(jnp.bfloat16)
    return (
        grad_query.reshape(query.shape),
        grad_keys.reshape(keys.shape),
        grad_values.reshape(values.shape),
        grad_scores,
    )


def forward(tokens, memory, weights, onehot, causal):
    gains, table, self_q, self_kv, self_out, cross_q, cross_kv, cross_out, gate_up, down = weights
    gain_rows = gains.astype(jnp.float32)
    start = tokens.astype(jnp.float32)
    normed_self = rms_norm(start, gain_rows[0]).astype(jnp.bfloat16)
    query_self = jnp.dot(normed_self, self_q, preferred_element_type=jnp.float32).astype(
        jnp.bfloat16
    )
    pair_self = jnp.dot(normed_self, flatten(self_kv), preferred_element_type=jnp.float32).astype(
        jnp.bfloat16
    )
    half = pair_self.shape[-1] // 2
    keys_self = pair_self[..., :half]
    values_self = pair_self[..., half:]
    groups = half // DH
    heads = table.shape[1]
    rows = tokens.shape[1]
    bias = jnp.einsum("ijn,nh->hij", onehot, table, preferred_element_type=jnp.float32).reshape(
        groups, heads // groups, rows, rows
    )
    mixed_self, log_self = attend_forward(query_self, keys_self, values_self, bias, causal)
    after_self = start + branch_total(
        jnp.dot(mixed_self, self_out, preferred_element_type=jnp.float32)
    )
    normed_cross = rms_norm(after_self, gain_rows[1]).astype(jnp.bfloat16)
    query_cross = jnp.dot(normed_cross, cross_q, preferred_element_type=jnp.float32).astype(
        jnp.bfloat16
    )
    pair_cross = jnp.dot(memory, flatten(cross_kv), preferred_element_type=jnp.float32).astype(
        jnp.bfloat16
    )
    keys_cross = pair_cross[..., :half]
    values_cross = pair_cross[..., half:]
    mixed_cross, log_cross = attend_forward(query_cross, keys_cross, values_cross, None, None)
    after_cross = after_self + branch_total(
        jnp.dot(mixed_cross, cross_out, preferred_element_type=jnp.float32)
    )
    normed_ffn = rms_norm(after_cross, gain_rows[2]).astype(jnp.bfloat16)
    joined = jnp.dot(normed_ffn, flatten(gate_up), preferred_element_type=jnp.float32)
    hidden_width = joined.shape[-1] // 2
    gate = joined[..., :hidden_width]
    up = joined[..., hidden_width:]
    hidden = gelu_product(gate, up).astype(jnp.bfloat16)
    output = after_cross + branch_total(jnp.dot(hidden, down, preferred_element_type=jnp.float32))
    saved = (
        start,
        after_self,
        after_cross,
        normed_self,
        query_self,
        keys_self,
        values_self,
        bias,
        mixed_self,
        log_self,
        normed_cross,
        query_cross,
        keys_cross,
        values_cross,
        mixed_cross,
        log_cross,
        normed_ffn,
        gate,
        up,
        hidden,
    )
    return (output, saved)


def backward(saved, grad_out, memory, weights, onehot, causal):
    (
        start,
        after_self,
        after_cross,
        normed_self,
        query_self,
        keys_self,
        values_self,
        bias,
        mixed_self,
        log_self,
        normed_cross,
        query_cross,
        keys_cross,
        values_cross,
        mixed_cross,
        log_cross,
        normed_ffn,
        gate,
        up,
        hidden,
    ) = saved
    gains, table, self_q, self_kv, self_out, cross_q, cross_kv, cross_out, gate_up, down = weights
    gain_rows = gains.astype(jnp.float32)
    grad_ffn = grad_out.astype(jnp.float32)
    rounded = grad_ffn.astype(jnp.bfloat16)
    down_grad = jnp.einsum("blf,bld->fd", hidden, rounded, preferred_element_type=jnp.float32)
    grad_hidden = jnp.einsum("bld,fd->blf", rounded, down, preferred_element_type=jnp.float32)
    _, pull = jax.vjp(gelu_product, gate, up)
    grad_gate, grad_up = pull(grad_hidden)
    grad_joined = jnp.concatenate([grad_gate, grad_up], axis=-1).astype(jnp.bfloat16)
    gate_up_grad = jnp.einsum(
        "bld,blf->df", normed_ffn, grad_joined, preferred_element_type=jnp.float32
    ).reshape(gate_up.shape)
    grad_normed = input_total(
        jnp.einsum("blf,df->bld", grad_joined, flatten(gate_up), preferred_element_type=jnp.float32)
    )
    _, pull = jax.vjp(rms_norm, after_cross, gain_rows[2])
    grad_residual, gain_ffn = pull(grad_normed)
    grad_cross = grad_ffn + grad_residual
    rounded = grad_cross.astype(jnp.bfloat16)
    cross_out_grad = jnp.einsum(
        "blh,bld->hd", mixed_cross, rounded, preferred_element_type=jnp.float32
    )
    grad_mixed = jnp.einsum(
        "bld,hd->blh", rounded, cross_out, preferred_element_type=jnp.float32
    ).astype(jnp.bfloat16)
    grad_query, grad_keys, grad_values, _ = attend_backward(
        query_cross, keys_cross, values_cross, None, None, log_cross, grad_mixed
    )
    grad_pair_cross = jnp.concatenate([grad_keys, grad_values], axis=-1)
    cross_q_grad = jnp.einsum(
        "bld,blh->dh", normed_cross, grad_query, preferred_element_type=jnp.float32
    )
    cross_kv_grad = jnp.einsum(
        "bsd,bsw->dw", memory, grad_pair_cross, preferred_element_type=jnp.float32
    ).reshape(cross_kv.shape)
    grad_normed = input_total(
        jnp.einsum("blh,dh->bld", grad_query, cross_q, preferred_element_type=jnp.float32)
    )
    _, pull = jax.vjp(rms_norm, after_self, gain_rows[1])
    grad_residual, gain_cross = pull(grad_normed)
    grad_self = grad_cross + grad_residual
    rounded = grad_self.astype(jnp.bfloat16)
    self_out_grad = jnp.einsum(
        "blh,bld->hd", mixed_self, rounded, preferred_element_type=jnp.float32
    )
    grad_mixed = jnp.einsum(
        "bld,hd->blh", rounded, self_out, preferred_element_type=jnp.float32
    ).astype(jnp.bfloat16)
    grad_query, grad_keys, grad_values, grad_scores = attend_backward(
        query_self, keys_self, values_self, bias, causal, log_self, grad_mixed
    )
    batch = grad_scores.shape[0]
    rows = grad_scores.shape[-1]
    table_grad = jnp.einsum(
        "ijn,bhij->nh",
        onehot,
        grad_scores.reshape(batch, -1, rows, rows),
        preferred_element_type=jnp.float32,
    )
    grad_pair = jnp.concatenate([grad_keys, grad_values], axis=-1)
    self_q_grad = jnp.einsum(
        "bld,blh->dh", normed_self, grad_query, preferred_element_type=jnp.float32
    )
    self_kv_grad = jnp.einsum(
        "bld,blw->dw", normed_self, grad_pair, preferred_element_type=jnp.float32
    ).reshape(self_kv.shape)
    grad_normed = input_total(
        jnp.einsum("blh,dh->bld", grad_query, self_q, preferred_element_type=jnp.float32)
        + jnp.einsum("blw,dw->bld", grad_pair, flatten(self_kv), preferred_element_type=jnp.float32)
    )
    _, pull = jax.vjp(rms_norm, start, gain_rows[0])
    grad_residual, gain_self = pull(grad_normed)
    grad_tokens = grad_self + grad_residual
    gains_grad = jnp.stack([gain_self, gain_cross, gain_ffn])
    grads = (
        gains_grad,
        table_grad,
        self_q_grad,
        self_kv_grad,
        self_out_grad,
        cross_q_grad,
        cross_kv_grad,
        cross_out_grad,
        gate_up_grad,
        down_grad,
    )
    return (grad_tokens, grad_pair_cross, grads)


def per_device(
    decoder_in,
    memory,
    buckets,
    norm_gains,
    rel_bias,
    self_q,
    self_kv,
    self_out,
    cross_q,
    cross_kv,
    cross_out,
    gate_up,
    down,
    cotangent,
):
    local = decoder_in.shape[0]
    rows = decoder_in.shape[1]
    per_batch = local // MICRO
    positions = jnp.arange(rows, dtype=jnp.int32)
    causal = positions[:, None] >= positions[None, :]
    onehot = (buckets[:, :, None] == jnp.arange(NB, dtype=jnp.int32)[None, None, :]).astype(
        jnp.bfloat16
    )
    weights = gather_weights(
        norm_gains, rel_bias, self_q, self_kv, self_out, cross_q, cross_kv, cross_out, gate_up, down
    )
    outputs = []
    token_grads = []
    memory_grads = []
    totals = None
    for index in range(MICRO):
        lower = index * per_batch
        upper = lower + per_batch
        memory_part = memory[lower:upper]
        output, saved = forward(decoder_in[lower:upper], memory_part, weights, onehot, causal)
        grad_tokens, grad_pair_cross, grads = backward(
            saved, cotangent[lower:upper], memory_part, weights, onehot, causal
        )
        memory_term = jnp.einsum(
            "bsw,dw->bsd", grad_pair_cross, flatten(weights[6]), preferred_element_type=jnp.float32
        )
        memory_part_grad = lax.psum_scatter(
            memory_term.astype(jnp.bfloat16), "tp", scatter_dimension=2, tiled=True
        )
        memory_grads.append(memory_part_grad)
        outputs.append(output.astype(jnp.bfloat16))
        token_grads.append(grad_tokens)
        grads = (
            lax.psum_scatter(
                grads[0].astype(jnp.bfloat16), ("seq", "fsdp"), scatter_dimension=1, tiled=True
            ).astype(jnp.float32),
            lax.psum_scatter(
                grads[1].astype(jnp.bfloat16), ("seq", "fsdp"), scatter_dimension=0, tiled=True
            ).astype(jnp.float32),
            lax.psum_scatter(
                grads[2].astype(jnp.bfloat16), ("seq", "fsdp"), scatter_dimension=0, tiled=True
            ).astype(jnp.float32),
            lax.psum_scatter(
                grads[3].astype(jnp.bfloat16), ("seq", "fsdp"), scatter_dimension=0, tiled=True
            ).astype(jnp.float32),
            lax.psum_scatter(
                grads[4].astype(jnp.bfloat16), ("seq", "fsdp"), scatter_dimension=1, tiled=True
            ).astype(jnp.float32),
            lax.psum_scatter(
                grads[5].astype(jnp.bfloat16), ("seq", "fsdp"), scatter_dimension=0, tiled=True
            ).astype(jnp.float32),
            lax.psum_scatter(
                grads[6].astype(jnp.bfloat16), ("seq", "fsdp"), scatter_dimension=0, tiled=True
            ).astype(jnp.float32),
            lax.psum_scatter(
                grads[7].astype(jnp.bfloat16), ("seq", "fsdp"), scatter_dimension=1, tiled=True
            ).astype(jnp.float32),
            lax.psum_scatter(
                grads[8].astype(jnp.bfloat16), ("seq", "fsdp"), scatter_dimension=0, tiled=True
            ).astype(jnp.float32),
            lax.psum_scatter(
                grads[9].astype(jnp.bfloat16), ("seq", "fsdp"), scatter_dimension=1, tiled=True
            ).astype(jnp.float32),
        )
        totals = grads if totals is None else jax.tree.map(jnp.add, totals, grads)
    return (
        jnp.concatenate(outputs, axis=0),
        jnp.concatenate(token_grads, axis=0),
        jnp.concatenate(memory_grads, axis=0),
        totals[0],
        totals[1],
        totals[2],
        totals[3],
        totals[4],
        totals[5],
        totals[6],
        totals[7],
        totals[8],
        totals[9],
    )


GROUP = 128


def lane_blocks(value):
    count = value.shape[1] // GROUP
    return jnp.concatenate(
        [value[:, b * GROUP : (b + 1) * GROUP] for b in range(count)], axis=0
    )


def dot(left, right):
    return jnp.dot(left, right, preferred_element_type=jnp.float32)


def dot_t(left, right):
    return lax.dot_general(left, right, (((1,), (1,)), ((), ())), preferred_element_type=jnp.float32)


def t_dot(left, right):
    return lax.dot_general(left, right, (((0,), (0,)), ((), ())), preferred_element_type=jnp.float32)


def low(value):
    return value.astype(jnp.bfloat16)


def high(value):
    return value.astype(jnp.float32)


def norm_backward(values, gain, cotangent):
    _, pull = jax.vjp(rms_norm, values, gain)
    return pull(cotangent)


def stacked(block, pair, lanes):
    block = high(block[:, pair * GROUP : (pair + 1) * GROUP])
    other = pltpu.roll(block, DH, 1)
    if pair == 0:
        rows = jnp.concatenate([block, other], axis=0)
        keep = lanes < DH
    else:
        rows = jnp.concatenate([other, block], axis=0)
        keep = lanes >= DH
    return low(jnp.where(keep, rows, 0.0))


def unstacked(parts):
    heads = []
    for pair, value in enumerate(parts):
        half = value[:, pair * DH : (pair + 1) * DH]
        heads += [half[0:GROUP], half[GROUP : 2 * GROUP]]
    return jnp.concatenate(heads, axis=1)


def all_stacked(block):
    lanes = lax.broadcasted_iota(jnp.int32, (1, GROUP), 1)
    return jnp.concatenate([stacked(block, 0, lanes), stacked(block, 1, lanes)], axis=0)


def all_unstacked(value):
    return low(unstacked([value[0 : 2 * GROUP], value[2 * GROUP :]]))


def pieces(span):
    return [slice(at, at + 512) for at in range(0, span, 512)]


def cross_forward_kernel(q_ref, kv_ref, o_ref, lse_ref, scores):
    query = all_stacked(q_ref[...])
    best = jnp.full((1, 4 * GROUP), MASKED, jnp.float32)
    for rows in pieces(kv_ref.shape[0]):
        part = dot_t(kv_ref[rows, 0:GROUP], query)
        scores[rows, :] = part
        best = jnp.maximum(best, jnp.max(part, axis=0, keepdims=True))
    total = jnp.zeros((1, 4 * GROUP), jnp.float32)
    mixed = jnp.zeros((GROUP, 4 * GROUP), jnp.float32)
    for rows in pieces(kv_ref.shape[0]):
        part = jnp.exp(scores[rows, :] - best)
        total = total + jnp.sum(part, axis=0, keepdims=True)
        mixed = mixed + t_dot(kv_ref[rows, GROUP : 2 * GROUP], low(part))
    o_ref[...] = all_unstacked((mixed / total).T)
    lse = best + jnp.log(total)
    lse_ref[0, 0:1, :] = lse[:, 0 : 2 * GROUP]
    lse_ref[0, 1:2, :] = lse[:, 2 * GROUP :]


def inner_of(dout, out):
    return jnp.sum((high(dout) * high(out)).T, axis=0, keepdims=True)


def cross_backward_kernel(q_ref, do_ref, o_ref, kv_ref, lse_ref, dq_ref, dkv_ref):
    query = all_stacked(q_ref[...])
    dout = all_stacked(do_ref[...])
    inner = inner_of(dout, all_stacked(o_ref[...]))
    lse = jnp.concatenate([lse_ref[0, 0:1, :], lse_ref[0, 1:2, :]], axis=1)
    dq = jnp.zeros((GROUP, 4 * GROUP), jnp.float32)
    for rows in pieces(kv_ref.shape[0]):
        keys = kv_ref[rows, 0:GROUP]
        prob = jnp.exp(dot_t(keys, query) - lse)
        grad = low(prob * (dot_t(kv_ref[rows, GROUP : 2 * GROUP], dout) - inner))
        dkv_ref[rows, 0:GROUP] = low(dot(grad, query))
        dkv_ref[rows, GROUP : 2 * GROUP] = low(dot(low(prob), dout))
        dq = dq + t_dot(keys, grad)
    dq_ref[...] = all_unstacked((dq * DH ** (-0.5)).T)


def self_scores(kv_ref, query, bias_ref, pair):
    rows = kv_ref.shape[0]
    scores = dot_t(kv_ref[:, 0:GROUP], query)
    scores = scores + jnp.concatenate([bias_ref[2 * pair], bias_ref[2 * pair + 1]], axis=1)
    key_at = lax.broadcasted_iota(jnp.int32, scores.shape, 0)
    query_at = lax.broadcasted_iota(jnp.int32, scores.shape, 1) % rows
    return scores, key_at <= query_at


def self_forward_kernel(q_ref, kv_ref, bias_ref, o_ref, lse_ref):
    lanes = lax.broadcasted_iota(jnp.int32, (1, GROUP), 1)
    outs = []
    for pair in range(2):
        query = stacked(q_ref[...], pair, lanes)
        scores, seen = self_scores(kv_ref, query, bias_ref, pair)
        scores = jnp.where(seen, scores, MASKED)
        best = jnp.max(scores, axis=0, keepdims=True)
        part = jnp.exp(scores - best)
        total = jnp.sum(part, axis=0, keepdims=True)
        mixed = t_dot(kv_ref[:, GROUP : 2 * GROUP], low(part / total))
        outs.append(mixed.T)
        lse_ref[0, pair : pair + 1, :] = best + jnp.log(total)
    o_ref[...] = low(unstacked(outs))


def self_backward_kernel(
    q_ref, do_ref, o_ref, kv_ref, lse_ref, bias_ref, dq_ref, dkv_ref, ds_ref
):
    lanes = lax.broadcasted_iota(jnp.int32, (1, GROUP), 1)
    dqs = []
    dk = 0.0
    dv = 0.0
    for pair in range(2):
        query = stacked(q_ref[...], pair, lanes)
        dout = stacked(do_ref[...], pair, lanes)
        inner = inner_of(dout, stacked(o_ref[...], pair, lanes))
        scores, seen = self_scores(kv_ref, query, bias_ref, pair)
        prob = jnp.exp(jnp.where(seen, scores - lse_ref[0, pair : pair + 1, :], MASKED))
        grad = low(prob * (dot_t(kv_ref[:, GROUP : 2 * GROUP], dout) - inner))
        ds_ref[2 * pair] = grad[:, 0:GROUP]
        ds_ref[2 * pair + 1] = grad[:, GROUP : 2 * GROUP]
        dk = dk + dot(grad, query)
        dv = dv + dot(low(prob), dout)
        dqs.append((t_dot(kv_ref[:, 0:GROUP], grad) * DH ** (-0.5)).T)
    dkv_ref[:, 0:GROUP] = low(dk)
    dkv_ref[:, GROUP : 2 * GROUP] = low(dv)
    dq_ref[...] = low(unstacked(dqs))


def attention_specs(rows, span):
    narrow = pl.BlockSpec((rows, 2 * GROUP), lambda k: (0, k))
    tall = pl.BlockSpec((span, 2 * GROUP), lambda k: (0, k))
    lse = pl.BlockSpec((1, 2, 2 * GROUP), lambda k: (k, 0, 0))
    square = pl.BlockSpec((4, rows, rows), lambda k: (k, 0, 0))
    return narrow, tall, lse, square


def kernel_call(kernel, name, blocks, specs, outs, scratch, cost, arguments, limit=32):
    return pl.pallas_call(
        kernel,
        grid=(blocks,),
        in_specs=specs,
        out_specs=[spec for spec, _, _ in outs],
        out_shape=[jax.ShapeDtypeStruct(shape, kind) for _, shape, kind in outs],
        scratch_shapes=scratch,
        compiler_params=pltpu.CompilerParams(vmem_limit_bytes=limit * 2**20),
        cost_estimate=pl.CostEstimate(flops=cost[0], bytes_accessed=cost[1], transcendentals=cost[2]),
        name=name,
    )(*arguments)


def attention_forward(query, pairs, bias):
    rows, span = query.shape[0], pairs.shape[0]
    blocks = query.shape[1] // (2 * GROUP)
    narrow, tall, lse, square = attention_specs(rows, span)
    cost = (
        16 * rows * span * DH * blocks,
        2 * (2 * query.size + pairs.size),
        4 * rows * span * blocks,
    )
    outs = [
        (narrow, query.shape, jnp.bfloat16),
        (lse, (blocks, 2, 2 * GROUP), jnp.float32),
    ]
    if bias is not None:
        return kernel_call(
            self_forward_kernel,
            "self_forward",
            blocks,
            [narrow, tall, square],
            outs,
            [],
            cost,
            (query, pairs, bias),
        )
    return kernel_call(
        cross_forward_kernel,
        "cross_forward",
        blocks,
        [narrow, tall],
        outs,
        [pltpu.VMEM((span, 4 * GROUP), jnp.float32)],
        cost,
        (query, pairs),
    )


def attention_backward(query, dout, out, pairs, lse_value, bias):
    rows, span = query.shape[0], pairs.shape[0]
    blocks = query.shape[1] // (2 * GROUP)
    narrow, tall, lse, square = attention_specs(rows, span)
    cost = (
        40 * rows * span * DH * blocks,
        2 * (4 * query.size + 2 * pairs.size),
        4 * rows * span * blocks,
    )
    outs = [(narrow, query.shape, jnp.bfloat16), (tall, pairs.shape, jnp.bfloat16)]
    if bias is not None:
        return kernel_call(
            self_backward_kernel,
            "self_backward",
            blocks,
            [narrow, narrow, narrow, tall, lse, square],
            outs + [(square, (4 * blocks, rows, rows), jnp.bfloat16)],
            [],
            cost,
            (query, dout, out, pairs, lse_value, bias),
        )
    return kernel_call(
        cross_backward_kernel,
        "cross_backward",
        blocks,
        [narrow, narrow, narrow, tall, lse],
        outs,
        [],
        cost,
        (query, dout, out, pairs, lse_value),
    )


def with_index(kernel, name, grid, specs, outs, scratch, cost, index, arguments, limit=32):
    return pl.pallas_call(
        kernel,
        grid_spec=pltpu.PrefetchScalarGridSpec(
            num_scalar_prefetch=1,
            grid=grid,
            in_specs=specs,
            out_specs=[spec for spec, _, _ in outs],
            scratch_shapes=scratch,
        ),
        out_shape=[jax.ShapeDtypeStruct(shape, kind) for _, shape, kind in outs],
        compiler_params=pltpu.CompilerParams(vmem_limit_bytes=limit * 2**20),
        cost_estimate=pl.CostEstimate(flops=cost[0], bytes_accessed=cost[1], transcendentals=0),
        name=name,
    )(index, *arguments)


def pack_shards(tp, cross_kv, self_q, self_kv, small, self_out, cross_q, cross_out):
    groups = [[cross_kv, self_q, self_kv, small], [self_out, cross_q, cross_out]]
    depths = [sum(part.size // GROUP for part in parts) for parts in groups]
    arguments = [part for parts in groups for part in parts]

    def kernel(*refs):
        ins, (near, *packs) = refs[: len(arguments)], refs[len(arguments) :]
        taken = 0
        above = 0
        for parts, pack, depth in zip(groups, packs, depths):
            at = 0
            for part in parts:
                rows = part.shape[0]
                for b in range(part.size // GROUP // rows):
                    if part.ndim == 3:
                        pack[at : at + rows, :] = ins[taken][:, b, :]
                    else:
                        pack[at : at + rows, :] = ins[taken][:, b * GROUP : (b + 1) * GROUP]
                    at += rows
                taken += 1
            for k in range(tp):
                near[k, above : above + depth, :] = pack[...]
            above += depth

    shapes = [(tp, depths[0] + depths[1], GROUP)] + [(depth, GROUP) for depth in depths]
    whole = [
        pl.BlockSpec(shape, lambda k, nothing=(0,) * len(shape): nothing) for shape in shapes
    ]
    return kernel_call(
        kernel,
        "pack_shards",
        1,
        [pl.BlockSpec(part.shape, lambda k, at=(0,) * part.ndim: at) for part in arguments],
        [(spec, shape, jnp.bfloat16) for spec, shape in zip(whole, shapes)],
        [],
        (0, 4 * sum(depths) * GROUP, 0),
        tuple(arguments),
        limit=56,
    )


def unpack_heads(index, near, far, depth, top, rows_first, width, extra):
    tp = near[0].shape[0]
    listed = isinstance(far[0], list)
    seq = (far[0][0].shape[0] if listed else far[0].shape[1]) + 1
    shard = width // (2 * seq)
    sides = tuple(far[0]) + tuple(far[1]) if listed else tuple(far)

    def kernel(index_ref, *refs):
        near_refs, far_refs = refs[0:2], refs[2 : 2 + len(sides)]
        outs = refs[2 + len(sides) :]

        def place(q, side, read):
            row = 2 * (index_ref[0] ^ q) + (index_ref[2] ^ side)
            at = pl.ds(pl.multiple_of(row * shard, shard), shard)
            for entry, (out, down) in enumerate(zip(outs, rows_first)):
                start = entry * 2 * shard
                if down:
                    out[:, at] = read(start, 2 * shard)
                else:
                    for b in range(2):
                        out[at, b * GROUP : (b + 1) * GROUP] = read(start + b * shard, shard)
            if extra:
                outs[-1][0, row] = read(depth - extra, extra)

        for side in range(2):
            place(0, side, lambda start, size: near_refs[side][0, top + start : top + start + size, :])
            for q in range(1, seq):
                if listed:
                    for k in range(tp):

                        @pl.when(pl.program_id(0) == k)
                        def _():
                            ref = far_refs[side * tp + k]
                            place(q, side, lambda start, size: ref[q - 1, start : start + size, :])

                else:
                    place(
                        q,
                        side,
                        lambda start, size: far_refs[side][0, q - 1, start : start + size, :],
                    )

    specs = [pl.BlockSpec((1,) + near[0].shape[1:], lambda k, index: (k ^ index[1], 0, 0))] * 2
    for value in sides:
        if listed:
            specs.append(pl.BlockSpec(value.shape, lambda k, index: (0, 0, 0)))
        else:
            specs.append(
                pl.BlockSpec((1,) + value.shape[1:], lambda k, index: (k ^ index[1], 0, 0, 0))
            )
    outs = []
    for down in rows_first:
        if down:
            spec = pl.BlockSpec((2 * GROUP, width), lambda k, index: (k, 0))
            outs.append((spec, (tp * 2 * GROUP, width), jnp.bfloat16))
        else:
            spec = pl.BlockSpec((width, 2 * GROUP), lambda k, index: (0, k))
            outs.append((spec, (width, tp * 2 * GROUP), jnp.bfloat16))
    if extra:
        spec = pl.BlockSpec((1, 2 * seq, extra, GROUP), lambda k, index: (k, 0, 0, 0))
        outs.append((spec, (tp, 2 * seq, extra, GROUP), jnp.bfloat16))
    return with_index(
        kernel,
        "unpack_heads",
        (tp,),
        specs,
        outs,
        [],
        (0, 8 * tp * seq * depth * GROUP),
        index,
        (*near, *sides),
    )


def unpack_hidden(value, width, hidden_width):
    count = value.shape[0]
    shard = width // count
    columns = 2 * hidden_width // GROUP

    def kernel(in_ref, gate_up_ref, down_ref):
        for b in range(columns):
            gate_up_ref[:, b * GROUP : (b + 1) * GROUP] = in_ref[0, b * shard : (b + 1) * shard, :]
        down_ref[...] = in_ref[0, columns * shard :, :]

    return kernel_call(
        kernel,
        "unpack_hidden",
        count,
        [pl.BlockSpec((1, value.shape[1], GROUP), lambda k: (k, 0, 0))],
        [
            (
                pl.BlockSpec((shard, 2 * hidden_width), lambda k: (k, 0)),
                (width, 2 * hidden_width),
                jnp.bfloat16,
            ),
            (
                pl.BlockSpec((hidden_width, shard), lambda k: (0, k)),
                (hidden_width, width),
                jnp.bfloat16,
            ),
        ],
        [],
        (0, 4 * value.size, 0),
        (value,),
    )


def memory_terms(index, seq, memory, pairs, weight, tp):
    rows, width = pairs.shape
    shard = width // (2 * seq)
    features = weight.shape[0] // tp
    steps = 2 * seq
    block = rows // steps
    early = max(steps // 4, 1)

    def row_of(step, index):
        return 2 * (index[0] ^ (step % seq)) + (index[2] ^ (1 - step // seq))

    def kernel(index_ref, memory_ref, pairs_ref, weight_ref, sent_ref, kept_ref, *outs):
        step = pl.program_id(0)
        part = t_dot(memory_ref[0], pairs_ref[...])

        @pl.when(step < seq)
        def _():
            sent_ref[0] = low(part)

        @pl.when(step >= seq)
        def _():
            kept_ref[0] = part

        values = pairs_ref[pl.ds(pl.multiple_of(step * block, block), block), :]
        for k in range(tp):
            at = pl.multiple_of((index_ref[1] ^ k) * features, features)
            outs[tp + k][...] = low(dot_t(values, weight_ref[pl.ds(at, features), :]))

        @pl.when(step < early)
        def _():
            for k in range(tp):
                outs[k][...] = outs[tp + k][...]

    shape = (seq, shard, width)
    first = pl.BlockSpec((block, features), lambda s, index: (jnp.minimum(s, early - 1), 0))
    second = pl.BlockSpec((block, features), lambda s, index: (jnp.maximum(s - early, 0), 0))
    return with_index(
        kernel,
        "memory_terms",
        (steps,),
        [
            pl.BlockSpec((1, rows, shard), lambda s, index: (index[1], 0, row_of(s, index))),
            pl.BlockSpec(pairs.shape, lambda s, index: (0, 0)),
            pl.BlockSpec(weight.shape, lambda s, index: (0, 0)),
        ],
        [
            (
                pl.BlockSpec((1, shard, width), lambda s, index: (jnp.minimum(s, seq - 1), 0, 0)),
                shape,
                jnp.bfloat16,
            ),
            (
                pl.BlockSpec((1, shard, width), lambda s, index: (jnp.maximum(s - seq, 0), 0, 0)),
                shape,
                jnp.float32,
            ),
        ]
        + [(first, (early * block, features), jnp.bfloat16)] * tp
        + [(second, (rows - early * block, features), jnp.bfloat16)] * tp,
        [],
        (4 * rows * width * width, 6 * pairs.size),
        index,
        (memory, pairs, weight),
    )


def hidden_out(index, hidden, weight, values, tp):
    rows = hidden.shape[0] // tp
    width = weight.shape[1]

    def kernel(index_ref, hidden_ref, weight_ref, values_ref, out_ref):
        part = dot(hidden_ref[...], weight_ref[...])

        @pl.when(pl.program_id(0) == 0)
        def _():
            out_ref[0] = low(part + values_ref[...])

        @pl.when(pl.program_id(0) != 0)
        def _():
            out_ref[0] = low(part)

    return with_index(
        kernel,
        "hidden_out",
        (tp,),
        [
            pl.BlockSpec((rows, hidden.shape[1]), lambda k, index: (k, 0)),
            pl.BlockSpec(weight.shape, lambda k, index: (0, 0)),
            pl.BlockSpec(values.shape, lambda k, index: (0, 0)),
        ],
        [
            (
                pl.BlockSpec((1, rows, width), lambda k, index: (k ^ index[1], 0, 0)),
                (tp, rows, width),
                jnp.bfloat16,
            )
        ],
        [],
        (2 * hidden.size * width, 2 * (hidden.size + weight.size + tp * rows * width)),
        index,
        (hidden, weight, values),
    )[0]


def row_terms(index, seq, name, pairs):
    width = pairs[0][0][0].shape[-1] if isinstance(pairs[0][0], list) else pairs[0][0].shape[-1]
    shard = width // (2 * seq)
    columns = sum(right[0][2] - right[0][1] for _, right in pairs)

    def row_of(step, index):
        return 2 * (index[0] ^ (step % seq)) + (index[2] ^ (1 - step // seq))

    def kernel(index_ref, *refs):
        sent_ref, kept_ref = refs[-2:]
        parts = []
        at = 0
        for left, right in pairs:
            if isinstance(left, list):
                value = jnp.concatenate([ref[...] for ref in refs[at : at + len(left)]], axis=0)
                at += len(left)
            else:
                value = refs[at][0]
                at += 1
            other = [ref[:, low_at:high_at] for ref, (_, low_at, high_at) in zip(refs[at:], right)]
            at += len(right)
            parts.append(t_dot(value, jnp.concatenate(other, axis=0)))

        def put(ref, kind):
            at = 0
            for part in parts:
                ref[0, :, at : at + part.shape[1]] = part.astype(kind)
                at += part.shape[1]

        @pl.when(pl.program_id(0) < seq)
        def _():
            put(sent_ref, jnp.bfloat16)

        @pl.when(pl.program_id(0) >= seq)
        def _():
            put(kept_ref, jnp.float32)

    specs = []
    arguments = []
    depth = 0
    for left, right in pairs:
        if isinstance(left, list):
            for part in left:
                rows = part.shape[0]
                specs.append(pl.BlockSpec((rows, shard), lambda s, index: (0, row_of(s, index))))
                arguments.append(part)
        else:
            specs.append(
                pl.BlockSpec(
                    (1, left.shape[1], shard), lambda s, index: (index[1], 0, row_of(s, index))
                )
            )
            arguments.append(left)
        for part, _, _ in right:
            specs.append(pl.BlockSpec(part.shape, lambda s, index: (0, 0)))
            arguments.append(part)
        depth = max(depth, sum(part.shape[0] for part, _, _ in right))
    shape = (seq, shard, columns)
    block = (1, shard, columns)
    return with_index(
        kernel,
        name,
        (2 * seq,),
        specs,
        [
            (
                pl.BlockSpec(block, lambda s, index: (jnp.minimum(s, seq - 1), 0, 0)),
                shape,
                jnp.bfloat16,
            ),
            (
                pl.BlockSpec(block, lambda s, index: (jnp.maximum(s - seq, 0), 0, 0)),
                shape,
                jnp.float32,
            ),
        ],
        [],
        (2 * depth * width * columns, 2 * depth * (width + columns) + 3 * width * columns),
        index,
        tuple(arguments),
        limit=56,
    )


def hidden_terms(normed, grad_joined, rounded, hidden):
    rows, width = normed.shape
    columns = grad_joined.shape[1] + hidden.shape[1]
    split = grad_joined.shape[1]
    steps = width // GROUP

    def kernel(normed_ref, joined_ref, rounded_ref, hidden_ref, out_ref):
        out_ref[:, :split] = low(t_dot(normed_ref[...], joined_ref[...]))
        out_ref[:, split:] = low(t_dot(rounded_ref[...], hidden_ref[...]))

    left = pl.BlockSpec((rows, GROUP), lambda k: (0, k))
    return kernel_call(
        kernel,
        "hidden_terms",
        steps,
        [
            left,
            pl.BlockSpec(grad_joined.shape, lambda k: (0, 0)),
            left,
            pl.BlockSpec(hidden.shape, lambda k: (0, 0)),
        ],
        [(pl.BlockSpec((GROUP, columns), lambda k: (k, 0)), (width, columns), jnp.bfloat16)],
        [],
        (2 * rows * width * columns, 4 * rows * (width + columns) + 2 * width * columns, 0),
        (normed, grad_joined, rounded, hidden),
    )[0]


def one_each(seq, tp):
    everyone = ("seq", "tp", "fsdp")

    def after(value, *earlier):
        return lax.optimization_barrier((value, earlier))[0]

    def together(*values):
        return lax.optimization_barrier(values)

    def swap(value, axis, flip):
        size = {"seq": seq, "tp": tp, "fsdp": 2}[axis]
        return lax.ppermute(value, axis, [(place, place ^ flip) for place in range(size)])

    def gather(value, axis, size):
        return [value] + [swap(value, axis, flip) for flip in range(1, size)]

    def exchange(parts, axis):
        return [parts[0]] + [swap(parts[k], axis, k) for k in range(1, len(parts))]

    def exchange_all(value):
        return lax.all_to_all(value, "tp", 0, 0, tiled=True)

    def to_everyone(value):
        return exchange_all(jnp.broadcast_to(value[None], (tp,) + value.shape))

    def total(parts):
        result = high(parts[0])
        for part in parts[1:]:
            result = result + high(part)
        return result

    def run(
        decoder_in,
        memory,
        buckets,
        norm_gains,
        rel_bias,
        self_q,
        self_kv,
        self_out,
        cross_q,
        cross_kv,
        cross_out,
        gate_up,
        down,
        cotangent,
    ):
        count, rows, width = decoder_in.shape
        z = lax.axis_index("seq")
        t = lax.axis_index("tp")
        c = lax.axis_index("fsdp")
        index = jnp.stack([z, t, c]).astype(jnp.int32)
        cores = 2
        shard = self_q.shape[0]
        tables = rel_bias.shape[0]
        heads = rel_bias.shape[1]
        hidden_width = down.shape[0]
        extra = 16

        def own(value):
            return lax.dynamic_index_in_dim(value, t, 0, keepdims=False)

        def from_here(value):
            return [
                lax.dynamic_index_in_dim(value, t ^ k, 0, keepdims=False) for k in range(tp)
            ]

        def in_order(parts, kind):
            result = jnp.zeros((count,) + parts[0].shape, kind)
            for k, part in enumerate(parts):
                result = lax.dynamic_update_index_in_dim(result, part.astype(kind), t ^ k, 0)
            return result

        def head_blocks(value):
            size = value.shape[1] // tp
            return [value[:, k * size : (k + 1) * size] for k in range(tp)]

        small = jnp.concatenate(
            [
                norm_gains,
                jnp.pad(rel_bias.reshape(1, -1), ((0, 0), (0, GROUP - rel_bias.size))),
                jnp.zeros((extra - 4, GROUP), jnp.bfloat16),
            ],
            axis=0,
        )
        near, pack_a, pack_b = pack_shards(
            tp, cross_kv, self_q, self_kv, small, self_out, cross_q, cross_out
        )
        gate_up, down = after((gate_up, down), near)
        pack_f = jnp.concatenate([lane_blocks(flatten(gate_up)), down], axis=0)

        depth_a, depth_b = pack_a.shape[0], pack_b.shape[0]
        near = exchange_all(near)
        ring_a = gather(pack_a, "seq", seq)
        onehot = (
            buckets.T[:, :, None] == jnp.arange(NB, dtype=jnp.int32)[None, None, :]
        ).astype(jnp.bfloat16)
        start = high(own(decoder_in))
        unit_self = start * lax.rsqrt(jnp.mean(start * start, axis=-1, keepdims=True) + EPSILON)
        pack_b, onehot, unit_self = together(pack_b, onehot, unit_self)
        ring_b = gather(after(pack_b, *ring_a), "seq", seq)
        far_a = to_everyone(after(jnp.stack(ring_a[1:]), near))
        far_b = after(jnp.stack(ring_b[1:]), far_a)
        decoder_in, cotangent = after((decoder_in, cotangent), far_b)
        far_b = gather(far_b, "tp", tp)
        full_f = lax.all_gather(after(pack_f, *ring_b), ("seq", "fsdp"), axis=0, tiled=True)
        near = [near, swap(near, "fsdp", 1)]
        far_a = [far_a, swap(far_a, "fsdp", 1)]

        cross_pairs, weight_self_q, weight_self_kv, smalls = unpack_heads(
            index, near, far_a, depth_a, 0, (False, False, False), width, extra
        )
        weight_gate_up, weight_down = unpack_hidden(
            full_f.reshape(seq * cores, -1, GROUP), width, hidden_width
        )
        gain_rows = high(smalls[0, :, 0:3].transpose(1, 0, 2).reshape(3, width))
        table = smalls[:, :, 3, 0 : tables * heads].reshape(tp, seq * cores, tables, heads)
        table = table.transpose(1, 2, 0, 3).reshape(NB, tp * heads)
        bias = jnp.einsum("jin,nh->hji", onehot, table, preferred_element_type=jnp.float32)

        pairs = low(dot(own(memory), cross_pairs))
        scale = DH ** (-0.5)

        normed_self = low(unit_self * gain_rows[0])
        query_self = low(dot(normed_self, weight_self_q) * scale)
        pair_self = low(dot(normed_self, weight_self_kv))
        mixed_self, log_self = attention_forward(query_self, pair_self, bias)
        far_b = [after(part, mixed_self, pairs) for part in far_b]
        far_b = [far_b, [swap(part, "fsdp", 1) for part in far_b]]
        weight_self_out, weight_cross_q, weight_cross_out = unpack_heads(
            index, near, far_b, depth_b, depth_a, (True, False, True), width, 0
        )
        after_self = start + dot(mixed_self, weight_self_out)

        normed_cross = low(rms_norm(after_self, gain_rows[1]))
        query_cross = low(dot(normed_cross, weight_cross_q) * scale)
        mixed_cross, log_cross = attention_forward(query_cross, pairs, None)
        after_cross = after_self + dot(mixed_cross, weight_cross_out)
        normed_ffn = low(rms_norm(after_cross, gain_rows[2]))

        all_cross = lax.all_gather(normed_cross, "tp", axis=0, tiled=True)
        normed_parts, weight_gate_up, weight_down, own_cotangent, rounded = together(
            gather(normed_ffn, "tp", tp),
            weight_gate_up,
            weight_down,
            own(cotangent),
            jnp.concatenate(from_here(cotangent), axis=0),
        )
        all_normed = jnp.concatenate(normed_parts, axis=0)
        joined = dot(all_normed, weight_gate_up)
        gate = joined[:, :hidden_width]
        up = joined[:, hidden_width:]
        grad_hidden = dot_t(rounded, weight_down)
        hidden = low(gelu_product(gate, up))
        _, pull = jax.vjp(gelu_product, gate, up)
        grad_gate, grad_up = pull(grad_hidden)
        grad_joined = low(jnp.concatenate([grad_gate, grad_up], axis=-1))

        def row_parts(value):
            return [value[k * rows : (k + 1) * rows] for k in range(tp)]

        partial_normed = row_parts(low(dot_t(grad_joined, weight_gate_up)))
        grad_parts = exchange(partial_normed, "tp")
        all_normed, grad_joined, rounded, hidden, o_self, o_cross = after(
            (all_normed, grad_joined, rounded, hidden, mixed_self, mixed_cross), partial_normed
        )
        hidden_grads = hidden_terms(all_normed, grad_joined, rounded, hidden)
        o_blocks = [
            jnp.concatenate(blocks, axis=1)
            for blocks in zip(head_blocks(o_self), head_blocks(o_cross))
        ]
        grad_parts, hidden_grads, o_blocks = together(grad_parts, hidden_grads, o_blocks)
        hidden_grads = high(
            lax.psum_scatter(hidden_grads, ("seq", "fsdp"), scatter_dimension=0, tiled=True)
        )

        grad_normed = total(grad_parts)
        grad_residual, gain_ffn = norm_backward(after_cross, gain_rows[2], grad_normed)
        grad_cross = high(own_cotangent) + grad_residual
        rounded_cross = low(grad_cross)
        cross_operands = [jnp.concatenate([rounded_cross, block], axis=1) for block in o_blocks]
        cross_parts = exchange(cross_operands, "tp")
        grad_mixed = low(dot_t(after(rounded_cross, cross_operands), weight_cross_out))
        grad_query, grad_pairs = attention_backward(
            query_cross, grad_mixed, mixed_cross, pairs, log_cross, None
        )
        cross_parts, grad_query, grad_pairs = together(cross_parts, grad_query, grad_pairs)
        grad_normed = dot_t(grad_query, weight_cross_q)
        grad_residual, gain_cross = norm_backward(after_self, gain_rows[1], grad_normed)
        grad_self = grad_cross + grad_residual
        rounded_self = low(grad_self)
        self_operands = [
            jnp.concatenate([rounded_self, block], axis=1) for block in head_blocks(grad_query)
        ]
        self_parts = exchange(self_operands, "tp")

        grad_mixed_self = low(dot_t(after(rounded_self, self_operands), weight_self_out))
        grad_query_self, grad_pair_self, grad_scores = attention_backward(
            query_self, grad_mixed_self, mixed_self, pair_self, log_self, bias
        )
        grad_normed = dot_t(grad_query_self, weight_self_q) + dot_t(grad_pair_self, weight_self_kv)
        grad_residual, gain_self = norm_backward(start, gain_rows[0], grad_normed)
        grad_tokens = low(grad_self + grad_residual)
        last_operands = [
            jnp.concatenate([grad_tokens, q_block, kv_block], axis=1)
            for q_block, kv_block in zip(head_blocks(grad_query_self), head_blocks(grad_pair_self))
        ]
        partial_out = hidden_out(
            index, after(hidden, last_operands), weight_down, after_cross, tp
        )
        partial_out, self_parts, last_operands, memory_pairs, decoder_in, gains, grad_scores = together(
            partial_out,
            self_parts,
            last_operands,
            grad_pairs,
            decoder_in,
            (gain_self, gain_cross, gain_ffn),
            grad_scores,
        )
        last_parts = exchange(last_operands, "tp")

        kv_sent, kv_rows, *memory_parts = memory_terms(
            index, seq, memory, memory_pairs, cross_pairs, tp
        )
        decoder_out = lax.psum(partial_out, "tp")
        last_parts, kv_sent, kv_rows, memory_parts, gains, grad_scores, all_cross = (
            together(
                last_parts,
                kv_sent,
                kv_rows,
                memory_parts,
                gains,
                grad_scores,
                all_cross,
            )
        )
        first_parts = exchange(memory_parts[:tp], "tp")
        kv_rows = kv_rows + high(swap(kv_sent, "fsdp", 1))

        def span_of(parts, first, last):
            return [(part, first, last) for part in parts]

        all_start = [
            low(rms_norm(high(part), gain_rows[0])) for part in from_here(decoder_in)
        ]
        both_sent, both_kept = row_terms(
            index,
            seq,
            "head_weights",
            [
                (
                    from_here(all_cross.reshape(tp, rows, width)),
                    span_of(self_parts, width, width + 2 * GROUP),
                ),
                (cross_parts, span_of(cross_parts, width + 2 * GROUP, width + 4 * GROUP)),
                (all_start, span_of(last_parts, width, width + 4 * GROUP)),
                (self_parts, span_of(cross_parts, width, width + 2 * GROUP)),
            ],
        )
        kv_far = low(kv_rows[seq // 2 :])
        first_parts, kv_far, kv_rows, both_sent, both_kept, second_parts = together(
            first_parts, kv_far, kv_rows, both_sent, both_kept, memory_parts[tp:]
        )
        kv_far = swap(kv_far, "seq", seq // 2)
        second_parts = exchange(second_parts, "tp")
        both_grads = low(both_kept + high(swap(both_sent, "fsdp", 1)))
        both_grads = jnp.concatenate(
            [
                lax.dynamic_index_in_dim(both_grads, z ^ k, 0, keepdims=True) for k in range(seq)
            ],
            axis=0,
        )
        gains, grad_scores, last_parts, hidden_grads = after(
            (gains, grad_scores, last_parts, hidden_grads), both_sent
        )
        gate_up_grad = hidden_grads[:, : 2 * hidden_width].reshape(gate_up.shape)
        down_grad = hidden_grads[:, 2 * hidden_width :].T
        decoder_grad = in_order([part[:, :width] for part in last_parts], jnp.float32)
        cut = first_parts[0].shape[0]
        memory_grad = jnp.zeros((count, memory.shape[1], first_parts[0].shape[1]), jnp.bfloat16)
        for k in range(tp):
            memory_grad = lax.dynamic_update_slice(
                memory_grad, first_parts[k][None], (t ^ k, 0, 0)
            )
        table_grad = jnp.einsum(
            "jin,hji->nh", onehot, grad_scores, preferred_element_type=jnp.float32
        )
        gain_parts = jnp.stack([gain.reshape(-1, GROUP) for gain in gains], axis=1)
        table_parts = jnp.pad(
            table_grad.reshape(seq * cores, 1, -1),
            ((0, 0), (0, 0), (0, GROUP - tables * tp * heads)),
        )
        little = low(jnp.concatenate([gain_parts, table_parts], axis=1))
        little = jnp.broadcast_to(
            little.reshape(seq, 1, cores, 4, GROUP), (seq, tp, cores, 4, GROUP)
        )
        both_grads, kv_far, little, gate_up_grad, down_grad, decoder_grad, memory_grad = together(
            both_grads, kv_far, little, gate_up_grad, down_grad, decoder_grad, memory_grad
        )
        both_grads = lax.all_to_all(both_grads, "seq", 0, 0, tiled=True)
        kv_rows = kv_rows[: seq // 2] + high(kv_far)
        step = seq // 4
        while step:
            kv_rows = kv_rows[:step] + high(swap(low(kv_rows[step:]), "seq", step))
            step //= 2
        kv_rows = kv_rows[0]
        for k in range(tp):
            memory_grad = lax.dynamic_update_slice(
                memory_grad, second_parts[k][None], (t ^ k, cut, 0)
            )
        both_grads, little, kv_rows, memory_grad = together(
            both_grads, little, kv_rows, memory_grad
        )
        cross_kv_grad = total(
            exchange([kv_rows[:, : 2 * GROUP]] + head_blocks(low(kv_rows))[1:], "tp")
        )
        little = lax.all_to_all(little.reshape(-1, 4, GROUP), everyone, 0, 0, tiled=True)
        little = jnp.sum(high(little).reshape(seq, tp, cores, 4, GROUP), axis=(0, 2))
        sender = jnp.arange(tp, dtype=jnp.int32)
        chosen = (sender[:, None] ^ sender[None, :]) == t
        table_sum = little[:, 3, : tables * tp * heads].reshape(tp, tables, tp, heads)
        table_sum = jnp.sum(jnp.where(chosen[:, None, :, None], table_sum, 0.0), axis=(0, 2))
        little = jnp.sum(little, axis=0)
        both_grads = jnp.sum(high(both_grads), axis=0)
        cross_grads = both_grads[:, : 4 * GROUP]
        self_grads = both_grads[:, 4 * GROUP :]

        return (
            decoder_out,
            decoder_grad,
            memory_grad,
            little[0:3],
            table_sum,
            self_grads[:, 0 : 2 * GROUP],
            self_grads[:, 2 * GROUP : 4 * GROUP].reshape(self_kv.shape),
            self_grads[:, 4 * GROUP :].T,
            cross_grads[:, 0 : 2 * GROUP],
            cross_kv_grad.reshape(cross_kv.shape),
            cross_grads[:, 2 * GROUP :].T,
            gate_up_grad,
            down_grad,
        )

    return run


def plan_of(mesh):
    seq, tp, cores = (mesh.shape[axis] for axis in ("seq", "tp", "fsdp"))

    def chosen(*arrays):
        count, rows, width = arrays[0].shape
        fits = (
            cores == 2
            and seq & (seq - 1) == 0
            and tp & (tp - 1) == 0
            and count == tp
            and rows == GROUP
            and arrays[1].shape[1] % 512 == 0
            and width == 2 * seq * GROUP
            and arrays[5].shape[1] == 4 * DH
            and arrays[6].shape[2] == 2 * DH
            and tp * arrays[4].size <= GROUP
            and 2 * arrays[12].shape[0] % GROUP == 0
        )
        return (one_each(seq, tp) if fits else per_device)(*arrays)

    return chosen


def solution(mesh):
    return jax.shard_map(
        plan_of(mesh),
        mesh=mesh,
        in_specs=(
            P(("seq", "fsdp"), None, None),
            P(("seq", "fsdp"), None, None),
            P(),
            P(None, ("seq", "fsdp")),
            P(("seq", "fsdp"), "tp"),
            P(("seq", "fsdp"), "tp"),
            P(("seq", "fsdp"), None, "tp"),
            P("tp", ("seq", "fsdp")),
            P(("seq", "fsdp"), "tp"),
            P(("seq", "fsdp"), None, "tp"),
            P("tp", ("seq", "fsdp")),
            P(("seq", "fsdp"), None, "tp"),
            P("tp", ("seq", "fsdp")),
            P(("seq", "fsdp"), None, None),
        ),
        out_specs=(
            P(("seq", "fsdp"), None, None),
            P(("seq", "fsdp"), None, None),
            P(("seq", "fsdp"), None, "tp"),
            P(None, ("seq", "fsdp")),
            P(("seq", "fsdp"), "tp"),
            P(("seq", "fsdp"), "tp"),
            P(("seq", "fsdp"), None, "tp"),
            P("tp", ("seq", "fsdp")),
            P(("seq", "fsdp"), "tp"),
            P(("seq", "fsdp"), None, "tp"),
            P("tp", ("seq", "fsdp")),
            P(("seq", "fsdp"), None, "tp"),
            P("tp", ("seq", "fsdp")),
        ),
        check_vma=False,
    )
```

```python
import jax
import jax.numpy as jnp
from jax import lax
from jax.experimental import pallas as pl
from jax.experimental.pallas import tpu as pltpu
from jax.sharding import PartitionSpec as P

DH = 64
NB = 32
MICRO = 2


EPSILON = 1e-06
MASKED = -1e30


def rms_norm(values, gain):
    return values * lax.rsqrt(jnp.mean(values * values, axis=-1, keepdims=True) + EPSILON) * gain


def gelu_product(gate, up):
    return jax.nn.gelu(gate, approximate=True) * up


def flatten(weight):
    return weight.reshape(weight.shape[0], -1)


def gather_weights(
    gains, table, self_q, self_kv, self_out, cross_q, cross_kv, cross_out, gate_up, down
):
    return (
        lax.all_gather(gains, ("seq", "fsdp"), axis=1, tiled=True),
        lax.all_gather(table, ("seq", "fsdp"), axis=0, tiled=True),
        lax.all_gather(self_q, ("seq", "fsdp"), axis=0, tiled=True),
        lax.all_gather(self_kv, ("seq", "fsdp"), axis=0, tiled=True),
        lax.all_gather(self_out, ("seq", "fsdp"), axis=1, tiled=True),
        lax.all_gather(cross_q, ("seq", "fsdp"), axis=0, tiled=True),
        lax.all_gather(cross_kv, ("seq", "fsdp"), axis=0, tiled=True),
        lax.all_gather(cross_out, ("seq", "fsdp"), axis=1, tiled=True),
        lax.all_gather(gate_up, ("seq", "fsdp"), axis=0, tiled=True),
        lax.all_gather(down, ("seq", "fsdp"), axis=1, tiled=True),
    )


def branch_total(partial_value):
    return lax.psum(partial_value.astype(jnp.bfloat16), "tp").astype(jnp.float32)


def input_total(partial_value):
    return lax.psum(partial_value.astype(jnp.bfloat16), "tp").astype(jnp.float32)


def split_heads(query, keys, values):
    batch, rows, width = query.shape
    span = keys.shape[1]
    groups = keys.shape[2] // DH
    ratio = width // DH // groups
    return (
        query.reshape(batch, rows, groups, ratio, DH),
        keys.reshape(batch, span, groups, DH),
        values.reshape(batch, span, groups, DH),
    )


def scores_of(query_heads, key_heads, bias, causal):
    scores = jnp.einsum(
        "bigrd,bjgd->bgrij", query_heads, key_heads, preferred_element_type=jnp.float32
    ) * DH ** (-0.5)
    if bias is not None:
        scores = scores + bias
    if causal is not None:
        scores = jnp.where(causal, scores, MASKED)
    return scores


def attend_forward(query, keys, values, bias, causal):
    query_heads, key_heads, value_heads = split_heads(query, keys, values)
    scores = scores_of(query_heads, key_heads, bias, causal)
    row_max = jnp.max(scores, axis=-1, keepdims=True)
    exponent = jnp.exp(scores - row_max)
    total = jnp.sum(exponent, axis=-1, keepdims=True)
    probs = (exponent / total).astype(jnp.bfloat16)
    mixed = jnp.einsum("bgrij,bjgd->bigrd", probs, value_heads, preferred_element_type=jnp.float32)
    return (mixed.reshape(query.shape).astype(jnp.bfloat16), row_max + jnp.log(total))


def attend_backward(query, keys, values, bias, causal, log_total, grad_mixed):
    query_heads, key_heads, value_heads = split_heads(query, keys, values)
    probs = jnp.exp(scores_of(query_heads, key_heads, bias, causal) - log_total)
    grad_heads = grad_mixed.reshape(query_heads.shape)
    grad_probs = jnp.einsum(
        "bigrd,bjgd->bgrij", grad_heads, value_heads, preferred_element_type=jnp.float32
    )
    inner = jnp.sum(probs * grad_probs, axis=-1, keepdims=True)
    grad_scores = (probs * (grad_probs - inner)).astype(jnp.bfloat16)
    scale = DH ** (-0.5)
    grad_query = (
        jnp.einsum("bgrij,bjgd->bigrd", grad_scores, key_heads, preferred_element_type=jnp.float32)
        * scale
    ).astype(jnp.bfloat16)
    grad_keys = (
        jnp.einsum(
            "bgrij,bigrd->bjgd", grad_scores, query_heads, preferred_element_type=jnp.float32
        )
        * scale
    ).astype(jnp.bfloat16)
    grad_values = jnp.einsum(
        "bgrij,bigrd->bjgd",
        probs.astype(jnp.bfloat16),
        grad_heads,
        preferred_element_type=jnp.float32,
    ).astype(jnp.bfloat16)
    return (
        grad_query.reshape(query.shape),
        grad_keys.reshape(keys.shape),
        grad_values.reshape(values.shape),
        grad_scores,
    )


def forward(tokens, memory, weights, onehot, causal):
    gains, table, self_q, self_kv, self_out, cross_q, cross_kv, cross_out, gate_up, down = weights
    gain_rows = gains.astype(jnp.float32)
    start = tokens.astype(jnp.float32)
    normed_self = rms_norm(start, gain_rows[0]).astype(jnp.bfloat16)
    query_self = jnp.dot(normed_self, self_q, preferred_element_type=jnp.float32).astype(
        jnp.bfloat16
    )
    pair_self = jnp.dot(normed_self, flatten(self_kv), preferred_element_type=jnp.float32).astype(
        jnp.bfloat16
    )
    half = pair_self.shape[-1] // 2
    keys_self = pair_self[..., :half]
    values_self = pair_self[..., half:]
    groups = half // DH
    heads = table.shape[1]
    rows = tokens.shape[1]
    bias = jnp.einsum("ijn,nh->hij", onehot, table, preferred_element_type=jnp.float32).reshape(
        groups, heads // groups, rows, rows
    )
    mixed_self, log_self = attend_forward(query_self, keys_self, values_self, bias, causal)
    after_self = start + branch_total(
        jnp.dot(mixed_self, self_out, preferred_element_type=jnp.float32)
    )
    normed_cross = rms_norm(after_self, gain_rows[1]).astype(jnp.bfloat16)
    query_cross = jnp.dot(normed_cross, cross_q, preferred_element_type=jnp.float32).astype(
        jnp.bfloat16
    )
    pair_cross = jnp.dot(memory, flatten(cross_kv), preferred_element_type=jnp.float32).astype(
        jnp.bfloat16
    )
    keys_cross = pair_cross[..., :half]
    values_cross = pair_cross[..., half:]
    mixed_cross, log_cross = attend_forward(query_cross, keys_cross, values_cross, None, None)
    after_cross = after_self + branch_total(
        jnp.dot(mixed_cross, cross_out, preferred_element_type=jnp.float32)
    )
    normed_ffn = rms_norm(after_cross, gain_rows[2]).astype(jnp.bfloat16)
    joined = jnp.dot(normed_ffn, flatten(gate_up), preferred_element_type=jnp.float32)
    hidden_width = joined.shape[-1] // 2
    gate = joined[..., :hidden_width]
    up = joined[..., hidden_width:]
    hidden = gelu_product(gate, up).astype(jnp.bfloat16)
    output = after_cross + branch_total(jnp.dot(hidden, down, preferred_element_type=jnp.float32))
    saved = (
        start,
        after_self,
        after_cross,
        normed_self,
        query_self,
        keys_self,
        values_self,
        bias,
        mixed_self,
        log_self,
        normed_cross,
        query_cross,
        keys_cross,
        values_cross,
        mixed_cross,
        log_cross,
        normed_ffn,
        gate,
        up,
        hidden,
    )
    return (output, saved)


def backward(saved, grad_out, memory, weights, onehot, causal):
    (
        start,
        after_self,
        after_cross,
        normed_self,
        query_self,
        keys_self,
        values_self,
        bias,
        mixed_self,
        log_self,
        normed_cross,
        query_cross,
        keys_cross,
        values_cross,
        mixed_cross,
        log_cross,
        normed_ffn,
        gate,
        up,
        hidden,
    ) = saved
    gains, table, self_q, self_kv, self_out, cross_q, cross_kv, cross_out, gate_up, down = weights
    gain_rows = gains.astype(jnp.float32)
    grad_ffn = grad_out.astype(jnp.float32)
    rounded = grad_ffn.astype(jnp.bfloat16)
    down_grad = jnp.einsum("blf,bld->fd", hidden, rounded, preferred_element_type=jnp.float32)
    grad_hidden = jnp.einsum("bld,fd->blf", rounded, down, preferred_element_type=jnp.float32)
    _, pull = jax.vjp(gelu_product, gate, up)
    grad_gate, grad_up = pull(grad_hidden)
    grad_joined = jnp.concatenate([grad_gate, grad_up], axis=-1).astype(jnp.bfloat16)
    gate_up_grad = jnp.einsum(
        "bld,blf->df", normed_ffn, grad_joined, preferred_element_type=jnp.float32
    ).reshape(gate_up.shape)
    grad_normed = input_total(
        jnp.einsum("blf,df->bld", grad_joined, flatten(gate_up), preferred_element_type=jnp.float32)
    )
    _, pull = jax.vjp(rms_norm, after_cross, gain_rows[2])
    grad_residual, gain_ffn = pull(grad_normed)
    grad_cross = grad_ffn + grad_residual
    rounded = grad_cross.astype(jnp.bfloat16)
    cross_out_grad = jnp.einsum(
        "blh,bld->hd", mixed_cross, rounded, preferred_element_type=jnp.float32
    )
    grad_mixed = jnp.einsum(
        "bld,hd->blh", rounded, cross_out, preferred_element_type=jnp.float32
    ).astype(jnp.bfloat16)
    grad_query, grad_keys, grad_values, _ = attend_backward(
        query_cross, keys_cross, values_cross, None, None, log_cross, grad_mixed
    )
    grad_pair_cross = jnp.concatenate([grad_keys, grad_values], axis=-1)
    cross_q_grad = jnp.einsum(
        "bld,blh->dh", normed_cross, grad_query, preferred_element_type=jnp.float32
    )
    cross_kv_grad = jnp.einsum(
        "bsd,bsw->dw", memory, grad_pair_cross, preferred_element_type=jnp.float32
    ).reshape(cross_kv.shape)
    grad_normed = input_total(
        jnp.einsum("blh,dh->bld", grad_query, cross_q, preferred_element_type=jnp.float32)
    )
    _, pull = jax.vjp(rms_norm, after_self, gain_rows[1])
    grad_residual, gain_cross = pull(grad_normed)
    grad_self = grad_cross + grad_residual
    rounded = grad_self.astype(jnp.bfloat16)
    self_out_grad = jnp.einsum(
        "blh,bld->hd", mixed_self, rounded, preferred_element_type=jnp.float32
    )
    grad_mixed = jnp.einsum(
        "bld,hd->blh", rounded, self_out, preferred_element_type=jnp.float32
    ).astype(jnp.bfloat16)
    grad_query, grad_keys, grad_values, grad_scores = attend_backward(
        query_self, keys_self, values_self, bias, causal, log_self, grad_mixed
    )
    batch = grad_scores.shape[0]
    rows = grad_scores.shape[-1]
    table_grad = jnp.einsum(
        "ijn,bhij->nh",
        onehot,
        grad_scores.reshape(batch, -1, rows, rows),
        preferred_element_type=jnp.float32,
    )
    grad_pair = jnp.concatenate([grad_keys, grad_values], axis=-1)
    self_q_grad = jnp.einsum(
        "bld,blh->dh", normed_self, grad_query, preferred_element_type=jnp.float32
    )
    self_kv_grad = jnp.einsum(
        "bld,blw->dw", normed_self, grad_pair, preferred_element_type=jnp.float32
    ).reshape(self_kv.shape)
    grad_normed = input_total(
        jnp.einsum("blh,dh->bld", grad_query, self_q, preferred_element_type=jnp.float32)
        + jnp.einsum("blw,dw->bld", grad_pair, flatten(self_kv), preferred_element_type=jnp.float32)
    )
    _, pull = jax.vjp(rms_norm, start, gain_rows[0])
    grad_residual, gain_self = pull(grad_normed)
    grad_tokens = grad_self + grad_residual
    gains_grad = jnp.stack([gain_self, gain_cross, gain_ffn])
    grads = (
        gains_grad,
        table_grad,
        self_q_grad,
        self_kv_grad,
        self_out_grad,
        cross_q_grad,
        cross_kv_grad,
        cross_out_grad,
        gate_up_grad,
        down_grad,
    )
    return (grad_tokens, grad_pair_cross, grads)


def per_device(
    decoder_in,
    memory,
    buckets,
    norm_gains,
    rel_bias,
    self_q,
    self_kv,
    self_out,
    cross_q,
    cross_kv,
    cross_out,
    gate_up,
    down,
    cotangent,
):
    local = decoder_in.shape[0]
    rows = decoder_in.shape[1]
    per_batch = local // MICRO
    positions = jnp.arange(rows, dtype=jnp.int32)
    causal = positions[:, None] >= positions[None, :]
    onehot = (buckets[:, :, None] == jnp.arange(NB, dtype=jnp.int32)[None, None, :]).astype(
        jnp.bfloat16
    )
    weights = gather_weights(
        norm_gains, rel_bias, self_q, self_kv, self_out, cross_q, cross_kv, cross_out, gate_up, down
    )
    outputs = []
    token_grads = []
    memory_grads = []
    totals = None
    for index in range(MICRO):
        lower = index * per_batch
        upper = lower + per_batch
        memory_part = memory[lower:upper]
        output, saved = forward(decoder_in[lower:upper], memory_part, weights, onehot, causal)
        grad_tokens, grad_pair_cross, grads = backward(
            saved, cotangent[lower:upper], memory_part, weights, onehot, causal
        )
        memory_term = jnp.einsum(
            "bsw,dw->bsd", grad_pair_cross, flatten(weights[6]), preferred_element_type=jnp.float32
        )
        memory_part_grad = lax.psum_scatter(
            memory_term.astype(jnp.bfloat16), "tp", scatter_dimension=2, tiled=True
        )
        memory_grads.append(memory_part_grad)
        outputs.append(output.astype(jnp.bfloat16))
        token_grads.append(grad_tokens)
        grads = (
            lax.psum_scatter(
                grads[0].astype(jnp.bfloat16), ("seq", "fsdp"), scatter_dimension=1, tiled=True
            ).astype(jnp.float32),
            lax.psum_scatter(
                grads[1].astype(jnp.bfloat16), ("seq", "fsdp"), scatter_dimension=0, tiled=True
            ).astype(jnp.float32),
            lax.psum_scatter(
                grads[2].astype(jnp.bfloat16), ("seq", "fsdp"), scatter_dimension=0, tiled=True
            ).astype(jnp.float32),
            lax.psum_scatter(
                grads[3].astype(jnp.bfloat16), ("seq", "fsdp"), scatter_dimension=0, tiled=True
            ).astype(jnp.float32),
            lax.psum_scatter(
                grads[4].astype(jnp.bfloat16), ("seq", "fsdp"), scatter_dimension=1, tiled=True
            ).astype(jnp.float32),
            lax.psum_scatter(
                grads[5].astype(jnp.bfloat16), ("seq", "fsdp"), scatter_dimension=0, tiled=True
            ).astype(jnp.float32),
            lax.psum_scatter(
                grads[6].astype(jnp.bfloat16), ("seq", "fsdp"), scatter_dimension=0, tiled=True
            ).astype(jnp.float32),
            lax.psum_scatter(
                grads[7].astype(jnp.bfloat16), ("seq", "fsdp"), scatter_dimension=1, tiled=True
            ).astype(jnp.float32),
            lax.psum_scatter(
                grads[8].astype(jnp.bfloat16), ("seq", "fsdp"), scatter_dimension=0, tiled=True
            ).astype(jnp.float32),
            lax.psum_scatter(
                grads[9].astype(jnp.bfloat16), ("seq", "fsdp"), scatter_dimension=1, tiled=True
            ).astype(jnp.float32),
        )
        totals = grads if totals is None else jax.tree.map(jnp.add, totals, grads)
    return (
        jnp.concatenate(outputs, axis=0),
        jnp.concatenate(token_grads, axis=0),
        jnp.concatenate(memory_grads, axis=0),
        totals[0],
        totals[1],
        totals[2],
        totals[3],
        totals[4],
        totals[5],
        totals[6],
        totals[7],
        totals[8],
        totals[9],
    )


GROUP = 128


def lane_blocks(value):
    count = value.shape[1] // GROUP
    return jnp.concatenate(
        [value[:, b * GROUP : (b + 1) * GROUP] for b in range(count)], axis=0
    )


def dot(left, right):
    return jnp.dot(left, right, preferred_element_type=jnp.float32)


def dot_t(left, right):
    return lax.dot_general(left, right, (((1,), (1,)), ((), ())), preferred_element_type=jnp.float32)


def t_dot(left, right):
    return lax.dot_general(left, right, (((0,), (0,)), ((), ())), preferred_element_type=jnp.float32)


def low(value):
    return value.astype(jnp.bfloat16)


def high(value):
    return value.astype(jnp.float32)


def norm_backward(values, gain, cotangent):
    _, pull = jax.vjp(rms_norm, values, gain)
    return pull(cotangent)


def stacked(block, pair, lanes):
    block = high(block[:, pair * GROUP : (pair + 1) * GROUP])
    other = pltpu.roll(block, DH, 1)
    if pair == 0:
        rows = jnp.concatenate([block, other], axis=0)
        keep = lanes < DH
    else:
        rows = jnp.concatenate([other, block], axis=0)
        keep = lanes >= DH
    return low(jnp.where(keep, rows, 0.0))


def unstacked(parts):
    heads = []
    for pair, value in enumerate(parts):
        half = value[:, pair * DH : (pair + 1) * DH]
        heads += [half[0:GROUP], half[GROUP : 2 * GROUP]]
    return jnp.concatenate(heads, axis=1)


def all_stacked(block):
    lanes = lax.broadcasted_iota(jnp.int32, (1, GROUP), 1)
    return jnp.concatenate([stacked(block, 0, lanes), stacked(block, 1, lanes)], axis=0)


def all_unstacked(value):
    return low(unstacked([value[0 : 2 * GROUP], value[2 * GROUP :]]))


def pieces(span):
    return [slice(at, at + 512) for at in range(0, span, 512)]


def cross_forward_kernel(q_ref, kv_ref, o_ref, lse_ref, scores):
    query = all_stacked(q_ref[...])
    best = jnp.full((1, 4 * GROUP), MASKED, jnp.float32)
    for rows in pieces(kv_ref.shape[0]):
        part = dot_t(kv_ref[rows, 0:GROUP], query)
        scores[rows, :] = part
        best = jnp.maximum(best, jnp.max(part, axis=0, keepdims=True))
    total = jnp.zeros((1, 4 * GROUP), jnp.float32)
    mixed = jnp.zeros((GROUP, 4 * GROUP), jnp.float32)
    for rows in pieces(kv_ref.shape[0]):
        part = jnp.exp(scores[rows, :] - best)
        total = total + jnp.sum(part, axis=0, keepdims=True)
        mixed = mixed + t_dot(kv_ref[rows, GROUP : 2 * GROUP], low(part))
    o_ref[...] = all_unstacked((mixed / total).T)
    lse = best + jnp.log(total)
    lse_ref[0, 0:1, :] = lse[:, 0 : 2 * GROUP]
    lse_ref[0, 1:2, :] = lse[:, 2 * GROUP :]


def inner_of(dout, out):
    return jnp.sum((high(dout) * high(out)).T, axis=0, keepdims=True)


def cross_backward_kernel(q_ref, do_ref, o_ref, kv_ref, lse_ref, dq_ref, dkv_ref):
    query = all_stacked(q_ref[...])
    dout = all_stacked(do_ref[...])
    inner = inner_of(dout, all_stacked(o_ref[...]))
    lse = jnp.concatenate([lse_ref[0, 0:1, :], lse_ref[0, 1:2, :]], axis=1)
    dq = jnp.zeros((GROUP, 4 * GROUP), jnp.float32)
    for rows in pieces(kv_ref.shape[0]):
        keys = kv_ref[rows, 0:GROUP]
        prob = jnp.exp(dot_t(keys, query) - lse)
        grad = low(prob * (dot_t(kv_ref[rows, GROUP : 2 * GROUP], dout) - inner))
        dkv_ref[rows, 0:GROUP] = low(dot(grad, query))
        dkv_ref[rows, GROUP : 2 * GROUP] = low(dot(low(prob), dout))
        dq = dq + t_dot(keys, grad)
    dq_ref[...] = all_unstacked((dq * DH ** (-0.5)).T)


def self_scores(kv_ref, query, bias_ref, pair):
    rows = kv_ref.shape[0]
    scores = dot_t(kv_ref[:, 0:GROUP], query)
    scores = scores + jnp.concatenate([bias_ref[2 * pair], bias_ref[2 * pair + 1]], axis=1)
    key_at = lax.broadcasted_iota(jnp.int32, scores.shape, 0)
    query_at = lax.broadcasted_iota(jnp.int32, scores.shape, 1) % rows
    return scores, key_at <= query_at


def self_forward_kernel(q_ref, kv_ref, bias_ref, o_ref, lse_ref):
    lanes = lax.broadcasted_iota(jnp.int32, (1, GROUP), 1)
    outs = []
    for pair in range(2):
        query = stacked(q_ref[...], pair, lanes)
        scores, seen = self_scores(kv_ref, query, bias_ref, pair)
        scores = jnp.where(seen, scores, MASKED)
        best = jnp.max(scores, axis=0, keepdims=True)
        part = jnp.exp(scores - best)
        total = jnp.sum(part, axis=0, keepdims=True)
        mixed = t_dot(kv_ref[:, GROUP : 2 * GROUP], low(part / total))
        outs.append(mixed.T)
        lse_ref[0, pair : pair + 1, :] = best + jnp.log(total)
    o_ref[...] = low(unstacked(outs))


def self_backward_kernel(
    q_ref, do_ref, o_ref, kv_ref, lse_ref, bias_ref, dq_ref, dkv_ref, ds_ref
):
    lanes = lax.broadcasted_iota(jnp.int32, (1, GROUP), 1)
    dqs = []
    dk = 0.0
    dv = 0.0
    for pair in range(2):
        query = stacked(q_ref[...], pair, lanes)
        dout = stacked(do_ref[...], pair, lanes)
        inner = inner_of(dout, stacked(o_ref[...], pair, lanes))
        scores, seen = self_scores(kv_ref, query, bias_ref, pair)
        prob = jnp.exp(jnp.where(seen, scores - lse_ref[0, pair : pair + 1, :], MASKED))
        grad = low(prob * (dot_t(kv_ref[:, GROUP : 2 * GROUP], dout) - inner))
        ds_ref[2 * pair] = grad[:, 0:GROUP]
        ds_ref[2 * pair + 1] = grad[:, GROUP : 2 * GROUP]
        dk = dk + dot(grad, query)
        dv = dv + dot(low(prob), dout)
        dqs.append((t_dot(kv_ref[:, 0:GROUP], grad) * DH ** (-0.5)).T)
    dkv_ref[:, 0:GROUP] = low(dk)
    dkv_ref[:, GROUP : 2 * GROUP] = low(dv)
    dq_ref[...] = low(unstacked(dqs))


def attention_specs(rows, span):
    narrow = pl.BlockSpec((rows, 2 * GROUP), lambda k: (0, k))
    tall = pl.BlockSpec((span, 2 * GROUP), lambda k: (0, k))
    lse = pl.BlockSpec((1, 2, 2 * GROUP), lambda k: (k, 0, 0))
    square = pl.BlockSpec((4, rows, rows), lambda k: (k, 0, 0))
    return narrow, tall, lse, square


def kernel_call(kernel, name, blocks, specs, outs, scratch, cost, arguments, limit=32):
    return pl.pallas_call(
        kernel,
        grid=(blocks,),
        in_specs=specs,
        out_specs=[spec for spec, _, _ in outs],
        out_shape=[jax.ShapeDtypeStruct(shape, kind) for _, shape, kind in outs],
        scratch_shapes=scratch,
        compiler_params=pltpu.CompilerParams(vmem_limit_bytes=limit * 2**20),
        cost_estimate=pl.CostEstimate(flops=cost[0], bytes_accessed=cost[1], transcendentals=cost[2]),
        name=name,
    )(*arguments)


def attention_forward(query, pairs, bias):
    rows, span = query.shape[0], pairs.shape[0]
    blocks = query.shape[1] // (2 * GROUP)
    narrow, tall, lse, square = attention_specs(rows, span)
    cost = (
        16 * rows * span * DH * blocks,
        2 * (2 * query.size + pairs.size),
        4 * rows * span * blocks,
    )
    outs = [
        (narrow, query.shape, jnp.bfloat16),
        (lse, (blocks, 2, 2 * GROUP), jnp.float32),
    ]
    if bias is not None:
        return kernel_call(
            self_forward_kernel,
            "self_forward",
            blocks,
            [narrow, tall, square],
            outs,
            [],
            cost,
            (query, pairs, bias),
        )
    return kernel_call(
        cross_forward_kernel,
        "cross_forward",
        blocks,
        [narrow, tall],
        outs,
        [pltpu.VMEM((span, 4 * GROUP), jnp.float32)],
        cost,
        (query, pairs),
    )


def attention_backward(query, dout, out, pairs, lse_value, bias):
    rows, span = query.shape[0], pairs.shape[0]
    blocks = query.shape[1] // (2 * GROUP)
    narrow, tall, lse, square = attention_specs(rows, span)
    cost = (
        40 * rows * span * DH * blocks,
        2 * (4 * query.size + 2 * pairs.size),
        4 * rows * span * blocks,
    )
    outs = [(narrow, query.shape, jnp.bfloat16), (tall, pairs.shape, jnp.bfloat16)]
    if bias is not None:
        return kernel_call(
            self_backward_kernel,
            "self_backward",
            blocks,
            [narrow, narrow, narrow, tall, lse, square],
            outs + [(square, (4 * blocks, rows, rows), jnp.bfloat16)],
            [],
            cost,
            (query, dout, out, pairs, lse_value, bias),
        )
    return kernel_call(
        cross_backward_kernel,
        "cross_backward",
        blocks,
        [narrow, narrow, narrow, tall, lse],
        outs,
        [],
        cost,
        (query, dout, out, pairs, lse_value),
    )


def with_index(kernel, name, grid, specs, outs, scratch, cost, index, arguments, limit=32):
    return pl.pallas_call(
        kernel,
        grid_spec=pltpu.PrefetchScalarGridSpec(
            num_scalar_prefetch=1,
            grid=grid,
            in_specs=specs,
            out_specs=[spec for spec, _, _ in outs],
            scratch_shapes=scratch,
        ),
        out_shape=[jax.ShapeDtypeStruct(shape, kind) for _, shape, kind in outs],
        compiler_params=pltpu.CompilerParams(vmem_limit_bytes=limit * 2**20),
        cost_estimate=pl.CostEstimate(flops=cost[0], bytes_accessed=cost[1], transcendentals=0),
        name=name,
    )(index, *arguments)


def pack_shards(tp, cross_kv, self_q, self_kv, small, self_out, cross_q, cross_out):
    groups = [[cross_kv, self_q, self_kv, small], [self_out, cross_q, cross_out]]
    depths = [sum(part.size // GROUP for part in parts) for parts in groups]
    arguments = [part for parts in groups for part in parts]

    def kernel(*refs):
        ins, (near, *packs) = refs[: len(arguments)], refs[len(arguments) :]
        taken = 0
        above = 0
        for parts, pack, depth in zip(groups, packs, depths):
            at = 0
            for part in parts:
                rows = part.shape[0]
                for b in range(part.size // GROUP // rows):
                    if part.ndim == 3:
                        pack[at : at + rows, :] = ins[taken][:, b, :]
                    else:
                        pack[at : at + rows, :] = ins[taken][:, b * GROUP : (b + 1) * GROUP]
                    at += rows
                taken += 1
            for k in range(tp):
                near[k, above : above + depth, :] = pack[...]
            above += depth

    shapes = [(tp, depths[0] + depths[1], GROUP)] + [(depth, GROUP) for depth in depths]
    whole = [
        pl.BlockSpec(shape, lambda k, nothing=(0,) * len(shape): nothing) for shape in shapes
    ]
    return kernel_call(
        kernel,
        "pack_shards",
        1,
        [pl.BlockSpec(part.shape, lambda k, at=(0,) * part.ndim: at) for part in arguments],
        [(spec, shape, jnp.bfloat16) for spec, shape in zip(whole, shapes)],
        [],
        (0, 4 * sum(depths) * GROUP, 0),
        tuple(arguments),
        limit=56,
    )


def unpack_heads(index, near, far, depth, top, rows_first, width, extra):
    tp = near[0].shape[0]
    listed = isinstance(far[0], list)
    seq = (far[0][0].shape[0] if listed else far[0].shape[1]) + 1
    shard = width // (2 * seq)
    sides = tuple(far[0]) + tuple(far[1]) if listed else tuple(far)

    def kernel(index_ref, *refs):
        near_refs, far_refs = refs[0:2], refs[2 : 2 + len(sides)]
        outs = refs[2 + len(sides) :]

        def place(q, side, read):
            row = 2 * (index_ref[0] ^ q) + (index_ref[2] ^ side)
            at = pl.ds(pl.multiple_of(row * shard, shard), shard)
            for entry, (out, down) in enumerate(zip(outs, rows_first)):
                start = entry * 2 * shard
                if down:
                    out[:, at] = read(start, 2 * shard)
                else:
                    for b in range(2):
                        out[at, b * GROUP : (b + 1) * GROUP] = read(start + b * shard, shard)
            if extra:
                outs[-1][0, row] = read(depth - extra, extra)

        for side in range(2):
            place(0, side, lambda start, size: near_refs[side][0, top + start : top + start + size, :])
            for q in range(1, seq):
                if listed:
                    for k in range(tp):

                        @pl.when(pl.program_id(0) == k)
                        def _():
                            ref = far_refs[side * tp + k]
                            place(q, side, lambda start, size: ref[q - 1, start : start + size, :])

                else:
                    place(
                        q,
                        side,
                        lambda start, size: far_refs[side][0, q - 1, start : start + size, :],
                    )

    specs = [pl.BlockSpec((1,) + near[0].shape[1:], lambda k, index: (k ^ index[1], 0, 0))] * 2
    for value in sides:
        if listed:
            specs.append(pl.BlockSpec(value.shape, lambda k, index: (0, 0, 0)))
        else:
            specs.append(
                pl.BlockSpec((1,) + value.shape[1:], lambda k, index: (k ^ index[1], 0, 0, 0))
            )
    outs = []
    for down in rows_first:
        if down:
            spec = pl.BlockSpec((2 * GROUP, width), lambda k, index: (k, 0))
            outs.append((spec, (tp * 2 * GROUP, width), jnp.bfloat16))
        else:
            spec = pl.BlockSpec((width, 2 * GROUP), lambda k, index: (0, k))
            outs.append((spec, (width, tp * 2 * GROUP), jnp.bfloat16))
    if extra:
        spec = pl.BlockSpec((1, 2 * seq, extra, GROUP), lambda k, index: (k, 0, 0, 0))
        outs.append((spec, (tp, 2 * seq, extra, GROUP), jnp.bfloat16))
    return with_index(
        kernel,
        "unpack_heads",
        (tp,),
        specs,
        outs,
        [],
        (0, 8 * tp * seq * depth * GROUP),
        index,
        (*near, *sides),
    )


def unpack_hidden(value, width, hidden_width):
    count = value.shape[0]
    shard = width // count
    columns = 2 * hidden_width // GROUP

    def kernel(in_ref, gate_up_ref, down_ref):
        for b in range(columns):
            gate_up_ref[:, b * GROUP : (b + 1) * GROUP] = in_ref[0, b * shard : (b + 1) * shard, :]
        down_ref[...] = in_ref[0, columns * shard :, :]

    return kernel_call(
        kernel,
        "unpack_hidden",
        count,
        [pl.BlockSpec((1, value.shape[1], GROUP), lambda k: (k, 0, 0))],
        [
            (
                pl.BlockSpec((shard, 2 * hidden_width), lambda k: (k, 0)),
                (width, 2 * hidden_width),
                jnp.bfloat16,
            ),
            (
                pl.BlockSpec((hidden_width, shard), lambda k: (0, k)),
                (hidden_width, width),
                jnp.bfloat16,
            ),
        ],
        [],
        (0, 4 * value.size, 0),
        (value,),
        limit=56,
    )


def memory_terms(index, seq, memory, pairs, weight, tp):
    rows, width = pairs.shape
    shard = width // (2 * seq)
    features = weight.shape[0] // tp
    steps = 2 * seq
    block = rows // steps
    early = max(steps // 4, 1)

    def row_of(step, index):
        return 2 * (index[0] ^ (step % seq)) + (index[2] ^ (1 - step // seq))

    def kernel(index_ref, memory_ref, pairs_ref, weight_ref, sent_ref, kept_ref, *outs):
        step = pl.program_id(0)
        part = t_dot(memory_ref[0], pairs_ref[...])

        @pl.when(step < seq)
        def _():
            sent_ref[0] = low(part)

        @pl.when(step >= seq)
        def _():
            kept_ref[0] = part

        values = pairs_ref[pl.ds(pl.multiple_of(step * block, block), block), :]
        for k in range(tp):
            at = pl.multiple_of((index_ref[1] ^ k) * features, features)
            outs[tp + k][...] = low(dot_t(values, weight_ref[pl.ds(at, features), :]))

        @pl.when(step < early)
        def _():
            for k in range(tp):
                outs[k][...] = outs[tp + k][...]

    shape = (seq, shard, width)
    first = pl.BlockSpec((block, features), lambda s, index: (jnp.minimum(s, early - 1), 0))
    second = pl.BlockSpec((block, features), lambda s, index: (jnp.maximum(s - early, 0), 0))
    return with_index(
        kernel,
        "memory_terms",
        (steps,),
        [
            pl.BlockSpec((1, rows, shard), lambda s, index: (index[1], 0, row_of(s, index))),
            pl.BlockSpec(pairs.shape, lambda s, index: (0, 0)),
            pl.BlockSpec(weight.shape, lambda s, index: (0, 0)),
        ],
        [
            (
                pl.BlockSpec((1, shard, width), lambda s, index: (jnp.minimum(s, seq - 1), 0, 0)),
                shape,
                jnp.bfloat16,
            ),
            (
                pl.BlockSpec((1, shard, width), lambda s, index: (jnp.maximum(s - seq, 0), 0, 0)),
                shape,
                jnp.float32,
            ),
        ]
        + [(first, (early * block, features), jnp.bfloat16)] * tp
        + [(second, (rows - early * block, features), jnp.bfloat16)] * tp,
        [],
        (4 * rows * width * width, 6 * pairs.size),
        index,
        (memory, pairs, weight),
        limit=56,
    )


def hidden_out(index, hidden, weight, values, tp):
    rows = hidden.shape[0] // tp
    width = weight.shape[1]

    def kernel(index_ref, hidden_ref, weight_ref, values_ref, out_ref):
        part = dot(hidden_ref[...], weight_ref[...])

        @pl.when(pl.program_id(0) == 0)
        def _():
            out_ref[0] = low(part + values_ref[...])

        @pl.when(pl.program_id(0) != 0)
        def _():
            out_ref[0] = low(part)

    return with_index(
        kernel,
        "hidden_out",
        (tp,),
        [
            pl.BlockSpec((rows, hidden.shape[1]), lambda k, index: (k, 0)),
            pl.BlockSpec(weight.shape, lambda k, index: (0, 0)),
            pl.BlockSpec(values.shape, lambda k, index: (0, 0)),
        ],
        [
            (
                pl.BlockSpec((1, rows, width), lambda k, index: (k ^ index[1], 0, 0)),
                (tp, rows, width),
                jnp.bfloat16,
            )
        ],
        [],
        (2 * hidden.size * width, 2 * (hidden.size + weight.size + tp * rows * width)),
        index,
        (hidden, weight, values),
    )[0]


def row_terms(index, seq, name, pairs):
    width = pairs[0][0][0].shape[-1] if isinstance(pairs[0][0], list) else pairs[0][0].shape[-1]
    shard = width // (2 * seq)
    columns = sum(right[0][2] - right[0][1] for _, right in pairs)

    def row_of(step, index):
        return 2 * (index[0] ^ (step % seq)) + (index[2] ^ (1 - step // seq))

    def kernel(index_ref, *refs):
        sent_ref, kept_ref = refs[-2:]
        parts = []
        at = 0
        for left, right in pairs:
            if isinstance(left, list):
                value = jnp.concatenate([ref[...] for ref in refs[at : at + len(left)]], axis=0)
                at += len(left)
            else:
                value = refs[at][0]
                at += 1
            other = [ref[:, low_at:high_at] for ref, (_, low_at, high_at) in zip(refs[at:], right)]
            at += len(right)
            parts.append(t_dot(value, jnp.concatenate(other, axis=0)))

        def put(ref, kind):
            at = 0
            for part in parts:
                ref[0, :, at : at + part.shape[1]] = part.astype(kind)
                at += part.shape[1]

        @pl.when(pl.program_id(0) < seq)
        def _():
            put(sent_ref, jnp.bfloat16)

        @pl.when(pl.program_id(0) >= seq)
        def _():
            put(kept_ref, jnp.float32)

    specs = []
    arguments = []
    depth = 0
    for left, right in pairs:
        if isinstance(left, list):
            for part in left:
                rows = part.shape[0]
                specs.append(pl.BlockSpec((rows, shard), lambda s, index: (0, row_of(s, index))))
                arguments.append(part)
        else:
            specs.append(
                pl.BlockSpec(
                    (1, left.shape[1], shard), lambda s, index: (index[1], 0, row_of(s, index))
                )
            )
            arguments.append(left)
        for part, _, _ in right:
            specs.append(pl.BlockSpec(part.shape, lambda s, index: (0, 0)))
            arguments.append(part)
        depth = max(depth, sum(part.shape[0] for part, _, _ in right))
    shape = (seq, shard, columns)
    block = (1, shard, columns)
    return with_index(
        kernel,
        name,
        (2 * seq,),
        specs,
        [
            (
                pl.BlockSpec(block, lambda s, index: (jnp.minimum(s, seq - 1), 0, 0)),
                shape,
                jnp.bfloat16,
            ),
            (
                pl.BlockSpec(block, lambda s, index: (jnp.maximum(s - seq, 0), 0, 0)),
                shape,
                jnp.float32,
            ),
        ],
        [],
        (2 * depth * width * columns, 2 * depth * (width + columns) + 3 * width * columns),
        index,
        tuple(arguments),
        limit=56,
    )


def hidden_terms(normed, grad_joined, rounded, hidden):
    rows, width = normed.shape
    columns = grad_joined.shape[1] + hidden.shape[1]
    split = grad_joined.shape[1]
    steps = width // GROUP

    def kernel(normed_ref, joined_ref, rounded_ref, hidden_ref, out_ref):
        out_ref[:, :split] = low(t_dot(normed_ref[...], joined_ref[...]))
        out_ref[:, split:] = low(t_dot(rounded_ref[...], hidden_ref[...]))

    left = pl.BlockSpec((rows, GROUP), lambda k: (0, k))
    return kernel_call(
        kernel,
        "hidden_terms",
        steps,
        [
            left,
            pl.BlockSpec(grad_joined.shape, lambda k: (0, 0)),
            left,
            pl.BlockSpec(hidden.shape, lambda k: (0, 0)),
        ],
        [(pl.BlockSpec((GROUP, columns), lambda k: (k, 0)), (width, columns), jnp.bfloat16)],
        [],
        (2 * rows * width * columns, 4 * rows * (width + columns) + 2 * width * columns, 0),
        (normed, grad_joined, rounded, hidden),
        limit=56,
    )[0]


def one_each(seq, tp):
    everyone = ("seq", "tp", "fsdp")

    def after(value, *earlier):
        return lax.optimization_barrier((value, earlier))[0]

    def together(*values):
        return lax.optimization_barrier(values)

    def swap(value, axis, flip):
        size = {"seq": seq, "tp": tp, "fsdp": 2}[axis]
        return lax.ppermute(value, axis, [(place, place ^ flip) for place in range(size)])

    def gather(value, axis, size):
        return [value] + [swap(value, axis, flip) for flip in range(1, size)]

    def exchange(parts, axis):
        return [parts[0]] + [swap(parts[k], axis, k) for k in range(1, len(parts))]

    def exchange_all(value):
        return lax.all_to_all(value, "tp", 0, 0, tiled=True)

    def to_everyone(value):
        return exchange_all(jnp.broadcast_to(value[None], (tp,) + value.shape))

    def total(parts):
        result = high(parts[0])
        for part in parts[1:]:
            result = result + high(part)
        return result

    def run(
        decoder_in,
        memory,
        buckets,
        norm_gains,
        rel_bias,
        self_q,
        self_kv,
        self_out,
        cross_q,
        cross_kv,
        cross_out,
        gate_up,
        down,
        cotangent,
    ):
        count, rows, width = decoder_in.shape
        z = lax.axis_index("seq")
        t = lax.axis_index("tp")
        c = lax.axis_index("fsdp")
        index = jnp.stack([z, t, c]).astype(jnp.int32)
        cores = 2
        shard = self_q.shape[0]
        tables = rel_bias.shape[0]
        heads = rel_bias.shape[1]
        hidden_width = down.shape[0]
        extra = 16

        def own(value):
            return lax.dynamic_index_in_dim(value, t, 0, keepdims=False)

        def from_here(value):
            return [
                lax.dynamic_index_in_dim(value, t ^ k, 0, keepdims=False) for k in range(tp)
            ]

        def in_order(parts, kind):
            result = jnp.zeros((count,) + parts[0].shape, kind)
            for k, part in enumerate(parts):
                result = lax.dynamic_update_index_in_dim(result, part.astype(kind), t ^ k, 0)
            return result

        def head_blocks(value):
            size = value.shape[1] // tp
            return [value[:, k * size : (k + 1) * size] for k in range(tp)]

        small = jnp.concatenate(
            [
                norm_gains,
                jnp.pad(rel_bias.reshape(1, -1), ((0, 0), (0, GROUP - rel_bias.size))),
                jnp.zeros((extra - 4, GROUP), jnp.bfloat16),
            ],
            axis=0,
        )
        near, pack_a, pack_b = pack_shards(
            tp, cross_kv, self_q, self_kv, small, self_out, cross_q, cross_out
        )
        gate_up, down = after((gate_up, down), near)
        pack_f = jnp.concatenate([lane_blocks(flatten(gate_up)), down], axis=0)

        depth_a, depth_b = pack_a.shape[0], pack_b.shape[0]
        near = exchange_all(near)
        ring_a = gather(pack_a, "seq", seq)
        onehot = (
            buckets.T[:, :, None] == jnp.arange(NB, dtype=jnp.int32)[None, None, :]
        ).astype(jnp.bfloat16)
        start = high(own(decoder_in))
        unit_self = start * lax.rsqrt(jnp.mean(start * start, axis=-1, keepdims=True) + EPSILON)
        pack_b, onehot, unit_self = together(pack_b, onehot, unit_self)
        ring_b = gather(after(pack_b, *ring_a), "seq", seq)
        far_a = to_everyone(after(jnp.stack(ring_a[1:]), near))
        far_b = after(jnp.stack(ring_b[1:]), far_a)
        decoder_in, cotangent = after((decoder_in, cotangent), far_b)
        far_b = gather(far_b, "tp", tp)
        full_f = lax.all_gather(after(pack_f, *ring_b), ("seq", "fsdp"), axis=0, tiled=True)
        near = [near, swap(near, "fsdp", 1)]
        far_a = [far_a, swap(far_a, "fsdp", 1)]

        cross_pairs, weight_self_q, weight_self_kv, smalls = unpack_heads(
            index, near, far_a, depth_a, 0, (False, False, False), width, extra
        )
        weight_gate_up, weight_down = unpack_hidden(
            full_f.reshape(seq * cores, -1, GROUP), width, hidden_width
        )
        gain_rows = high(smalls[0, :, 0:3].transpose(1, 0, 2).reshape(3, width))
        table = smalls[:, :, 3, 0 : tables * heads].reshape(tp, seq * cores, tables, heads)
        table = table.transpose(1, 2, 0, 3).reshape(NB, tp * heads)
        bias = jnp.einsum("jin,nh->hji", onehot, table, preferred_element_type=jnp.float32)

        pairs = low(dot(own(memory), cross_pairs))
        scale = DH ** (-0.5)

        normed_self = low(unit_self * gain_rows[0])
        query_self = low(dot(normed_self, weight_self_q) * scale)
        pair_self = low(dot(normed_self, weight_self_kv))
        mixed_self, log_self = attention_forward(query_self, pair_self, bias)
        far_b = [after(part, mixed_self, pairs) for part in far_b]
        far_b = [far_b, [swap(part, "fsdp", 1) for part in far_b]]
        weight_self_out, weight_cross_q, weight_cross_out = unpack_heads(
            index, near, far_b, depth_b, depth_a, (True, False, True), width, 0
        )
        after_self = start + dot(mixed_self, weight_self_out)

        normed_cross = low(rms_norm(after_self, gain_rows[1]))
        query_cross = low(dot(normed_cross, weight_cross_q) * scale)
        mixed_cross, log_cross = attention_forward(query_cross, pairs, None)
        after_cross = after_self + dot(mixed_cross, weight_cross_out)
        normed_ffn = low(rms_norm(after_cross, gain_rows[2]))

        all_cross = lax.all_gather(normed_cross, "tp", axis=0, tiled=True)
        normed_parts, weight_gate_up, weight_down, own_cotangent, rounded = together(
            gather(normed_ffn, "tp", tp),
            weight_gate_up,
            weight_down,
            own(cotangent),
            jnp.concatenate(from_here(cotangent), axis=0),
        )
        all_normed = jnp.concatenate(normed_parts, axis=0)
        joined = dot(all_normed, weight_gate_up)
        gate = joined[:, :hidden_width]
        up = joined[:, hidden_width:]
        grad_hidden = dot_t(rounded, weight_down)
        hidden = low(gelu_product(gate, up))
        _, pull = jax.vjp(gelu_product, gate, up)
        grad_gate, grad_up = pull(grad_hidden)
        grad_joined = low(jnp.concatenate([grad_gate, grad_up], axis=-1))

        def row_parts(value):
            return [value[k * rows : (k + 1) * rows] for k in range(tp)]

        partial_normed = row_parts(low(dot_t(grad_joined, weight_gate_up)))
        grad_parts = exchange(partial_normed, "tp")
        all_normed, grad_joined, rounded, hidden, o_self, o_cross = after(
            (all_normed, grad_joined, rounded, hidden, mixed_self, mixed_cross), partial_normed
        )
        hidden_grads = hidden_terms(all_normed, grad_joined, rounded, hidden)
        o_blocks = [
            jnp.concatenate(blocks, axis=1)
            for blocks in zip(head_blocks(o_self), head_blocks(o_cross))
        ]
        grad_parts, hidden_grads, o_blocks = together(grad_parts, hidden_grads, o_blocks)
        hidden_grads = high(
            lax.psum_scatter(hidden_grads, ("seq", "fsdp"), scatter_dimension=0, tiled=True)
        )

        grad_normed = total(grad_parts)
        grad_residual, gain_ffn = norm_backward(after_cross, gain_rows[2], grad_normed)
        grad_cross = high(own_cotangent) + grad_residual
        rounded_cross = low(grad_cross)
        cross_operands = [jnp.concatenate([rounded_cross, block], axis=1) for block in o_blocks]
        cross_parts = exchange(cross_operands, "tp")
        grad_mixed = low(dot_t(after(rounded_cross, cross_operands), weight_cross_out))
        grad_query, grad_pairs = attention_backward(
            query_cross, grad_mixed, mixed_cross, pairs, log_cross, None
        )
        cross_parts, grad_query, grad_pairs = together(cross_parts, grad_query, grad_pairs)
        grad_normed = dot_t(grad_query, weight_cross_q)
        grad_residual, gain_cross = norm_backward(after_self, gain_rows[1], grad_normed)
        grad_self = grad_cross + grad_residual
        rounded_self = low(grad_self)
        self_operands = [
            jnp.concatenate([rounded_self, block], axis=1) for block in head_blocks(grad_query)
        ]
        self_parts = exchange(self_operands, "tp")

        grad_mixed_self = low(dot_t(after(rounded_self, self_operands), weight_self_out))
        grad_query_self, grad_pair_self, grad_scores = attention_backward(
            query_self, grad_mixed_self, mixed_self, pair_self, log_self, bias
        )
        grad_normed = dot_t(grad_query_self, weight_self_q) + dot_t(grad_pair_self, weight_self_kv)
        grad_residual, gain_self = norm_backward(start, gain_rows[0], grad_normed)
        grad_tokens = low(grad_self + grad_residual)
        last_operands = [
            jnp.concatenate([grad_tokens, q_block, kv_block], axis=1)
            for q_block, kv_block in zip(head_blocks(grad_query_self), head_blocks(grad_pair_self))
        ]
        partial_out = hidden_out(
            index, after(hidden, last_operands), weight_down, after_cross, tp
        )
        partial_out, self_parts, last_operands, memory_pairs, decoder_in, gains, grad_scores = together(
            partial_out,
            self_parts,
            last_operands,
            grad_pairs,
            decoder_in,
            (gain_self, gain_cross, gain_ffn),
            grad_scores,
        )
        last_parts = exchange(last_operands, "tp")

        kv_sent, kv_rows, *memory_parts = memory_terms(
            index, seq, memory, memory_pairs, cross_pairs, tp
        )
        decoder_out = lax.psum(partial_out, "tp")
        last_parts, kv_sent, kv_rows, memory_parts, gains, grad_scores, all_cross = (
            together(
                last_parts,
                kv_sent,
                kv_rows,
                memory_parts,
                gains,
                grad_scores,
                all_cross,
            )
        )
        first_parts = exchange(memory_parts[:tp], "tp")
        kv_rows = kv_rows + high(swap(kv_sent, "fsdp", 1))

        def span_of(parts, first, last):
            return [(part, first, last) for part in parts]

        all_start = [
            low(rms_norm(high(part), gain_rows[0])) for part in from_here(decoder_in)
        ]
        both_sent, both_kept = row_terms(
            index,
            seq,
            "head_weights",
            [
                (
                    from_here(all_cross.reshape(tp, rows, width)),
                    span_of(self_parts, width, width + 2 * GROUP),
                ),
                (cross_parts, span_of(cross_parts, width + 2 * GROUP, width + 4 * GROUP)),
                (all_start, span_of(last_parts, width, width + 4 * GROUP)),
                (self_parts, span_of(cross_parts, width, width + 2 * GROUP)),
            ],
        )
        kv_far = low(kv_rows[seq // 2 :])
        first_parts, kv_far, kv_rows, both_sent, both_kept, second_parts = together(
            first_parts, kv_far, kv_rows, both_sent, both_kept, memory_parts[tp:]
        )
        kv_far = swap(kv_far, "seq", seq // 2)
        second_parts = exchange(second_parts, "tp")
        both_grads = low(both_kept + high(swap(both_sent, "fsdp", 1)))
        both_grads = jnp.concatenate(
            [
                lax.dynamic_index_in_dim(both_grads, z ^ k, 0, keepdims=True) for k in range(seq)
            ],
            axis=0,
        )
        gains, grad_scores, last_parts, hidden_grads = after(
            (gains, grad_scores, last_parts, hidden_grads), both_sent
        )
        gate_up_grad = hidden_grads[:, : 2 * hidden_width].reshape(gate_up.shape)
        down_grad = hidden_grads[:, 2 * hidden_width :].T
        cut = first_parts[0].shape[0]
        memory_grad = jnp.zeros((count, memory.shape[1], first_parts[0].shape[1]), jnp.bfloat16)
        for k in range(tp):
            memory_grad = lax.dynamic_update_slice(
                memory_grad, first_parts[k][None], (t ^ k, 0, 0)
            )
        table_grad = jnp.einsum(
            "jin,hji->nh", onehot, grad_scores, preferred_element_type=jnp.float32
        )
        gain_parts = jnp.stack([gain.reshape(-1, GROUP) for gain in gains], axis=1)
        table_parts = jnp.pad(
            table_grad.reshape(seq * cores, 1, -1),
            ((0, 0), (0, 0), (0, GROUP - tables * tp * heads)),
        )
        little = low(jnp.concatenate([gain_parts, table_parts], axis=1))
        little = jnp.broadcast_to(
            little.reshape(seq, 1, cores, 4, GROUP), (seq, tp, cores, 4, GROUP)
        )
        both_grads, kv_far, little, gate_up_grad, down_grad, last_parts, memory_grad = together(
            both_grads, kv_far, little, gate_up_grad, down_grad, last_parts, memory_grad
        )
        decoder_grad = in_order([part[:, :width] for part in last_parts], jnp.float32)
        both_grads = lax.all_to_all(both_grads, "seq", 0, 0, tiled=True)
        kv_rows = kv_rows[: seq // 2] + high(kv_far)
        step = seq // 4
        while step:
            kv_rows = kv_rows[:step] + high(swap(low(kv_rows[step:]), "seq", step))
            step //= 2
        kv_rows = kv_rows[0]
        for k in range(tp):
            memory_grad = lax.dynamic_update_slice(
                memory_grad, second_parts[k][None], (t ^ k, cut, 0)
            )
        both_grads, little, kv_rows, memory_grad, decoder_grad = together(
            both_grads, little, kv_rows, memory_grad, decoder_grad
        )
        cross_kv_grad = total(
            exchange([kv_rows[:, : 2 * GROUP]] + head_blocks(low(kv_rows))[1:], "tp")
        )
        little = lax.all_to_all(little.reshape(-1, 4, GROUP), everyone, 0, 0, tiled=True)
        little = jnp.sum(high(little).reshape(seq, tp, cores, 4, GROUP), axis=(0, 2))
        sender = jnp.arange(tp, dtype=jnp.int32)
        chosen = (sender[:, None] ^ sender[None, :]) == t
        table_sum = little[:, 3, : tables * tp * heads].reshape(tp, tables, tp, heads)
        table_sum = jnp.sum(jnp.where(chosen[:, None, :, None], table_sum, 0.0), axis=(0, 2))
        little = jnp.sum(little, axis=0)
        both_grads = jnp.sum(high(both_grads), axis=0)
        cross_grads = both_grads[:, : 4 * GROUP]
        self_grads = both_grads[:, 4 * GROUP :]

        return (
            decoder_out,
            decoder_grad,
            memory_grad,
            little[0:3],
            table_sum,
            self_grads[:, 0 : 2 * GROUP],
            self_grads[:, 2 * GROUP : 4 * GROUP].reshape(self_kv.shape),
            self_grads[:, 4 * GROUP :].T,
            cross_grads[:, 0 : 2 * GROUP],
            cross_kv_grad.reshape(cross_kv.shape),
            cross_grads[:, 2 * GROUP :].T,
            gate_up_grad,
            down_grad,
        )

    return run


def plan_of(mesh):
    seq, tp, cores = (mesh.shape[axis] for axis in ("seq", "tp", "fsdp"))

    def chosen(*arrays):
        count, rows, width = arrays[0].shape
        fits = (
            cores == 2
            and seq & (seq - 1) == 0
            and tp & (tp - 1) == 0
            and count == tp
            and rows == GROUP
            and arrays[1].shape[1] % 512 == 0
            and width == 2 * seq * GROUP
            and arrays[5].shape[1] == 4 * DH
            and arrays[6].shape[2] == 2 * DH
            and tp * arrays[4].size <= GROUP
            and 2 * arrays[12].shape[0] % GROUP == 0
        )
        return (one_each(seq, tp) if fits else per_device)(*arrays)

    return chosen


def solution(mesh):
    return jax.shard_map(
        plan_of(mesh),
        mesh=mesh,
        in_specs=(
            P(("seq", "fsdp"), None, None),
            P(("seq", "fsdp"), None, None),
            P(),
            P(None, ("seq", "fsdp")),
            P(("seq", "fsdp"), "tp"),
            P(("seq", "fsdp"), "tp"),
            P(("seq", "fsdp"), None, "tp"),
            P("tp", ("seq", "fsdp")),
            P(("seq", "fsdp"), "tp"),
            P(("seq", "fsdp"), None, "tp"),
            P("tp", ("seq", "fsdp")),
            P(("seq", "fsdp"), None, "tp"),
            P("tp", ("seq", "fsdp")),
            P(("seq", "fsdp"), None, None),
        ),
        out_specs=(
            P(("seq", "fsdp"), None, None),
            P(("seq", "fsdp"), None, None),
            P(("seq", "fsdp"), None, "tp"),
            P(None, ("seq", "fsdp")),
            P(("seq", "fsdp"), "tp"),
            P(("seq", "fsdp"), "tp"),
            P(("seq", "fsdp"), None, "tp"),
            P("tp", ("seq", "fsdp")),
            P(("seq", "fsdp"), "tp"),
            P(("seq", "fsdp"), None, "tp"),
            P("tp", ("seq", "fsdp")),
            P(("seq", "fsdp"), None, "tp"),
            P("tp", ("seq", "fsdp")),
        ),
        check_vma=False,
    )
```
